32 devices in a mesh: dp: 4 (over x, core), ty: 2 (over y), tx: 4 (over z).
Axes of the slice: x: 2, y: 2, z: 4, core: 2. Of those that a mesh axis runs over, the one named last changes fastest.
Arguments:
- features: bfloat16 [4, 12, 64, 64, 256], P('dp', None, 'ty', 'tx'), may hold values from -6 to 6
- extra_inputs: bfloat16 [4, 12, 64, 64, 9], P('dp', None, 'ty', 'tx'), may hold values from -6 to 6
- first_kernel: bfloat16 [3, 3, 265, 256], replicated, may hold values from -0.125 to 0.125
- first_bias: bfloat16 [256], replicated, may hold values from -3 to 3
- second_kernel: bfloat16 [3, 3, 256, 256], replicated, may hold values from -0.125 to 0.125
- second_bias: bfloat16 [256], replicated, may hold values from -3 to 3
- skip_kernel: bfloat16 [265, 256], replicated, may hold values from -0.375 to 0.375
- skip_bias: bfloat16 [256], replicated, may hold values from -3 to 3
- seam_table: int32 [12, 4, 4], replicated, may hold values from 0 to 11, as said below
- cotangent: bfloat16 [4, 12, 64, 64, 256], P('dp', None, 'ty', 'tx'), may hold values from -6 to 6
Outputs:
- block_output: bfloat16 [4, 12, 64, 64, 256], P('dp', None, 'ty', 'tx')
- grad_features: bfloat16 [4, 12, 64, 64, 256], P('dp', None, 'ty', 'tx')
- grad_extra: bfloat16 [4, 12, 64, 64, 9], P('dp', None, 'ty', 'tx')
- grad_first_kernel: float32 [3, 3, 265, 256], replicated
- grad_first_bias: float32 [256], replicated
- grad_second_kernel: float32 [3, 3, 256, 256], replicated
- grad_second_bias: float32 [256], replicated
- grad_skip_kernel: float32 [265, 256], replicated
- grad_skip_bias: float32 [256], replicated
The draws below stay inside these ranges and needn't reach their ends.
Inputs may be any that keep to these rules, and one draw needn't show every extreme that they name: seam_table[f, s] holds a source face below 12, a source side below 4, a reversal flag and a corner rule, each 0 or 1; every face is a source of exactly 4 sides.
All inputs are finite; a program needn't handle non-finite values.
Results may differ from the reference program's by a relative error of at most 0.006.
Values may be sent and summed in bfloat16 or wider, within the bound.
A program may use at most 320 MiB of HBM per device.

```python
import jax
import jax.numpy as jnp
from jax import lax

FACES = 12
FACE = 64
CH = 256
EXTRA = 9
IN_CH = 265
SAMPLES = 4


def draw_seam_table(key, part):
    key = jax.random.fold_in(key, 7)
    subkeys = jax.random.split(key, 4)
    entries = FACES * 4
    source_face = jax.random.permutation(subkeys[0], entries) % FACES
    source_side = jax.random.permutation(subkeys[1], entries) % 4
    reverse = jax.random.permutation(subkeys[2], entries) % 2
    corner = jax.random.permutation(subkeys[3], entries) % 2
    stacked = jnp.stack([source_face, source_side, reverse, corner], axis=-1)
    return stacked.reshape(FACES, 4, 4).astype(jnp.int32)


def block_scale(own_key, shape, shards, least, largest):
    def one(position, blocks):
        draws = jax.random.uniform(jax.random.fold_in(jax.random.fold_in(own_key, 6), position), (blocks,), jnp.float32, least / len(shards), largest / len(shards))
        return jnp.repeat(jnp.exp(draws), shape[position] // blocks).reshape((-1,) + (1,) * (len(shape) - position - 1))

    factor_of = one(*shards[0])
    for cut in shards[1:]:
        factor_of = factor_of * one(*cut)
    return factor_of


def centred(key, shape, spread, bound, cuts=(), kind=jnp.bfloat16):
    gain = block_scale(key, shape, cuts, -0.22, 0.18) if cuts else 1.0
    drawn = jax.random.normal(key, shape, jnp.float32) * spread * gain
    return jnp.minimum(jnp.maximum(drawn, -bound), bound).astype(kind)


def setup_inputs(seed: int = 0) -> dict:
    key_list = jax.random.split(jax.random.key(seed), 11)
    return {
        "features": centred(key_list[0], (SAMPLES, FACES, FACE, FACE, CH), 1.0, 6.0, ((0, 4), (2, 2), (3, 4))),
        "extra_inputs": centred(key_list[1], (SAMPLES, FACES, FACE, FACE, EXTRA), 1.0, 6.0, ((0, 4), (2, 2), (3, 4))),
        "first_kernel": centred(key_list[2], (3, 3, IN_CH, CH), (9 * IN_CH) ** -0.5, 0.125),
        "first_bias": centred(key_list[3], (CH,), 0.5, 3.0),
        "second_kernel": centred(key_list[4], (3, 3, CH, CH), (9 * CH) ** -0.5, 0.125),
        "second_bias": centred(key_list[5], (CH,), 0.5, 3.0),
        "skip_kernel": centred(key_list[6], (IN_CH, CH), IN_CH ** -0.5, 0.375),
        "skip_bias": centred(key_list[7], (CH,), 0.5, 3.0),
        "seam_table": draw_seam_table(jax.random.fold_in(key_list[10], 71), 0),
        "cotangent": centred(key_list[9], (SAMPLES, FACES, FACE, FACE, CH), 1.0, 6.0, ((0, 4), (2, 2), (3, 4))),
    }


@jax.custom_vjp
def low(v):
    return lax.optimization_barrier(v.astype(jnp.bfloat16)).astype(jnp.float32)

@jax.custom_vjp
def low_back(v):
    return v

def low_keep(v):
    return (low(v), None)

def low_pass(kept, grad):
    return (grad,)

def back_keep(v):
    return (v, None)

def back_low(kept, grad):
    return (low(grad),)
low.defvjp(low_keep, low_pass)
low_back.defvjp(back_keep, back_low)

def face_lines(edge_rows, seam_table):
    face_hot = (seam_table[:, :, 0][:, :, None] == jnp.arange(edge_rows.shape[1], dtype=jnp.int32)[None, None, :]).astype(edge_rows.dtype)
    side_hot = (seam_table[:, :, 1][:, :, None] == jnp.arange(4, dtype=jnp.int32)[None, None, :]).astype(edge_rows.dtype)
    chooser = face_hot[:, :, :, None] * side_hot[:, :, None, :]
    side_lines = jnp.einsum('fsgt,bgtnc->bfsnc', chooser, edge_rows, precision=lax.Precision.HIGHEST, preferred_element_type=jnp.float32).astype(edge_rows.dtype)
    flipped = seam_table[:, :, 2][None, :, :, None, None] == 1
    side_lines = jnp.where(flipped, side_lines[:, :, :, ::-1, :], side_lines)
    corner_rule = seam_table[:, :, 3][None, :, :, None] == 0
    upper_line = side_lines[:, :, 0]
    right_line = side_lines[:, :, 1]
    lower_line = side_lines[:, :, 2]
    left_line = side_lines[:, :, 3]
    upper_left = jnp.where(corner_rule[:, :, 0], upper_line[:, :, 0], left_line[:, :, 0])
    upper_right = jnp.where(corner_rule[:, :, 1], upper_line[:, :, -1], right_line[:, :, 0])
    lower_right = jnp.where(corner_rule[:, :, 2], lower_line[:, :, -1], right_line[:, :, -1])
    lower_left = jnp.where(corner_rule[:, :, 3], lower_line[:, :, 0], left_line[:, :, -1])
    upper_full = jnp.concatenate([upper_left[:, :, None], upper_line, upper_right[:, :, None]], axis=2)
    right_full = jnp.concatenate([upper_right[:, :, None], right_line, lower_right[:, :, None]], axis=2)
    lower_full = jnp.concatenate([lower_left[:, :, None], lower_line, lower_right[:, :, None]], axis=2)
    left_full = jnp.concatenate([upper_left[:, :, None], left_line, lower_left[:, :, None]], axis=2)
    return (upper_full, right_full, lower_full, left_full)

def pad_faces(field, seam_table):
    edge_rows = jnp.stack([field[:, :, 0], field[:, :, :, -1], field[:, :, -1], field[:, :, :, 0]], axis=2)
    upper_full, right_full, lower_full, left_full = face_lines(edge_rows, seam_table)
    middle = jnp.concatenate([left_full[:, :, 1:-1, None], field, right_full[:, :, 1:-1, None]], axis=3)
    return jnp.concatenate([upper_full[:, :, None], middle, lower_full[:, :, None]], axis=2)

def conv_valid(padded, kernel):
    height = padded.shape[2] - 2
    width = padded.shape[3] - 2
    total = None
    for offset_row in range(3):
        for offset_column in range(3):
            window = padded[:, :, offset_row:offset_row + height, offset_column:offset_column + width]
            term = jnp.einsum('bfhwc,cd->bfhwd', window, kernel[offset_row, offset_column], precision=lax.Precision.HIGHEST)
            total = term if total is None else total + term
    return total

def reference(features, extra_inputs, first_kernel, first_bias, second_kernel, second_bias, skip_kernel, skip_bias, seam_table, cotangent):

    def forward(feature_values, extra_values, kernel_one, bias_one, kernel_two, bias_two, kernel_skip, bias_skip):
        joined = jnp.concatenate([feature_values, extra_values], axis=-1)
        pre_one = low_back(conv_valid(pad_faces(joined, seam_table), kernel_one) + bias_one)
        hidden = low(jax.nn.gelu(pre_one, approximate=False))
        pre_two = low_back(conv_valid(pad_faces(hidden, seam_table), kernel_two) + bias_two)
        skipped = jnp.einsum('bfhwc,cd->bfhwd', joined, kernel_skip, precision=lax.Precision.HIGHEST) + bias_skip
        return jax.nn.gelu(pre_two, approximate=False) + skipped
    weights = tuple((value.astype(jnp.float32) for value in (first_kernel, first_bias, second_kernel, second_bias, skip_kernel, skip_bias)))

    def one_sample(totals, sample):
        feature_sample, extra_sample, cotangent_sample = sample
        primals = (feature_sample[None].astype(jnp.float32), extra_sample[None].astype(jnp.float32)) + weights
        result, pullback = jax.vjp(forward, *primals)
        grads = pullback(cotangent_sample[None].astype(jnp.float32))
        totals = tuple((total + grad for total, grad in zip(totals, grads[2:])))
        return (totals, (result[0].astype(jnp.bfloat16), grads[0][0].astype(jnp.bfloat16), grads[1][0].astype(jnp.bfloat16)))
    start = tuple((jnp.zeros(weight.shape, jnp.float32) for weight in weights))
    totals, stacked = lax.scan(one_sample, start, (features, extra_inputs, cotangent))
    return (stacked[0], stacked[1], stacked[2], totals[0], totals[1], totals[2], totals[3], totals[4], totals[5])
```

```python
from functools import partial

import jax
import jax.numpy as jnp
from jax import lax
from jax.experimental import pallas as pl
from jax.experimental.pallas import tpu as pltpu
from jax.sharding import PartitionSpec as P


def extended(value, sides, width):
    for axis, dim in sides:
        size, length = (lax.axis_size(axis), value.shape[dim])
        up = [(i, (i + 1) % size) for i in range(size - 1)]
        down = [(j, i) for i, j in up]
        last = lax.slice_in_dim(value, length - width, length, axis=dim)
        leading = lax.slice_in_dim(value, 0, width, axis=dim)
        before = lax.ppermute(last, axis, up)
        after = lax.ppermute(leading, axis, down)
        value = jnp.concatenate([before, value, after], axis=dim)
    return value


def face_lines(edge_rows, seam_table):
    face_hot = (
        seam_table[:, :, 0][:, :, None]
        == jnp.arange(edge_rows.shape[1], dtype=jnp.int32)[None, None, :]
    ).astype(edge_rows.dtype)
    side_hot = (
        seam_table[:, :, 1][:, :, None] == jnp.arange(4, dtype=jnp.int32)[None, None, :]
    ).astype(edge_rows.dtype)
    chooser = face_hot[:, :, :, None] * side_hot[:, :, None, :]
    side_lines = jnp.einsum(
        "fsgt,bgtnc->bfsnc",
        chooser,
        edge_rows,
        precision=lax.Precision.HIGHEST,
        preferred_element_type=jnp.float32,
    ).astype(edge_rows.dtype)
    flipped = seam_table[:, :, 2][None, :, :, None, None] == 1
    side_lines = jnp.where(flipped, side_lines[:, :, :, ::-1, :], side_lines)
    corner_rule = seam_table[:, :, 3][None, :, :, None] == 0
    upper_line = side_lines[:, :, 0]
    right_line = side_lines[:, :, 1]
    lower_line = side_lines[:, :, 2]
    left_line = side_lines[:, :, 3]
    upper_left = jnp.where(corner_rule[:, :, 0], upper_line[:, :, 0], left_line[:, :, 0])
    upper_right = jnp.where(corner_rule[:, :, 1], upper_line[:, :, -1], right_line[:, :, 0])
    lower_right = jnp.where(corner_rule[:, :, 2], lower_line[:, :, -1], right_line[:, :, -1])
    lower_left = jnp.where(corner_rule[:, :, 3], lower_line[:, :, 0], left_line[:, :, -1])
    upper_full = jnp.concatenate(
        [upper_left[:, :, None], upper_line, upper_right[:, :, None]], axis=2
    )
    right_full = jnp.concatenate(
        [upper_right[:, :, None], right_line, lower_right[:, :, None]], axis=2
    )
    lower_full = jnp.concatenate(
        [lower_left[:, :, None], lower_line, lower_right[:, :, None]], axis=2
    )
    left_full = jnp.concatenate([upper_left[:, :, None], left_line, lower_left[:, :, None]], axis=2)
    return (upper_full, right_full, lower_full, left_full)


def seam_layer(edge_rows, seam_table, place):
    row_index, column_index, row_count, column_count, tile_rows, tile_columns = place
    upper_full, right_full, lower_full, left_full = face_lines(edge_rows, seam_table)
    upper_piece = lax.dynamic_slice_in_dim(
        upper_full, column_index * tile_columns, tile_columns + 2, 2
    )
    lower_piece = lax.dynamic_slice_in_dim(
        lower_full, column_index * tile_columns, tile_columns + 2, 2
    )
    left_piece = lax.dynamic_slice_in_dim(left_full, row_index * tile_rows, tile_rows + 2, 2)
    right_piece = lax.dynamic_slice_in_dim(right_full, row_index * tile_rows, tile_rows + 2, 2)
    grid_rows = lax.broadcasted_iota(jnp.int32, (tile_rows + 2, tile_columns + 2, 1), 0)
    grid_columns = lax.broadcasted_iota(jnp.int32, (tile_rows + 2, tile_columns + 2, 1), 1)
    seam_cells = jnp.zeros(
        upper_piece.shape[:2] + (tile_rows + 2, tile_columns + 2, upper_piece.shape[-1]),
        edge_rows.dtype,
    )
    seam_cells = jnp.where((grid_rows == 0) & (row_index == 0), upper_piece[:, :, None], seam_cells)
    seam_cells = jnp.where(
        (grid_rows == tile_rows + 1) & (row_index == row_count - 1),
        lower_piece[:, :, None],
        seam_cells,
    )
    seam_cells = jnp.where(
        (grid_columns == 0) & (column_index == 0), left_piece[:, :, :, None], seam_cells
    )
    seam_cells = jnp.where(
        (grid_columns == tile_columns + 1) & (column_index == column_count - 1),
        right_piece[:, :, :, None],
        seam_cells,
    )
    return seam_cells


def join_tiles(tile_parts):
    moved = jnp.moveaxis(tile_parts, 0, 2)
    return moved.reshape(
        tile_parts.shape[1],
        tile_parts.shape[2],
        tile_parts.shape[0] * tile_parts.shape[3],
        tile_parts.shape[4],
    )


def face_edges(field):
    row_count = lax.axis_size("ty")
    column_count = lax.axis_size("tx")
    row_edges = jnp.stack([field[:, :, 0], field[:, :, -1]], axis=2)
    column_edges = jnp.stack([field[:, :, :, -1], field[:, :, :, 0]], axis=2)
    row_gathered, column_gathered = (
        lax.all_gather(row_edges[None], ("ty", "tx"), axis=0, tiled=True),
        lax.all_gather(column_edges[None], ("ty", "tx"), axis=0, tiled=True),
    )
    row_grid = row_gathered.reshape((row_count, column_count) + row_edges.shape)
    column_grid = column_gathered.reshape((row_count, column_count) + column_edges.shape)
    upper_edge = join_tiles(row_grid[0, :, :, :, 0])
    lower_edge = join_tiles(row_grid[row_count - 1, :, :, :, 1])
    right_edge = join_tiles(column_grid[:, column_count - 1, :, :, 0])
    left_edge = join_tiles(column_grid[:, 0, :, :, 1])
    return jnp.stack([upper_edge, right_edge, lower_edge, left_edge], axis=2)


def extend(field, seam_table, place):
    rimmed = extended(field, (("ty", 2), ("tx", 3)), 1)
    return rimmed + seam_layer(face_edges(field), seam_table, place)


def collect(grad_padded, seam_table, place):
    row_index, column_index, row_count, column_count, tile_rows, tile_columns = place
    widened = extended(grad_padded.astype(jnp.bfloat16), (("ty", 2), ("tx", 3)), 1).astype(
        grad_padded.dtype
    )
    inside = grad_padded[:, :, 1:-1, 1:-1]
    inside = inside.at[:, :, 0].add(widened[:, :, 0, 2 : tile_columns + 2])
    inside = inside.at[:, :, -1].add(widened[:, :, tile_rows + 3, 2 : tile_columns + 2])
    inside = inside.at[:, :, :, 0].add(widened[:, :, 2 : tile_rows + 2, 0])
    inside = inside.at[:, :, :, -1].add(widened[:, :, 2 : tile_rows + 2, tile_columns + 3])
    inside = inside.at[:, :, 0, 0].add(widened[:, :, 0, 0])
    inside = inside.at[:, :, 0, -1].add(widened[:, :, 0, tile_columns + 3])
    inside = inside.at[:, :, -1, 0].add(widened[:, :, tile_rows + 3, 0])
    inside = inside.at[:, :, -1, -1].add(widened[:, :, tile_rows + 3, tile_columns + 3])
    blank = jnp.zeros(
        grad_padded.shape[:2] + (4, tile_rows * row_count, grad_padded.shape[-1]), jnp.float32
    )
    unused, seam_pull = jax.vjp(
        lambda edge_values: seam_layer(edge_values, seam_table, place), blank
    )
    (edge_grads,) = seam_pull(grad_padded)
    edge_grads = lax.psum(edge_grads, ("ty", "tx"))
    upper_part = lax.dynamic_slice_in_dim(
        edge_grads[:, :, 0], column_index * tile_columns, tile_columns, 2
    )
    right_part = lax.dynamic_slice_in_dim(edge_grads[:, :, 1], row_index * tile_rows, tile_rows, 2)
    lower_part = lax.dynamic_slice_in_dim(
        edge_grads[:, :, 2], column_index * tile_columns, tile_columns, 2
    )
    left_part = lax.dynamic_slice_in_dim(edge_grads[:, :, 3], row_index * tile_rows, tile_rows, 2)
    inside = inside.at[:, :, 0].add(jnp.where(row_index == 0, upper_part, 0.0))
    inside = inside.at[:, :, -1].add(jnp.where(row_index == row_count - 1, lower_part, 0.0))
    inside = inside.at[:, :, :, 0].add(jnp.where(column_index == 0, left_part, 0.0))
    inside = inside.at[:, :, :, -1].add(
        jnp.where(column_index == column_count - 1, right_part, 0.0)
    )
    return inside


def conv_valid(padded, kernel):
    shape_in = padded.shape
    merged = padded.reshape(shape_in[0] * shape_in[1], shape_in[2], shape_in[3], shape_in[4])
    result = lax.conv_general_dilated(
        merged,
        kernel,
        (1, 1),
        "VALID",
        dimension_numbers=("NHWC", "HWIO", "NHWC"),
        preferred_element_type=jnp.float32,
    )
    return result.reshape(
        shape_in[0], shape_in[1], shape_in[2] - 2, shape_in[3] - 2, kernel.shape[-1]
    )


def conv_back(grad_pre, kernel):
    flipped = jnp.transpose(kernel[::-1, ::-1], (0, 1, 3, 2))
    surround = jnp.pad(grad_pre, ((0, 0), (0, 0), (2, 2), (2, 2), (0, 0)))
    return conv_valid(surround, flipped)


def kernel_grad(padded, grad_pre):
    tile_rows = grad_pre.shape[2]
    tile_columns = grad_pre.shape[3]
    pieces = []
    for offset_row in range(3):
        for offset_column in range(3):
            window = padded[
                :,
                :,
                offset_row : offset_row + tile_rows,
                offset_column : offset_column + tile_columns,
            ]
            pieces.append(
                jnp.einsum("sfhwc,sfhwd->cd", window, grad_pre, preferred_element_type=jnp.float32)
            )
    return jnp.stack(pieces).reshape(3, 3, padded.shape[-1], grad_pre.shape[-1])


def per_device(
    features,
    extra_inputs,
    first_kernel,
    first_bias,
    second_kernel,
    second_bias,
    skip_kernel,
    skip_bias,
    seam_table,
    cotangent,
):
    place = (
        lax.axis_index("ty"),
        lax.axis_index("tx"),
        lax.axis_size("ty"),
        lax.axis_size("tx"),
        features.shape[2],
        features.shape[3],
    )
    gelu_exact = partial(jax.nn.gelu, approximate=False)
    joined = jnp.concatenate([features, extra_inputs], axis=-1)
    padded_one = extend(joined, seam_table, place)
    pre_one = conv_valid(padded_one, first_kernel) + first_bias
    active_one, slope_one = jax.vjp(gelu_exact, pre_one)
    hidden = active_one.astype(jnp.bfloat16)
    padded_two = extend(hidden, seam_table, place)
    pre_two = conv_valid(padded_two, second_kernel) + second_bias
    active_two, slope_two = jax.vjp(gelu_exact, pre_two)
    skipped = (
        jnp.einsum("sfhwc,cd->sfhwd", joined, skip_kernel, preferred_element_type=jnp.float32)
        + skip_bias
    )
    block_output = (active_two + skipped).astype(jnp.bfloat16)
    (grad_two,) = slope_two(cotangent.astype(jnp.float32))
    grad_two = grad_two.astype(jnp.bfloat16)
    second_kernel_grad = kernel_grad(padded_two, grad_two)
    second_bias_grad = jnp.sum(grad_two, axis=(0, 1, 2, 3), dtype=jnp.float32)
    grad_hidden = collect(conv_back(grad_two, second_kernel), seam_table, place)
    (grad_one,) = slope_one(grad_hidden)
    grad_one = grad_one.astype(jnp.bfloat16)
    first_kernel_grad = kernel_grad(padded_one, grad_one)
    first_bias_grad = jnp.sum(grad_one, axis=(0, 1, 2, 3), dtype=jnp.float32)
    grad_joined = collect(conv_back(grad_one, first_kernel), seam_table, place)
    grad_joined = grad_joined + jnp.einsum(
        "sfhwd,cd->sfhwc", cotangent, skip_kernel, preferred_element_type=jnp.float32
    )
    skip_kernel_grad = jnp.einsum(
        "sfhwc,sfhwd->cd", joined, cotangent, preferred_element_type=jnp.float32
    )
    skip_bias_grad = jnp.sum(cotangent, axis=(0, 1, 2, 3), dtype=jnp.float32)
    summed = lax.psum(
        (
            first_kernel_grad,
            first_bias_grad,
            second_kernel_grad,
            second_bias_grad,
            skip_kernel_grad,
            skip_bias_grad,
        ),
        ("dp", "ty", "tx"),
    )
    grad_joined = grad_joined.astype(jnp.bfloat16)
    channels = features.shape[-1]
    return (
        block_output,
        grad_joined[..., :channels],
        grad_joined[..., channels:],
        summed[0],
        summed[1],
        summed[2],
        summed[3],
        summed[4],
        summed[5],
    )


TAPS = 9
SUM_ROWS = 2560
LANES = 128
PACK = 27
ONE = 27


def whole_block(
    x_in, ext_in, w1_in, w2_in, skip_in, biases, table, cot_in,
    out_ref, gx_ref, gext_ref, suma_ref, sumb_ref,
    w1, w2, wskip, we, wse, sel_t, rule,
    xv, ev, cv, t27, xc, hc, pre, slope, slev, sleh, cev, ceh,
    ost, ff, evf, ehf, rvf, rhf, cvf, chf, rc1v, rc1h, rc2v, rc2h, gev, geh,
    acca, accb, outa, landa, bufs, ssem, rsem, sum_ssem, sum_rsem, credit, ack, lsem,
):
    f32, bf = jnp.float32, jnp.bfloat16
    dp, ty, tx = lax.axis_index("dp"), lax.axis_index("ty"), lax.axis_index("tx")
    core, xx, place = dp % 2, dp // 2, ty * 4 + tx
    core_mate, x_mate = dp + 1 - 2 * core, dp + 2 - 4 * xx
    faces, rows, cols = x_in.shape[0], x_in.shape[1], x_in.shape[2]
    area = rows * cols
    is_mid = jnp.where((tx == 0) | (tx == 3), 0, 1)
    hx = jnp.where(tx >= 2, 1, 0)
    kk = ty + 2 * hx
    mm = kk + 4 * is_mid
    at_end = is_mid == 0

    def dev(y, x):
        return {"ty": y, "tx": x}

    def rows16(start, size):
        return pl.ds(pl.multiple_of(start, 16), size)

    def home(m):
        half = (m // 2) % 2
        return m % 2, (3 * half if m // 4 == 0 else 1 + half)

    def home_class(k):
        half = k // 2
        return k % 2, jnp.where(at_end, 3 * half, 1 + half)

    def flip48(flag, k, n):
        return 48 * jnp.where(flag, n - 1 - k, k)

    class Exchange:
        def __init__(self, index):
            self.index = index
            self.ed_v, self.ed_h, self.db, self.sb, self.rg_v, self.rg_h, self.rg_c, self.xw, self.xd = bufs[index]
            self.sent = []
            self.slot = 0

        def send(self, cond, src, dst, rs, target):
            copy = pltpu.make_async_remote_copy(
                src_ref=src, dst_ref=dst, send_sem=ssem.at[self.index, self.slot],
                recv_sem=rsem.at[self.index, rs], device_id=target, device_id_type=pl.DeviceIdType.MESH,
            )
            self.slot += 1
            self.sent.append((cond, copy))
            if cond is None:
                copy.start()
            else:
                pl.when(cond)(copy.start)

        def get(self, cond, dst, rs):
            copy = pltpu.make_async_remote_copy(
                src_ref=dst, dst_ref=dst, send_sem=ssem.at[self.index, 0],
                recv_sem=rsem.at[self.index, rs], device_id=dev(1 - ty, tx), device_id_type=pl.DeviceIdType.MESH,
            )
            if cond is None:
                copy.wait_recv()
            else:
                pl.when(cond)(copy.wait_recv)

        def drain(self):
            for cond, copy in self.sent:
                if cond is None:
                    copy.wait_send()
                else:
                    pl.when(cond)(copy.wait_send)

        def move(self, cond, dst, dst_at, src, src_at):
            @pl.when(cond)
            def _():
                dst[dst_at] = src[src_at]

    class Forward(Exchange):
        def start(self):
            ed_v, ed_h, db = self.ed_v, self.ed_h, self.db
            for k in range(4):
                at = rows16(flip48(hx == 1, k, 4), 48)
                to = rows16((2 * ty) * 96 + hx * 48, 48)
                y, x = home_class(k)
                self.send(kk != k, ed_v.at[ty, at], db.at[to], (2 * ty) * 2 + hx, dev(y, x))
                self.move(kk == k, db, (to,), ed_v, (ty, at))
            for m in range(8):
                at = rows16(flip48(ty == 1, m, 8), 48)
                side = jnp.where(hx == 1, 1, 3)
                to = rows16(side * 96 + ty * 48, 48)
                y, x = home(m)
                self.send(at_end & (mm != m), ed_h.at[hx, at], db.at[to], side * 2 + ty, dev(y, x))
                self.move(at_end & (mm == m), db, (to,), ed_h, (hx, at))
            rg_v, rg_h, rg_c = self.rg_v, self.rg_h, self.rg_c
            self.send(None, ed_v.at[1 - ty], rg_v.at[ty], 24, dev(1 - ty, tx))
            self.send(tx < 3, ed_h.at[1], rg_h.at[0], 25, dev(ty, tx + 1))
            self.send(tx > 0, ed_h.at[0], rg_h.at[1], 26, dev(ty, tx - 1))
            self.send(tx < 3, ed_v.at[1 - ty, pl.ds(176, 16)], rg_c.at[2 * ty], 20 + 2 * ty, dev(1 - ty, tx + 1))
            self.send(tx > 0, ed_v.at[1 - ty, pl.ds(0, 16)], rg_c.at[2 * ty + 1], 21 + 2 * ty, dev(1 - ty, tx - 1))

        def middle(self):
            db, sb = self.db, self.sb
            for t in range(4):
                for h in range(2):
                    if t % 2 == 0:
                        own = (ty == t // 2) & (hx == h)
                    else:
                        own = at_end & (ty == h) & (tx == (0 if t == 3 else 3))
                    self.get(jnp.logical_not(own), db.at[pl.ds(t * 96 + h * 48, 48)], t * 2 + h)
            sb[...] = dot_tn(sel_t[...], db[...]).astype(bf)
            for y in range(2):
                for h in range(2):
                    x = jnp.where(at_end, 3 * h, 1 + h)
                    own = (ty == y) & (tx == x)
                    at = pl.ds(2 * y * 96 + h * 48, 48)
                    to = rows16(48 * ((3 - kk) if h else kk), 48)
                    self.send(jnp.logical_not(own), sb.at[at], self.rg_v.at[y, to], 8 + kk, dev(y, x))
                    self.move(own, self.rg_v, (y, to), sb, (at,))
            for y in range(2):
                for h in range(2):
                    own = (ty == y) & (tx == 3 * h)
                    at = pl.ds((1 if h else 3) * 96 + y * 48, 48)
                    to = rows16(48 * ((7 - mm) if y else mm), 48)
                    self.send(jnp.logical_not(own), sb.at[at], self.rg_h.at[h, to], 12 + mm, dev(y, 3 * h))
                    self.move(own, self.rg_h, (h, to), sb, (at,))
            for y in range(2):
                for m, x, right, at in ((3, 1, 0, 32), (3, 2, 1, 48), (4, 3, 0, 80), (4, 0, 1, 0), (7, 2, 0, 32), (7, 1, 1, 48)):
                    spot = 2 * y + right
                    src = (pl.ds(2 * y * 96 + at, 16),)
                    if home(m) == (y, x):
                        self.move(mm == m, self.rg_c, (spot,), sb, src)
                    else:
                        self.send(mm == m, sb.at[src], self.rg_c.at[spot], 20 + spot, dev(y, x))
                for h in range(2):
                    spot = 2 * (1 - y) + h
                    src = pl.ds((1 if h else 3) * 96 + (32 if y else 48), 16)
                    self.send(mm == 7, sb.at[src], self.rg_c.at[spot], 20 + spot, dev(y, 3 * h))

        def finish(self):
            self.get(None, self.rg_v.at[1 - ty], 24)
            self.get(tx > 0, self.rg_h.at[0], 25)
            self.get(tx < 3, self.rg_h.at[1], 26)
            for k in range(4):
                self.get(kk != k, self.rg_v.at[ty, rows16(flip48(hx == 1, k, 4), 48)], 8 + k)
            for m in range(8):
                self.get(at_end & (mm != m), self.rg_h.at[hx, rows16(flip48(ty == 1, m, 8), 48)], 12 + m)
            for spot in range(4):
                y, right = spot // 2, spot % 2
                face_corner = (ty == y) & (tx == 3 * right)
                if spot == 2:
                    own = (ty == 1) & (tx == 2)
                    skip = face_corner | own
                else:
                    skip = face_corner
                self.get(jnp.logical_not(skip), self.rg_c.at[spot], 20 + spot)

    class Backward(Exchange):
        def start(self):
            rg_v, rg_h, rg_c, sb, xw, xd = self.rg_v, self.rg_h, self.rg_c, self.sb, self.xw, self.xd
            for k in range(4):
                at = rows16(flip48(hx == 1, k, 4), 48)
                to = rows16((2 * ty) * 96 + hx * 48, 48)
                y, x = home_class(k)
                self.send(kk != k, rg_v.at[ty, at], sb.at[to], (2 * ty) * 2 + hx, dev(y, x))
                self.move(kk == k, sb, (to,), rg_v, (ty, at))
            for m in range(8):
                at = rows16(flip48(ty == 1, m, 8), 48)
                side = jnp.where(hx == 1, 1, 3)
                to = rows16(side * 96 + ty * 48, 48)
                y, x = home(m)
                self.send(at_end & (mm != m), rg_h.at[hx, at], sb.at[to], side * 2 + ty, dev(y, x))
                self.move(at_end & (mm == m), sb, (to,), rg_h, (hx, at))
            for right in range(2):
                spot = 2 * ty + right
                away = (tx < 3) if right else (tx > 0)
                if right:
                    x, y = jnp.where(tx == 0, 1, jnp.where(tx == 1, 2, 3)), jnp.where(tx == 0, 0, 1)
                else:
                    x, y = jnp.where(tx == 1, 3, jnp.where(tx == 2, 2, 1)), jnp.where(tx == 3, 0, 1)
                own = away & (ty == y) & (tx == x)
                slot = ty * 2 + right
                self.send(away & jnp.logical_not(own), rg_c.at[spot], xw.at[slot], 8 + slot, dev(y, x))
                self.move(own, xw, (slot,), rg_c, (spot,))
                inner = 2 * (1 - ty) + right
                edge = (tx == 3) if right else (tx == 0)
                self.send(edge, rg_c.at[inner], xw.at[4 + ty * 2 + right], 12 + ty * 2 + right, dev(1, 2))
                self.send(away, rg_c.at[inner], xd.at[1 - right], 16 + 1 - right, dev(1 - ty, tx + (1 if right else -1)))
            ed_v, ed_h = self.ed_v, self.ed_h
            self.send(None, rg_v.at[1 - ty], ed_v.at[ty], 30, dev(1 - ty, tx))
            self.send(tx < 3, rg_h.at[1], ed_h.at[0], 31, dev(ty, tx + 1))
            self.send(tx > 0, rg_h.at[0], ed_h.at[1], 32, dev(ty, tx - 1))

        def middle(self):
            sb, db, xw = self.sb, self.db, self.xw
            for s in range(4):
                for h in range(2):
                    if s % 2 == 0:
                        own = (ty == s // 2) & (hx == h)
                    else:
                        own = at_end & (ty == h) & (tx == (0 if s == 3 else 3))
                    self.get(jnp.logical_not(own), sb.at[pl.ds(s * 96 + h * 48, 48)], s * 2 + h)
            for y in range(2):
                for right in range(2):
                    slot = 2 * y + right
                    wants = (mm == 3) | (mm == 4) | (mm == 7)
                    if slot == 2:
                        wants = (mm == 3) | (mm == 4)
                    self.get(wants, xw.at[slot], 8 + slot)
                    self.get(mm == 7, xw.at[4 + slot], 12 + slot)
                    for m, at in ((3, 48 if right else 32), (4, 0 if right else 80), (7, 48 if right else 32)):
                        @pl.when(mm == m)
                        def _(spot=2 * y * 96 + at, slot=slot):
                            here = pl.ds(spot, 16)
                            sb[here] = (sb[here].astype(f32) + xw[slot].astype(f32)).astype(bf)

                    @pl.when(mm == 7)
                    def _(spot=(1 if right else 3) * 96 + (32 if y else 48), slot=4 + slot):
                        here = pl.ds(spot, 16)
                        sb[here] = (sb[here].astype(f32) + xw[slot].astype(f32)).astype(bf)
            db[...] = dot(sel_t[...], sb[...]).astype(bf)
            for y in range(2):
                for h in range(2):
                    x = jnp.where(at_end, 3 * h, 1 + h)
                    own = (ty == y) & (tx == x)
                    at = pl.ds(2 * y * 96 + h * 48, 48)
                    to = rows16(48 * ((3 - kk) if h else kk), 48)
                    self.send(jnp.logical_not(own), db.at[at], self.ed_v.at[y, to], 18 + kk, dev(y, x))
                    self.move(own, self.ed_v, (y, to), db, (at,))
            for y in range(2):
                for h in range(2):
                    own = (ty == y) & (tx == 3 * h)
                    at = pl.ds((1 if h else 3) * 96 + y * 48, 48)
                    to = rows16(48 * ((7 - mm) if y else mm), 48)
                    self.send(jnp.logical_not(own), db.at[at], self.ed_h.at[h, to], 22 + mm, dev(y, 3 * h))
                    self.move(own, self.ed_h, (h, to), db, (at,))

        def finish(self):
            self.get(None, self.ed_v.at[1 - ty], 30)
            self.get(tx > 0, self.ed_h.at[0], 31)
            self.get(tx < 3, self.ed_h.at[1], 32)
            self.get(tx > 0, self.xd.at[0], 16)
            self.get(tx < 3, self.xd.at[1], 17)
            for k in range(4):
                self.get(kk != k, self.ed_v.at[ty, rows16(flip48(hx == 1, k, 4), 48)], 18 + k)
            for m in range(8):
                self.get(at_end & (mm != m), self.ed_h.at[hx, rows16(flip48(ty == 1, m, 8), 48)], 22 + m)

        def stage(self, blocks):
            for j in range(blocks):
                lanes = slice(128 * j, 128 * j + 128)
                for s in range(2):
                    evf[j, s] = self.ed_v[s, :, lanes].astype(f32)
                    ehf[j, s] = self.ed_h[s, :, lanes].astype(f32)

                @pl.when(tx > 0)
                def _(j=j, lanes=lanes):
                    evf[j, 1 - ty, pl.ds(0, 16)] += self.xd[0, :, lanes].astype(f32)

                @pl.when(tx < 3)
                def _(j=j, lanes=lanes):
                    evf[j, 1 - ty, pl.ds(176, 16)] += self.xd[1, :, lanes].astype(f32)

    class Total:
        def __init__(self, index, acc, out, out0, land, land0):
            self.index, self.acc, self.out, self.land = index, acc, out, land
            self.out0, self.land0 = out0, land0
            self.half = SUM_ROWS // 2 * core
            self.other_half = SUM_ROWS // 2 * (1 - core)
            self.quarter = self.half + SUM_ROWS // 4 * xx
            self.other_quarter = self.half + SUM_ROWS // 4 * (1 - xx)
            self.own = self.quarter + SUM_ROWS // 32 * place

        def copy(self, slot, src, dst, rslot, target):
            return pltpu.make_async_remote_copy(
                src_ref=src, dst_ref=dst, send_sem=sum_ssem.at[self.index, slot],
                recv_sem=sum_rsem.at[self.index, rslot], device_id=target, device_id_type=pl.DeviceIdType.MESH,
            )

        def outs(self, start, size):
            return self.out.at[rows16(self.out0 + start, size)]

        def lands(self, start, size):
            return self.land.at[rows16(self.land0 + start, size)]

        def cast(self, start, size):
            step = SUM_ROWS // 32

            @pl.loop(0, size // step)
            def _(i):
                at = start + i * step
                self.out[rows16(self.out0 + at, step)] = self.acc[rows16(at, step)].astype(bf)

        def add(self, start, size, land):
            step = SUM_ROWS // 32

            @pl.loop(0, size // step)
            def _(i):
                self.acc[rows16(start + i * step, step)] += self.land[
                    rows16(self.land0 + land + i * step, step)].astype(f32)

        def to_core(self):
            if self.index:
                pl.semaphore_wait(credit.at[0], 1)
            size = SUM_ROWS // 2
            self.cast(self.other_half, size)
            self.first = self.copy(0, self.outs(self.other_half, size), self.lands(0, size), 0, {"dp": core_mate})
            self.first.start()

        def to_x(self):
            if self.index:
                pl.semaphore_wait(credit.at[1], 1)
            self.first.wait()
            pl.semaphore_signal(ack.at[self.index, 0], inc=1, device_id={"dp": core_mate}, device_id_type=pl.DeviceIdType.MESH)
            size = SUM_ROWS // 4
            self.add(self.half, SUM_ROWS // 2, 0)
            self.cast(self.other_quarter, size)
            self.second = self.copy(
                1, self.outs(self.other_quarter, size), self.lands(SUM_ROWS // 2, size), 1, {"dp": x_mate})
            self.second.start()

        def peers(self):
            for q in range(8):
                yield q, place != q, {"ty": q // 4, "tx": q % 4}

        def to_group(self):
            if self.index:
                pl.semaphore_wait(credit.at[2], 7)
            self.second.wait()
            size, step = SUM_ROWS // 4, SUM_ROWS // 32
            self.add(self.quarter, size, SUM_ROWS // 2)

            @pl.loop(0, 8)
            def _(q):
                here = self.acc[rows16(self.quarter + step * q, step)]
                self.land[rows16(self.land0 + step * q, step)] = here.astype(bf)

            pl.semaphore_signal(ack.at[self.index, 1], inc=1, device_id={"dp": x_mate}, device_id_type=pl.DeviceIdType.MESH)
            self.third = []
            base = SUM_ROWS // 4 * 3
            for q, cond, target in self.peers():
                copy = self.copy(2 + q, self.lands(step * q, step), self.lands(base + step * place, step), 2 + place, target)
                pl.when(cond)(copy.start)
                self.third.append((cond, copy))

        def got(self, slot, dst):
            return self.copy(slot, dst, dst, slot, {"dp": core_mate})

        def from_group(self):
            step, base = SUM_ROWS // 32, SUM_ROWS // 4 * 3
            for q, cond, _ in self.peers():
                pl.when(cond)(self.got(2 + q, self.lands(base + step * q, step)).wait_recv)
            for q, cond, _ in self.peers():
                @pl.when(cond)
                def _(q=q):
                    self.acc[rows16(self.own, step)] += self.land[rows16(self.land0 + base + step * q, step)].astype(f32)
            for cond, copy in self.third:
                pl.when(cond)(copy.wait_send)
            self.cast(self.own, step)
            self.fourth = []
            for q, cond, target in self.peers():
                copy = self.copy(10 + q, self.outs(self.own, step), self.outs(self.own, step), 10 + place, target)
                pl.when(cond)(copy.start)
                self.fourth.append((cond, copy))

        def back_x(self):
            step = SUM_ROWS // 32
            for q, cond, _ in self.peers():
                pl.when(cond)(self.got(10 + q, self.outs(self.quarter + step * q, step)).wait_recv)
            size = SUM_ROWS // 4
            pl.semaphore_wait(ack.at[self.index, 1], 1)
            self.fifth = self.copy(18, self.outs(self.quarter, size), self.outs(self.quarter, size), 18, {"dp": x_mate})
            self.fifth.start()

        def back_core(self):
            self.got(18, self.outs(self.other_quarter, SUM_ROWS // 4)).wait_recv()
            size = SUM_ROWS // 2
            pl.semaphore_wait(ack.at[self.index, 0], 1)
            self.sixth = self.copy(19, self.outs(self.half, size), self.outs(self.half, size), 19, {"dp": core_mate})
            self.sixth.start()

        def finish(self, ref, sem):
            self.got(19, self.outs(self.other_half, SUM_ROWS // 2)).wait_recv()
            for cond, copy in self.fourth:
                pl.when(cond)(copy.wait_send)
            self.fifth.wait_send()
            self.sixth.wait_send()
            self.store = pltpu.make_async_copy(self.outs(0, SUM_ROWS), ref, lsem.at[sem])
            self.store.start()

    def dot(a, b):
        return jnp.dot(a, b, preferred_element_type=f32)

    def dot_nt(a, b):
        return lax.dot_general(a, b, (((1,), (1,)), ((), ())), preferred_element_type=f32)

    def dot_tn(a, b):
        return lax.dot_general(a, b, (((0,), (0,)), ((), ())), preferred_element_type=f32)

    def cat(parts, axis=-1):
        return jnp.concatenate(parts, axis=axis)

    def face_rows(f):
        return pl.ds(pl.multiple_of(f * area, area), area)

    def top(f, s):
        return pl.ds(f * area + (area - cols if s else 0), cols)

    def side(f, s):
        return pl.ds(f * area + (cols - 1 if s else 0), rows, stride=cols)

    def ring_v(f):
        return pl.ds(f, cols, stride=faces)

    def ring_h(f):
        return pl.ds(f, rows, stride=faces)

    def shifts(v):
        zero = jnp.zeros((rows, 1, v.shape[-1]), v.dtype)
        return cat([zero, v[:, : cols - 1]], 1), cat([v[:, 1:], zero], 1)

    def fill(ref, v):
        left, right = shifts(v)
        wide = v.shape[-1]
        ref[1 : rows + 1, :, 0:wide] = left
        ref[1 : rows + 1, :, wide : 2 * wide] = v
        ref[1 : rows + 1, :, 2 * wide : 3 * wide] = right

    def windows(ref):
        return [ref[a : a + rows].reshape(area, ref.shape[-1]) for a in range(3)]

    def split(ref, at, v):
        for h in range(2):
            ref[(h,) + at] = v[:, 128 * h : 128 * h + 128]

    def join(ref, at, blocks=2):
        return cat([ref[(h,) + at] for h in range(blocks)])

    def gelu_slope(u):
        phi = 0.5 + 0.5 * lax.erf(u * 0.7071067811865476)
        return u * phi, phi + u * (0.3989422804014327 * jnp.exp(-0.5 * u * u))

    lane = lax.broadcasted_iota(jnp.int32, (1, LANES), 1)

    first, second = Forward(0), Forward(1)
    third, fourth = Backward(2), Backward(3)
    def load(src, dst, sem):
        copy = pltpu.make_async_copy(src, dst, lsem.at[sem])
        copy.start()
        return copy

    eload, xload = load(ext_in, ev, 1), load(x_in, xv, 0)
    w1load, skipload = load(w1_in, w1, 5), load(skip_in, wskip, 6)
    cload, w2load = load(cot_in, cv, 2), load(w2_in, w2, 7)
    barrier = pltpu.get_barrier_semaphore()
    for e in (0, 1):
        bufs[e][6][...] = jnp.zeros_like(bufs[e][6])
    for y in range(2):
        for x in range(4):
            @pl.when((ty != y) | (tx != x))
            def _(y=y, x=x):
                pl.semaphore_signal(barrier, inc=1, device_id=dev(y, x), device_id_type=pl.DeviceIdType.MESH)
    for mate in (core_mate, x_mate):
        pl.semaphore_signal(barrier, inc=1, device_id={"dp": mate}, device_id_type=pl.DeviceIdType.MESH)
    pl.semaphore_wait(barrier, 9)

    for ref in (xc[0], xc[1]):
        ref[0] = jnp.zeros(ref.shape[1:], bf)
        ref[rows + 1] = jnp.zeros(ref.shape[1:], bf)

    @pl.loop(0, faces)
    def _(f):
        hc[f, 0] = jnp.zeros(hc.shape[2:], bf)
        hc[f, rows + 1] = jnp.zeros(hc.shape[2:], bf)
        t27[f, 0] = jnp.zeros(t27.shape[2:], bf)
        t27[f, rows + 1] = jnp.zeros(t27.shape[2:], bf)

    count, span = 9 * cols, cols * LANES
    eload.wait()
    turned = cat([ev[f].astype(f32).reshape(count, rows).T for f in range(faces)], 0).astype(bf)

    def packing(moves):
        line = lax.broadcasted_iota(jnp.int32, (count, span), 0)
        spot = lax.broadcasted_iota(jnp.int32, (count, span), 1)
        channel, column, to_column, to_lane = line // cols, line % cols, spot // LANES, spot % LANES
        hot = jnp.zeros((count, span), f32)
        for start, step in moves:
            hot = hot + jnp.where((to_lane == start + channel) & (column == to_column + step), 1.0, 0.0)
        return hot.astype(bf)

    flat = dot(turned, packing([(0, -1), (9, 0), (18, 1)]))
    for c in range(cols):
        pre[0, pl.ds(c * faces * rows, faces * rows)] = flat[:, c * LANES : c * LANES + LANES]
    xload.wait()

    @pl.loop(0, faces)
    def _(f):
        for c in range(cols):
            ff[2, pl.ds(c, rows, stride=cols)] = pre[0, pl.ds(c * faces * rows + f * rows, rows)]
        packed = ff[2] + jnp.where(lane == ONE, 1.0, 0.0)
        t27[f, 1 : rows + 1] = packed.astype(bf).reshape(rows, cols, LANES)
        ff[2] = jnp.where(lane < 9, pltpu.roll(packed, LANES - 9, axis=1), 0.0)
        for h in range(2):
            ff[h] = xv[f, :, :, 128 * h : 128 * h + 128].astype(f32).reshape(area, LANES)
        for j in range(3):
            for s in range(2):
                evf[j, s, ring_v(f)] = ff[j, pl.ds(area - cols if s else 0, cols)]
                ehf[j, s, ring_h(f)] = ff[j, pl.ds(cols - 1 if s else 0, rows, stride=cols)]

    def edges_out(ex, blocks):
        for s in range(2):
            ex.ed_v[s] = join(evf, (s,), blocks).astype(bf)
            ex.ed_h[s] = join(ehf, (s,), blocks).astype(bf)

    edges_out(first, 3)
    first.start()

    acca[...] = jnp.zeros_like(acca)
    accb[...] = jnp.zeros_like(accb)
    w1load.wait()
    skipload.wait()
    ff[...] = jnp.zeros_like(ff)
    for h in range(2):
        lanes = slice(128 * h, 128 * h + 128)
        for a in range(3):
            for b in range(3):
                ff[h, pl.ds(128 * a + 9 * b, 9)] = w1[3 * a + b, 256:265, lanes].astype(f32)
        ff[h, pl.ds(128 + ONE, 1)] = biases[0:1, lanes].astype(f32)
        ff[h, pl.ds(384 + 9, 9)] = wskip[256:265, lanes].astype(f32)
        ff[h, pl.ds(384 + ONE, 1)] = biases[2:3, lanes].astype(f32)
        for a in range(3):
            we[a, :, lanes] = ff[h, pl.ds(128 * a, 128)].astype(bf)
        wse[:, lanes] = ff[h, pl.ds(384, 128)].astype(bf)
    total = 32 * faces
    spread = jnp.where(
        lax.broadcasted_iota(jnp.int32, (faces, total), 1) % faces
        == lax.broadcasted_iota(jnp.int32, (faces, total), 0), 1.0, 0.0)
    spot = lax.broadcasted_iota(jnp.int32, (1, total), 1)
    side_of, step_of = spot // (8 * faces), (spot // faces % 8).astype(f32)
    source = jnp.zeros((1, total), f32)
    for s in range(4):
        entry = dot(table[s].astype(f32), spread)
        step = jnp.where(entry[2:3] > 0.5, 7.0 - step_of, step_of)
        source = source + jnp.where(side_of == s, (entry[1:2] * 8.0 + step) * faces + entry[0:1], 0.0)
    sel_t[...] = jnp.where(
        lax.broadcasted_iota(jnp.int32, (total, total), 0) == source.astype(jnp.int32), 1.0, 0.0).astype(bf)
    same = jnp.where(
        lax.broadcasted_iota(jnp.int32, (faces, faces), 1) == lax.broadcasted_iota(jnp.int32, (faces, faces), 0), 1.0, 0.0)
    for spot_index, k in enumerate((0, 1, 3, 2)):
        column = jnp.sum(same * table[k, 3:4].astype(f32), axis=1, keepdims=True)
        rule[spot_index, 0:faces] = jnp.broadcast_to(1.0 - column, (faces, LANES))

    def ring_in(ex, blocks):
        for j in range(blocks):
            lanes = slice(128 * j, 128 * j + 128)
            for s in range(2):
                rvf[j, s, pl.ds(12, 192)] = ex.rg_v[s, :, lanes].astype(f32)
                rhf[j, s, pl.ds(12, 384)] = ex.rg_h[s, :, lanes].astype(f32)
            for spot in range(4):
                s, right = spot // 2, spot % 2
                win = ex.rg_c[spot, :, lanes].astype(f32)
                edge = (tx == 3) if right else (tx == 0)
                late = jnp.where(edge, ty == 1, right == 0)
                got = jnp.where(late, win[4:16], win[0:12])
                from_v = rvf[j, s, pl.ds(192 if right else 12, 12)]
                from_h = rhf[j, right, pl.ds(384 if s else 12, 12)]
                local = jnp.where(rule[spot, 0:12] > 0.0, from_v, from_h)
                rvf[j, s, pl.ds(204 if right else 0, 12)] = jnp.where((ty == s) & edge, local, got)

    def ring_cat(rcv, rch, blocks):
        for s in range(2):
            for b in range(3):
                for j in range(2):
                    at = slice(256 * b + 128 * j, 256 * b + 128 * j + 128)
                    rcv[s, :, at] = rvf[j, s, pl.ds(12 * b, 192)].astype(bf)
                    rch[s, :, at] = rhf[j, s, pl.ds(12 * b, 384)].astype(bf)
            if blocks == 3:
                total = rvf[2, s, pl.ds(0, 192)]
                for b in (1, 2):
                    total = total + pltpu.roll(rvf[2, s, pl.ds(12 * b, 192)], 9 * b, axis=1)
                rcv[s, :, 768:896] = total.astype(bf)
                for a in range(3):
                    line = rhf[2, s, pl.ds(12 * a, 384)]
                    line = pltpu.roll(line, 18, axis=1) if s else line
                    rch[s, :, 768 + 128 * a : 896 + 128 * a] = line.astype(bf)

    def zero_h_ends(blocks):
        for j in range(blocks):
            for s in range(2):
                rhf[j, s, pl.ds(0, 12)] = jnp.zeros((12, LANES), f32)
                rhf[j, s, pl.ds(396, 12)] = jnp.zeros((12, LANES), f32)

    zero_h_ends(3)

    def add_to_edges(source_v, source_h):
        @pl.loop(0, faces)
        def _(f):
            for h in range(2):
                for s in range(2):
                    pre[h, top(f, s)] += source_v[h, s, ring_v(f)]
            for h in range(2):
                for s in range(2):
                    pre[h, side(f, s)] += source_h[h, s, ring_h(f)]
            for h in range(2):
                for s in range(2):
                    evf[h, s, ring_v(f)] = pre[h, top(f, s)]
                    ehf[h, s, ring_h(f)] = pre[h, side(f, s)]

    def w_first(t):
        return w1[t, 0:256]

    def conv_first(f, ref):
        lhs = cat(windows(ref) + windows(t27.at[f]))
        rhs = cat([w_first(t) for t in range(TAPS)] + [we[a] for a in range(3)], 0)
        split(pre, (face_rows(f),), dot(lhs, rhs))

    def first_part(lo, hi):
        @pl.loop(lo, hi)
        def _(i):
            for u in range(2):
                fill(xc[u], xv[2 * i + u])
            for u in range(2):
                conv_first(2 * i + u, xc[u])

    first_part(0, 3)
    first.middle()
    first_part(3, 6)
    cload.wait()

    @pl.loop(0, faces)
    def _(f):
        for h in range(2):
            ff[h] = cv[f, :, 128 * h : 128 * h + 128].astype(f32)
            for s in range(2):
                cvf[h, s, ring_v(f)] = ff[h, pl.ds(area - cols if s else 0, cols)]
                chf[h, s, ring_h(f)] = ff[h, pl.ds(cols - 1 if s else 0, rows, stride=cols)]

    for s in range(2):
        cev[s] = join(cvf, (s,)).astype(bf)
        ceh[s] = join(chf, (s,)).astype(bf)
    first.finish()
    ring_in(first, 3)
    ring_cat(rc1v, rc1h, 3)
    for s in range(2):
        rhs = cat([w_first(6 * s + b) for b in range(3)] + [we[2 * s]], 0)
        split(cvf, (s,), dot(rc1v[s], rhs))
        rhs = cat([w_first(3 * a + 2 * s) for a in range(3)] + [we[a] for a in range(3)], 0)
        split(chf, (s,), dot(rc1h[s], rhs))
    add_to_edges(cvf, chf)
    for h in range(2):
        for s in range(2):
            evf[h, s], slev[h, s] = gelu_slope(evf[h, s])
            ehf[h, s], sleh[h, s] = gelu_slope(ehf[h, s])
    edges_out(second, 2)
    second.start()

    def conv_second(f):
        lhs = cat(windows(hc.at[f]))
        rhs = cat([w2[t] for t in range(TAPS)], 0)
        split(pre, (face_rows(f),), dot(lhs, rhs))

    def second_part(lo, hi):
        @pl.loop(lo, hi)
        def _(i):
            for u in range(2):
                f = 2 * i + u
                act, sl = gelu_slope(join(pre, (face_rows(f),)))
                slope[face_rows(f)] = sl.astype(bf)
                fill(hc.at[f], act.astype(bf).reshape(rows, cols, 256))
            for u in range(2):
                conv_second(2 * i + u)

    w2load.wait()
    second_part(0, 3)
    second.middle()
    second_part(3, 6)
    second.finish()
    ring_in(second, 2)
    ring_cat(rc2v, rc2h, 2)
    for s in range(2):
        split(cvf, (s,), dot(rc2v[s], cat([w2[6 * s + b] for b in range(3)], 0)))
        split(chf, (s,), dot(rc2h[s], cat([w2[3 * a + 2 * s] for a in range(3)], 0)))
    add_to_edges(cvf, chf)

    def ring_grads(ex, taps, blocks):
        for s in range(2):
            lhs = cat([cat([rvf[j, s, pl.ds(12 * b, 216)] for j in range(2)]).astype(bf) for b in range(3)])
            base = 0 if s else 6
            rhs = cat([taps(8 - (base + b)) for b in range(3)], 1)
            out = dot_nt(lhs, rhs)
            if blocks == 3:
                mid = dot_nt(gev[s], we[2 * s])
                pad = jnp.zeros((24, LANES), f32)
                mid = cat([pad, mid, pad], 0)
                tail = mid[24:240]
                for b in (1, 2):
                    tail = tail + pltpu.roll(mid[24 - 12 * b : 240 - 12 * b], LANES - 9 * b, axis=1)
                out = cat([out, jnp.where(lane < 9, tail, 0.0)])
            for j in range(blocks):
                cvf[j, s] = out[12:204, 128 * j : 128 * j + 128]
                ff[j, pl.ds(256 * s, 12)] = out[0:12, 128 * j : 128 * j + 128]
                ff[j, pl.ds(256 * s + 128, 12)] = out[204:216, 128 * j : 128 * j + 128]
            lhs = cat([cat([rhf[j, s, pl.ds(12 * a, 384)] for j in range(2)]).astype(bf) for a in range(3)])
            base = 0 if s else 2
            rhs = cat([taps(8 - (base + 3 * a)) for a in range(3)], 1)
            out = dot_nt(lhs, rhs)
            if blocks == 3:
                tail = dot_nt(lhs, cat([we[2 - a] for a in range(3)], 1))
                tail = pltpu.roll(tail, LANES - 18, axis=1) if s else tail
                out = cat([out, jnp.where(lane < 9, tail, 0.0)])
            for j in range(blocks):
                chf[j, s] = out[:, 128 * j : 128 * j + 128]
        for j in range(blocks):
            lanes = slice(128 * j, 128 * j + 128)
            for spot in range(4):
                s, right = spot // 2, spot % 2
                v = ff[j, pl.ds(256 * s + 128 * right, 12)]
                edge = (tx == 3) if right else (tx == 0)
                late = jnp.where(edge, ty == 1, right == 0)
                zero = jnp.zeros((4, LANES), f32)
                ex.rg_c[spot, :, lanes] = jnp.where(late, cat([zero, v], 0), cat([v, zero], 0)).astype(bf)

                @pl.when((ty == s) & edge)
                def _(j=j, s=s, right=right, spot=spot, v=v):
                    take = rule[spot, 0:12] > 0.0
                    cvf[j, s, pl.ds(180 if right else 0, 12)] += jnp.where(take, v, 0.0)
                    chf[j, right, pl.ds(372 if s else 0, 12)] += jnp.where(take, 0.0, v)
        for s in range(2):
            ex.rg_v[s] = join(cvf, (s,), blocks).astype(bf)
            ex.rg_h[s] = join(chf, (s,), blocks).astype(bf)

    def edge_grads(make_v, make_h):
        for s in range(2):
            for h in range(2):
                lanes = slice(128 * h, 128 * h + 128)
                v = make_v(h, s).astype(bf)
                gev[s, :, lanes] = v
                rvf[h, s, pl.ds(0, 24)] = jnp.zeros((24, LANES), f32)
                rvf[h, s, pl.ds(216, 24)] = jnp.zeros((24, LANES), f32)
                rvf[h, s, pl.ds(24, 192)] = v.astype(f32)
                v = make_h(h, s).astype(bf)
                geh[s, :, lanes] = v
                rhf[h, s, pl.ds(12, 384)] = v.astype(f32)

    def slope_two(u, h):
        return gelu_slope(u + biases[1:2, 128 * h : 128 * h + 128].astype(f32))[1]

    edge_grads(
        lambda h, s: slope_two(evf[h, s], h) * cev[s, :, 128 * h : 128 * h + 128].astype(f32),
        lambda h, s: slope_two(ehf[h, s], h) * ceh[s, :, 128 * h : 128 * h + 128].astype(f32),
    )
    ring_grads(third, lambda t: w2[t], 2)
    third.start()

    def out_copy(u, f):
        return pltpu.make_async_copy(ost.at[u], out_ref.at[f], lsem.at[3 + u])

    def third_part(lo, hi):
        @pl.loop(lo, hi)
        def _(i):
            grads = []
            for u in range(2):
                f = 2 * i + u
                act, sl = gelu_slope(join(pre, (face_rows(f),)) + biases[1:2].astype(f32))
                cot = cv[f]
                grad = (cot.astype(f32) * sl).astype(bf)
                accb[2432:2433] += jnp.sum(grad.astype(f32), axis=0, keepdims=True)
                fill(xc[u], grad.reshape(rows, cols, 256))
                field = cat([xv[f].reshape(area, 256), t27[f, 1 : rows + 1].reshape(area, LANES)])
                skip = dot(field, cat([wskip[0:256], wse[...]], 0))
                fresh = dot_tn(field, cot)
                acca[2304:2560] += fresh[0:256]
                accb[2400:2432] += fresh[256:288]

                @pl.when(i > 0)
                def _(u=u, f=f):
                    out_copy(u, f).wait()

                ost[u] = (act + skip).astype(bf)
                out_copy(u, f).start()
                grads.append(grad)
            pair = cat(grads, 0)
            for a in range(3):
                field = cat([hc[2 * i + u, a : a + rows].reshape(area, 768) for u in range(2)], 0)
                acca[768 * a : 768 * a + 768] += dot_tn(field, pair)
            rhs = cat([w2[8 - t] for t in range(TAPS)], 1)
            for u in range(2):
                split(pre, (face_rows(2 * i + u),), dot_nt(cat(windows(xc[u])), rhs))

    third_part(0, 3)
    third.middle()
    third_part(3, 6)
    for u in range(2):
        out_copy(u, 0).wait()

    def ring_kernel_grads(grad_ref, extra, rcv, rch):
        for s in range(2):
            fresh = dot_tn(rcv[s], gev[s])
            grad_ref[1536 * s : 1536 * s + 768] += fresh[0:768]
            if extra:
                grad_ref[2304 + 64 * s : 2336 + 64 * s] += fresh[768:800]
            fresh = dot_tn(rch[s], geh[s])
            for a in range(3):
                t = 3 * a + 2 * s
                grad_ref[256 * t : 256 * t + 256] += fresh[256 * a : 256 * a + 256]
                if extra:
                    grad_ref[2304 + 32 * a : 2336 + 32 * a] += fresh[768 + 128 * a : 800 + 128 * a]

    ring_kernel_grads(acca, False, rc2v, rc2h)
    total_a = Total(0, acca, outa, 0, landa, 0)
    total_b = Total(1, accb, slope, 3584, slope, 0)
    total_a.to_core()
    third.finish()
    third.stage(2)

    @pl.loop(0, faces)
    def _(f):
        for h in range(2):
            for s in range(2):
                pre[h, top(f, s)] += evf[h, s, ring_v(f)]
        for h in range(2):
            for s in range(2):
                pre[h, side(f, s)] += ehf[h, s, ring_h(f)]
        for h in range(2):
            for s in range(2):
                evf[h, s, ring_v(f)] = pre[h, top(f, s)]
                ehf[h, s, ring_h(f)] = pre[h, side(f, s)]

    edge_grads(lambda h, s: evf[h, s] * slev[h, s], lambda h, s: ehf[h, s] * sleh[h, s])
    ring_grads(fourth, w_first, 3)
    fourth.start()
    total_a.to_x()

    def fourth_part(lo, hi):
        @pl.loop(lo, hi)
        def _(i):
            grads = []
            for u in range(2):
                f = 2 * i + u
                grad = (join(pre, (face_rows(f),)) * slope[face_rows(f)].astype(f32)).astype(bf)
                fill(hc.at[f], grad.reshape(rows, cols, 256))
                fill(xc[u], xv[f])
                grads.append(grad)
            pair = cat(grads, 0)
            for a in range(3):
                field = cat([xc[u][a : a + rows].reshape(area, 768) for u in range(2)], 0)
                accb[768 * a : 768 * a + 768] += dot_tn(field, pair)
                extra = cat([t27[2 * i + u, a : a + rows].reshape(area, LANES) for u in range(2)], 0)
                accb[2304 + 32 * a : 2336 + 32 * a] += dot_tn(extra, pair)[0:32]

    fourth_part(0, 3)
    fourth.middle()
    total_a.to_group()
    fourth_part(3, 6)
    for q in range(8):
        @pl.when(place != q)
        def _(q=q):
            pl.semaphore_signal(credit.at[2], inc=1, device_id=dev(q // 4, q % 4), device_id_type=pl.DeviceIdType.MESH)
    for c, mate in ((0, core_mate), (1, x_mate)):
        pl.semaphore_signal(credit.at[c], inc=1, device_id={"dp": mate}, device_id_type=pl.DeviceIdType.MESH)
    ring_kernel_grads(accb, True, rc1v, rc1h)
    total_b.to_core()
    total_a.from_group()
    fourth.finish()
    fourth.stage(3)

    def gx_copy(f):
        return pltpu.make_async_copy(ost.at[f % 2], gx_ref.at[f], lsem.at[3 + f % 2])

    def last_face(f):
        cot = cv[f]
        lhs = cat(windows(hc.at[f]) + [cot])
        rhs = cat([w_first(8 - t) for t in range(TAPS)] + [wskip[0:256]], 1)
        main = dot_nt(lhs, rhs)
        for h in range(2):
            ff[h] = main[:, 128 * h : 128 * h + 128]
        lhs = cat([hc[f, a : a + rows, :, 256:512].reshape(area, 256) for a in range(3)] + [cot])
        packed = dot_nt(lhs, cat([we[2], we[1], we[0], wse[...]], 1))
        col = lax.broadcasted_iota(jnp.int32, (area, 1), 0) % cols
        after = jnp.where(col == cols - 1, 0.0, pltpu.roll(packed, area - 1, axis=0))
        before = jnp.where(col == 0, 0.0, pltpu.roll(packed, 1, axis=0))
        ff[2] = after + pltpu.roll(packed, LANES - 9, axis=1) + pltpu.roll(before, LANES - 18, axis=1)
        for j in range(3):
            for s in range(2):
                ff[j, pl.ds(area - cols if s else 0, cols)] += evf[j, s, ring_v(f)]
        for j in range(3):
            for s in range(2):
                ff[j, pl.ds(cols - 1 if s else 0, rows, stride=cols)] += ehf[j, s, ring_h(f)]
        for c in range(cols):
            here = ff[2, pl.ds(c, rows, stride=cols)].astype(bf)
            rc1h[c // 8, rows16(f * rows, rows), c % 8 * LANES : c % 8 * LANES + LANES] = here

        @pl.when(f > 1)
        def _():
            gx_copy(f).wait()

        ost[f % 2] = cat([ff[0], ff[1]]).astype(bf)
        gx_copy(f).start()

    def last_part(lo, hi):
        @pl.loop(lo, hi)
        def _(f):
            last_face(f)

    last_part(0, 4)
    total_b.to_x()
    total_a.back_x()
    last_part(4, 8)
    total_b.to_group()
    total_a.back_core()
    last_part(8, 12)
    total_b.from_group()
    total_a.finish(suma_ref, 8)
    hot = packing([(0, 0)])
    back = dot_nt(rc1h[0, :, 0 : span // 2], hot[:, 0 : span // 2]) + dot_nt(rc1h[1, :, 0 : span // 2], hot[:, span // 2 :])
    for f in range(faces):
        ev[f] = back[f * rows : f * rows + rows].T.astype(bf).reshape(9, cols, rows)
    eout = pltpu.make_async_copy(ev, gext_ref, lsem.at[1])
    eout.start()
    total_b.back_x()
    for u in range(2):
        gx_copy(u).wait()
    total_b.back_core()
    total_b.finish(sumb_ref, 9)
    eout.wait()
    total_a.store.wait()
    total_b.store.wait()
    for ex in (first, second, third, fourth):
        ex.drain()


def fast_device(
    features, extra_inputs, first_kernel, first_bias, second_kernel, second_bias,
    skip_kernel, skip_bias, seam_table, cotangent,
):
    f32, bf = jnp.float32, jnp.bfloat16
    _, faces, rows, cols, ch = features.shape
    area = rows * cols
    extra = extra_inputs.shape[-1]
    biases = jnp.stack([first_bias, second_bias, skip_bias])
    vm, hbm = pl.BlockSpec(memory_space=pltpu.VMEM), pl.BlockSpec(memory_space=pl.ANY)
    shape = jax.ShapeDtypeStruct

    def exchange_bufs(lanes, windows):
        return [
            pltpu.VMEM((2, 192, lanes), bf), pltpu.VMEM((2, 384, lanes), bf), pltpu.VMEM((384, lanes), bf),
            pltpu.VMEM((384, lanes), bf), pltpu.VMEM((2, 192, lanes), bf), pltpu.VMEM((2, 384, lanes), bf),
            pltpu.VMEM((4, 16, lanes), bf), pltpu.VMEM((8 * windows, 16, lanes), bf),
            pltpu.VMEM((2 * windows, 16, lanes), bf),
        ]

    cat_shape = (rows + 2, cols, 3 * ch)
    sums = (SUM_ROWS, ch)
    scratch = [
        pltpu.VMEM((TAPS, ch + extra, ch), bf), pltpu.VMEM((TAPS, ch, ch), bf), pltpu.VMEM((ch + extra, ch), bf),
        pltpu.VMEM((3, LANES, ch), bf), pltpu.VMEM((LANES, ch), bf), pltpu.VMEM((384, 384), bf),
        pltpu.VMEM((4, 16, LANES), f32),
        pltpu.VMEM((faces, rows, cols, ch), bf), pltpu.VMEM((faces, extra, cols, rows), bf),
        pltpu.VMEM((faces, area, ch), bf), pltpu.VMEM((faces, rows + 2, cols, LANES), bf),
        [pltpu.VMEM(cat_shape, bf)] * 2, pltpu.VMEM((faces,) + cat_shape, bf),
        pltpu.VMEM((2, faces * area, LANES), f32), pltpu.VMEM((faces * area, ch), bf),
        pltpu.VMEM((2, 2, 192, LANES), f32), pltpu.VMEM((2, 2, 384, LANES), f32),
        pltpu.VMEM((2, 192, ch), bf), pltpu.VMEM((2, 384, ch), bf),
        pltpu.VMEM((2, area, ch), bf),
        pltpu.VMEM((3, area, LANES), f32),
        pltpu.VMEM((3, 2, 192, LANES), f32), pltpu.VMEM((3, 2, 384, LANES), f32),
        pltpu.VMEM((3, 2, 240, LANES), f32), pltpu.VMEM((3, 2, 408, LANES), f32),
        pltpu.VMEM((3, 2, 192, LANES), f32), pltpu.VMEM((3, 2, 384, LANES), f32),
        pltpu.VMEM((2, 192, 896), bf), pltpu.VMEM((2, 384, 1152), bf),
        pltpu.VMEM((2, 192, 768), bf), pltpu.VMEM((2, 384, 768), bf),
        pltpu.VMEM((2, 192, ch), bf), pltpu.VMEM((2, 384, ch), bf),
        pltpu.VMEM(sums, f32), pltpu.VMEM(sums, f32), pltpu.VMEM(sums, bf), pltpu.VMEM(sums, bf),
        [exchange_bufs(384, 0 + 1), exchange_bufs(256, 1), exchange_bufs(256, 1), exchange_bufs(384, 1)],
        pltpu.SemaphoreType.DMA((4, 48)), pltpu.SemaphoreType.DMA((4, 33)),
        pltpu.SemaphoreType.DMA((2, 20)), pltpu.SemaphoreType.DMA((2, 20)),
        pltpu.SemaphoreType.REGULAR((3,)), pltpu.SemaphoreType.REGULAR((2, 2)), pltpu.SemaphoreType.DMA((10,)),
    ]
    out = pl.pallas_call(
        whole_block,
        out_shape=(
            shape((faces, area, ch), bf), shape((faces, area, ch), bf), shape((faces, extra, cols, rows), bf),
            shape(sums, bf), shape(sums, bf),
        ),
        in_specs=[hbm] * 5 + [vm] * 2 + [hbm],
        out_specs=[hbm] * 5,
        scratch_shapes=scratch,
        compiler_params=pltpu.CompilerParams(
            collective_id=0, has_side_effects=True, vmem_limit_bytes=65400 * 1024),
    )(
        features[0], extra_inputs[0].transpose(0, 3, 2, 1), first_kernel.reshape(TAPS, ch + extra, ch),
        second_kernel.reshape(TAPS, ch, ch), skip_kernel, biases, seam_table.transpose(1, 2, 0),
        cotangent.reshape(faces, area, ch),
    )
    block_output, grad_features, grad_extra, second_sum, first_sum = out
    tall = TAPS * ch
    tail = first_sum[tall : tall + 96].reshape(3, 32, ch)
    first_grad = jnp.concatenate(
        [first_sum[:tall].reshape(3, 3, ch, ch), tail[:, :PACK].reshape(3, 3, extra, ch)], 2)
    skip = first_sum[tall + 96 : tall + 128]
    return (
        block_output.reshape(features.shape),
        grad_features.reshape(features.shape),
        grad_extra.transpose(0, 3, 2, 1)[None],
        first_grad.astype(f32),
        tail[1, ONE].astype(f32),
        second_sum[:tall].reshape(3, 3, ch, ch).astype(f32),
        first_sum[tall + 128].astype(f32),
        jnp.concatenate([second_sum[tall:], skip[extra : 2 * extra]], 0).astype(f32),
        skip[ONE].astype(f32),
    )


def solution(mesh):
    fits = mesh.shape["ty"] == 2 and mesh.shape["tx"] == 4

    def block(*args):
        tile = args[0].shape
        if fits and tile[1:] == (12, 32, 16, 256) and args[1].shape[-1] == 9:
            return fast_device(*args)
        return per_device(*args)

    return jax.shard_map(
        block,
        mesh=mesh,
        in_specs=(
            P("dp", None, "ty", "tx", None),
            P("dp", None, "ty", "tx", None),
            P(),
            P(),
            P(),
            P(),
            P(),
            P(),
            P(),
            P("dp", None, "ty", "tx", None),
        ),
        out_specs=(
            P("dp", None, "ty", "tx", None),
            P("dp", None, "ty", "tx", None),
            P("dp", None, "ty", "tx", None),
            P(),
            P(),
            P(),
            P(),
            P(),
            P(),
        ),
        check_vma=False,
    )
```

```python
from functools import partial

import jax
import jax.numpy as jnp
import ml_dtypes
import numpy as np
from jax import lax
from jax.experimental import pallas as pl
from jax.experimental.pallas import tpu as pltpu
from jax.sharding import PartitionSpec as P


def extended(value, sides, width):
    for axis, dim in sides:
        size, length = (lax.axis_size(axis), value.shape[dim])
        up = [(i, (i + 1) % size) for i in range(size - 1)]
        down = [(j, i) for i, j in up]
        last = lax.slice_in_dim(value, length - width, length, axis=dim)
        leading = lax.slice_in_dim(value, 0, width, axis=dim)
        before = lax.ppermute(last, axis, up)
        after = lax.ppermute(leading, axis, down)
        value = jnp.concatenate([before, value, after], axis=dim)
    return value


def face_lines(edge_rows, seam_table):
    face_hot = (
        seam_table[:, :, 0][:, :, None]
        == jnp.arange(edge_rows.shape[1], dtype=jnp.int32)[None, None, :]
    ).astype(edge_rows.dtype)
    side_hot = (
        seam_table[:, :, 1][:, :, None] == jnp.arange(4, dtype=jnp.int32)[None, None, :]
    ).astype(edge_rows.dtype)
    chooser = face_hot[:, :, :, None] * side_hot[:, :, None, :]
    side_lines = jnp.einsum(
        "fsgt,bgtnc->bfsnc",
        chooser,
        edge_rows,
        precision=lax.Precision.HIGHEST,
        preferred_element_type=jnp.float32,
    ).astype(edge_rows.dtype)
    flipped = seam_table[:, :, 2][None, :, :, None, None] == 1
    side_lines = jnp.where(flipped, side_lines[:, :, :, ::-1, :], side_lines)
    corner_rule = seam_table[:, :, 3][None, :, :, None] == 0
    upper_line = side_lines[:, :, 0]
    right_line = side_lines[:, :, 1]
    lower_line = side_lines[:, :, 2]
    left_line = side_lines[:, :, 3]
    upper_left = jnp.where(corner_rule[:, :, 0], upper_line[:, :, 0], left_line[:, :, 0])
    upper_right = jnp.where(corner_rule[:, :, 1], upper_line[:, :, -1], right_line[:, :, 0])
    lower_right = jnp.where(corner_rule[:, :, 2], lower_line[:, :, -1], right_line[:, :, -1])
    lower_left = jnp.where(corner_rule[:, :, 3], lower_line[:, :, 0], left_line[:, :, -1])
    upper_full = jnp.concatenate(
        [upper_left[:, :, None], upper_line, upper_right[:, :, None]], axis=2
    )
    right_full = jnp.concatenate(
        [upper_right[:, :, None], right_line, lower_right[:, :, None]], axis=2
    )
    lower_full = jnp.concatenate(
        [lower_left[:, :, None], lower_line, lower_right[:, :, None]], axis=2
    )
    left_full = jnp.concatenate([upper_left[:, :, None], left_line, lower_left[:, :, None]], axis=2)
    return (upper_full, right_full, lower_full, left_full)


def seam_layer(edge_rows, seam_table, place):
    row_index, column_index, row_count, column_count, tile_rows, tile_columns = place
    upper_full, right_full, lower_full, left_full = face_lines(edge_rows, seam_table)
    upper_piece = lax.dynamic_slice_in_dim(
        upper_full, column_index * tile_columns, tile_columns + 2, 2
    )
    lower_piece = lax.dynamic_slice_in_dim(
        lower_full, column_index * tile_columns, tile_columns + 2, 2
    )
    left_piece = lax.dynamic_slice_in_dim(left_full, row_index * tile_rows, tile_rows + 2, 2)
    right_piece = lax.dynamic_slice_in_dim(right_full, row_index * tile_rows, tile_rows + 2, 2)
    grid_rows = lax.broadcasted_iota(jnp.int32, (tile_rows + 2, tile_columns + 2, 1), 0)
    grid_columns = lax.broadcasted_iota(jnp.int32, (tile_rows + 2, tile_columns + 2, 1), 1)
    seam_cells = jnp.zeros(
        upper_piece.shape[:2] + (tile_rows + 2, tile_columns + 2, upper_piece.shape[-1]),
        edge_rows.dtype,
    )
    seam_cells = jnp.where((grid_rows == 0) & (row_index == 0), upper_piece[:, :, None], seam_cells)
    seam_cells = jnp.where(
        (grid_rows == tile_rows + 1) & (row_index == row_count - 1),
        lower_piece[:, :, None],
        seam_cells,
    )
    seam_cells = jnp.where(
        (grid_columns == 0) & (column_index == 0), left_piece[:, :, :, None], seam_cells
    )
    seam_cells = jnp.where(
        (grid_columns == tile_columns + 1) & (column_index == column_count - 1),
        right_piece[:, :, :, None],
        seam_cells,
    )
    return seam_cells


def join_tiles(tile_parts):
    moved = jnp.moveaxis(tile_parts, 0, 2)
    return moved.reshape(
        tile_parts.shape[1],
        tile_parts.shape[2],
        tile_parts.shape[0] * tile_parts.shape[3],
        tile_parts.shape[4],
    )


def face_edges(field):
    row_count = lax.axis_size("ty")
    column_count = lax.axis_size("tx")
    row_edges = jnp.stack([field[:, :, 0], field[:, :, -1]], axis=2)
    column_edges = jnp.stack([field[:, :, :, -1], field[:, :, :, 0]], axis=2)
    row_gathered, column_gathered = (
        lax.all_gather(row_edges[None], ("ty", "tx"), axis=0, tiled=True),
        lax.all_gather(column_edges[None], ("ty", "tx"), axis=0, tiled=True),
    )
    row_grid = row_gathered.reshape((row_count, column_count) + row_edges.shape)
    column_grid = column_gathered.reshape((row_count, column_count) + column_edges.shape)
    upper_edge = join_tiles(row_grid[0, :, :, :, 0])
    lower_edge = join_tiles(row_grid[row_count - 1, :, :, :, 1])
    right_edge = join_tiles(column_grid[:, column_count - 1, :, :, 0])
    left_edge = join_tiles(column_grid[:, 0, :, :, 1])
    return jnp.stack([upper_edge, right_edge, lower_edge, left_edge], axis=2)


def extend(field, seam_table, place):
    rimmed = extended(field, (("ty", 2), ("tx", 3)), 1)
    return rimmed + seam_layer(face_edges(field), seam_table, place)


def collect(grad_padded, seam_table, place):
    row_index, column_index, row_count, column_count, tile_rows, tile_columns = place
    widened = extended(grad_padded.astype(jnp.bfloat16), (("ty", 2), ("tx", 3)), 1).astype(
        grad_padded.dtype
    )
    inside = grad_padded[:, :, 1:-1, 1:-1]
    inside = inside.at[:, :, 0].add(widened[:, :, 0, 2 : tile_columns + 2])
    inside = inside.at[:, :, -1].add(widened[:, :, tile_rows + 3, 2 : tile_columns + 2])
    inside = inside.at[:, :, :, 0].add(widened[:, :, 2 : tile_rows + 2, 0])
    inside = inside.at[:, :, :, -1].add(widened[:, :, 2 : tile_rows + 2, tile_columns + 3])
    inside = inside.at[:, :, 0, 0].add(widened[:, :, 0, 0])
    inside = inside.at[:, :, 0, -1].add(widened[:, :, 0, tile_columns + 3])
    inside = inside.at[:, :, -1, 0].add(widened[:, :, tile_rows + 3, 0])
    inside = inside.at[:, :, -1, -1].add(widened[:, :, tile_rows + 3, tile_columns + 3])
    blank = jnp.zeros(
        grad_padded.shape[:2] + (4, tile_rows * row_count, grad_padded.shape[-1]), jnp.float32
    )
    unused, seam_pull = jax.vjp(
        lambda edge_values: seam_layer(edge_values, seam_table, place), blank
    )
    (edge_grads,) = seam_pull(grad_padded)
    edge_grads = lax.psum(edge_grads, ("ty", "tx"))
    upper_part = lax.dynamic_slice_in_dim(
        edge_grads[:, :, 0], column_index * tile_columns, tile_columns, 2
    )
    right_part = lax.dynamic_slice_in_dim(edge_grads[:, :, 1], row_index * tile_rows, tile_rows, 2)
    lower_part = lax.dynamic_slice_in_dim(
        edge_grads[:, :, 2], column_index * tile_columns, tile_columns, 2
    )
    left_part = lax.dynamic_slice_in_dim(edge_grads[:, :, 3], row_index * tile_rows, tile_rows, 2)
    inside = inside.at[:, :, 0].add(jnp.where(row_index == 0, upper_part, 0.0))
    inside = inside.at[:, :, -1].add(jnp.where(row_index == row_count - 1, lower_part, 0.0))
    inside = inside.at[:, :, :, 0].add(jnp.where(column_index == 0, left_part, 0.0))
    inside = inside.at[:, :, :, -1].add(
        jnp.where(column_index == column_count - 1, right_part, 0.0)
    )
    return inside


def conv_valid(padded, kernel):
    shape_in = padded.shape
    merged = padded.reshape(shape_in[0] * shape_in[1], shape_in[2], shape_in[3], shape_in[4])
    result = lax.conv_general_dilated(
        merged,
        kernel,
        (1, 1),
        "VALID",
        dimension_numbers=("NHWC", "HWIO", "NHWC"),
        preferred_element_type=jnp.float32,
    )
    return result.reshape(
        shape_in[0], shape_in[1], shape_in[2] - 2, shape_in[3] - 2, kernel.shape[-1]
    )


def conv_back(grad_pre, kernel):
    flipped = jnp.transpose(kernel[::-1, ::-1], (0, 1, 3, 2))
    surround = jnp.pad(grad_pre, ((0, 0), (0, 0), (2, 2), (2, 2), (0, 0)))
    return conv_valid(surround, flipped)


def kernel_grad(padded, grad_pre):
    tile_rows = grad_pre.shape[2]
    tile_columns = grad_pre.shape[3]
    pieces = []
    for offset_row in range(3):
        for offset_column in range(3):
            window = padded[
                :,
                :,
                offset_row : offset_row + tile_rows,
                offset_column : offset_column + tile_columns,
            ]
            pieces.append(
                jnp.einsum("sfhwc,sfhwd->cd", window, grad_pre, preferred_element_type=jnp.float32)
            )
    return jnp.stack(pieces).reshape(3, 3, padded.shape[-1], grad_pre.shape[-1])


def per_device(
    features,
    extra_inputs,
    first_kernel,
    first_bias,
    second_kernel,
    second_bias,
    skip_kernel,
    skip_bias,
    seam_table,
    cotangent,
):
    place = (
        lax.axis_index("ty"),
        lax.axis_index("tx"),
        lax.axis_size("ty"),
        lax.axis_size("tx"),
        features.shape[2],
        features.shape[3],
    )
    gelu_exact = partial(jax.nn.gelu, approximate=False)
    joined = jnp.concatenate([features, extra_inputs], axis=-1)
    padded_one = extend(joined, seam_table, place)
    pre_one = conv_valid(padded_one, first_kernel) + first_bias
    active_one, slope_one = jax.vjp(gelu_exact, pre_one)
    hidden = active_one.astype(jnp.bfloat16)
    padded_two = extend(hidden, seam_table, place)
    pre_two = conv_valid(padded_two, second_kernel) + second_bias
    active_two, slope_two = jax.vjp(gelu_exact, pre_two)
    skipped = (
        jnp.einsum("sfhwc,cd->sfhwd", joined, skip_kernel, preferred_element_type=jnp.float32)
        + skip_bias
    )
    block_output = (active_two + skipped).astype(jnp.bfloat16)
    (grad_two,) = slope_two(cotangent.astype(jnp.float32))
    grad_two = grad_two.astype(jnp.bfloat16)
    second_kernel_grad = kernel_grad(padded_two, grad_two)
    second_bias_grad = jnp.sum(grad_two, axis=(0, 1, 2, 3), dtype=jnp.float32)
    grad_hidden = collect(conv_back(grad_two, second_kernel), seam_table, place)
    (grad_one,) = slope_one(grad_hidden)
    grad_one = grad_one.astype(jnp.bfloat16)
    first_kernel_grad = kernel_grad(padded_one, grad_one)
    first_bias_grad = jnp.sum(grad_one, axis=(0, 1, 2, 3), dtype=jnp.float32)
    grad_joined = collect(conv_back(grad_one, first_kernel), seam_table, place)
    grad_joined = grad_joined + jnp.einsum(
        "sfhwd,cd->sfhwc", cotangent, skip_kernel, preferred_element_type=jnp.float32
    )
    skip_kernel_grad = jnp.einsum(
        "sfhwc,sfhwd->cd", joined, cotangent, preferred_element_type=jnp.float32
    )
    skip_bias_grad = jnp.sum(cotangent, axis=(0, 1, 2, 3), dtype=jnp.float32)
    summed = lax.psum(
        (
            first_kernel_grad,
            first_bias_grad,
            second_kernel_grad,
            second_bias_grad,
            skip_kernel_grad,
            skip_bias_grad,
        ),
        ("dp", "ty", "tx"),
    )
    grad_joined = grad_joined.astype(jnp.bfloat16)
    channels = features.shape[-1]
    return (
        block_output,
        grad_joined[..., :channels],
        grad_joined[..., channels:],
        summed[0],
        summed[1],
        summed[2],
        summed[3],
        summed[4],
        summed[5],
    )


TAPS = 9
SUM_ROWS = 2560
LANES = 128
PACK = 27
ONE = 27
FOUR = ("core", "x", "y", "z")
THREE = ("core", "x", "yz")
SUMS = (("a", 0, 2560, FOUR), ("b", 0, 1024, THREE), ("c", 1024, 512, THREE), ("d", 1536, 512, THREE), ("e", 2048, 512, THREE))
BLOCKS = (0, 1024, 1792)
SUM_PLAN = {
    ("middle", 0): (("a", 0),),
    ("back", 2): (("a", 1),),
    ("sent", 0): (("a", 2),),
    ("first", 0): (("b", 0), ("a", 3)),
    ("more", 4): (("c", 0), ("b", 1)),
    ("more", 6): (("a", 4),),
    ("third", 0): (("d", 0), ("e", 0), ("c", 1)),
    ("last", 1): (("d", 1), ("e", 1), ("b", 2), ("a", 5)),
    ("last", 2): (("c", 2),),
    ("last", 3): (("d", 2), ("e", 2), ("b", 3), ("a", 6)),
    ("last", 4): (("c", 3),),
    ("last", 5): (("d", 3), ("e", 3), ("b", 4)),
    ("end", 0): (("c", 4), ("a", 7), ("d", 4), ("e", 4), ("b", 5)),
    ("rest", 0): (("c", 5), ("d", 5), ("e", 5), ("a", 8), ("b", 6), ("c", 6), ("d", 6), ("e", 6)),
}


def whole_block(
    x_in, ext_in, w1_in, w2_in, skip_in, bias_one, bias_two, bias_skip, table, cot_in, hot_in, hot_back_in,
    out_ref, gx_ref, gext_ref, suma_ref, sumb_ref, tails, rests,
    w1, w2, wskip, we, wse, we81, sel_t, rule,
    xv, ev, cv, t27, xc, hc, pre, slope, slev, sleh, cev, ceh,
    ost, ff, evf, ehf, rvf, rhf, cvf, chf, rc1v, rc1h, rc2v, rc2h, gev, geh,
    acca, accb, outa, landa, bufs, ssem, rsem, sum_ssem, sum_rsem, credit, ack, lsem,
):
    f32, bf = jnp.float32, jnp.bfloat16
    dp, ty, tx = lax.axis_index("dp"), lax.axis_index("ty"), lax.axis_index("tx")
    core, xx, place = dp % 2, dp // 2, ty * 4 + tx
    core_mate, x_mate = dp + 1 - 2 * core, dp + 2 - 4 * xx
    faces, rows, cols = x_in.shape[0], x_in.shape[1], x_in.shape[2]
    area = rows * cols
    is_mid = jnp.where((tx == 0) | (tx == 3), 0, 1)
    hx = jnp.where(tx >= 2, 1, 0)
    kk = ty + 2 * hx
    mm = kk + 4 * is_mid
    at_end = is_mid == 0

    def dev(y, x):
        return {"ty": y, "tx": x}

    def rows16(start, size):
        return pl.ds(pl.multiple_of(start, 16), size)

    def home(m):
        half = (m // 2) % 2
        return m % 2, (3 * half if m // 4 == 0 else 1 + half)

    def home_class(k):
        half = k // 2
        return k % 2, jnp.where(at_end, 3 * half, 1 + half)

    def flip48(flag, k, n):
        return 48 * jnp.where(flag, n - 1 - k, k)

    def maybe(cond, call):
        if cond is None:
            call()
        else:
            pl.when(cond)(call)

    class Exchange:
        def __init__(self, index):
            self.index = index
            self.ed_v, self.ed_h, self.db, self.sb, self.rg_v, self.rg_h, self.rg_c, self.xw, self.xd = bufs[index]

        def copies(self, sends, first_slot):
            for n, (cond, src, dst, rs, target) in enumerate(sends):
                yield cond, pltpu.make_async_remote_copy(
                    src_ref=src, dst_ref=dst, send_sem=ssem.at[self.index, first_slot + n],
                    recv_sem=rsem.at[self.index, rs], device_id=target, device_id_type=pl.DeviceIdType.MESH,
                )

        def start(self):
            for cond, copy in self.copies(self.first_sends(), 0):
                maybe(cond, copy.start)
            self.first_moves()

        def middle(self):
            self.relay()
            for cond, copy in self.copies(self.second_sends(), 24):
                maybe(cond, copy.start)
            self.second_moves()

        def drain(self):
            for cond, copy in self.copies(self.first_sends(), 0):
                maybe(cond, copy.wait_send)
            for cond, copy in self.copies(self.second_sends(), 24):
                maybe(cond, copy.wait_send)

        def get(self, cond, dst, rs):
            copy = pltpu.make_async_remote_copy(
                src_ref=dst, dst_ref=dst, send_sem=ssem.at[self.index, 0],
                recv_sem=rsem.at[self.index, rs], device_id=dev(1 - ty, tx), device_id_type=pl.DeviceIdType.MESH,
            )
            maybe(cond, copy.wait_recv)

        def move(self, cond, dst, dst_at, src, src_at):
            @pl.when(cond)
            def _():
                dst[dst_at] = src[src_at]

    class Forward(Exchange):
        def row_pieces(self):
            to = rows16((2 * ty) * 96 + hx * 48, 48)
            for k in range(4):
                yield k, rows16(flip48(hx == 1, k, 4), 48), to

        def column_pieces(self):
            to = rows16(jnp.where(hx == 1, 1, 3) * 96 + ty * 48, 48)
            for m in range(8):
                yield m, rows16(flip48(ty == 1, m, 8), 48), to

        def first_sends(self):
            ed_v, ed_h, db, rg_v, rg_h, rg_c = self.ed_v, self.ed_h, self.db, self.rg_v, self.rg_h, self.rg_c
            for k, at, to in self.row_pieces():
                yield kk != k, ed_v.at[ty, at], db.at[to], (2 * ty) * 2 + hx, dev(*home_class(k))
            for m, at, to in self.column_pieces():
                yield at_end & (mm != m), ed_h.at[hx, at], db.at[to], jnp.where(hx == 1, 2, 6) + ty, dev(*home(m))
            yield None, ed_v.at[1 - ty], rg_v.at[ty], 24, dev(1 - ty, tx)
            yield tx < 3, ed_h.at[1], rg_h.at[0], 25, dev(ty, tx + 1)
            yield tx > 0, ed_h.at[0], rg_h.at[1], 26, dev(ty, tx - 1)
            yield tx < 3, ed_v.at[1 - ty, pl.ds(176, 16)], rg_c.at[2 * ty], 20 + 2 * ty, dev(1 - ty, tx + 1)
            yield tx > 0, ed_v.at[1 - ty, pl.ds(0, 16)], rg_c.at[2 * ty + 1], 21 + 2 * ty, dev(1 - ty, tx - 1)

        def first_moves(self):
            for k, at, to in self.row_pieces():
                self.move(kk == k, self.db, (to,), self.ed_v, (ty, at))
            for m, at, to in self.column_pieces():
                self.move(at_end & (mm == m), self.db, (to,), self.ed_h, (hx, at))

        def relay(self):
            db, sb = self.db, self.sb
            for t in range(4):
                for h in range(2):
                    if t % 2 == 0:
                        own = (ty == t // 2) & (hx == h)
                    else:
                        own = at_end & (ty == h) & (tx == (0 if t == 3 else 3))
                    self.get(jnp.logical_not(own), db.at[pl.ds(t * 96 + h * 48, 48)], t * 2 + h)
            sb[...] = dot_tn(sel_t[...], db[...]).astype(bf)

        def out_rows(self):
            for y in range(2):
                for h in range(2):
                    x = jnp.where(at_end, 3 * h, 1 + h)
                    own = (ty == y) & (tx == x)
                    yield own, y, x, pl.ds(2 * y * 96 + h * 48, 48), rows16(48 * ((3 - kk) if h else kk), 48)

        def out_columns(self):
            for y in range(2):
                for h in range(2):
                    own = (ty == y) & (tx == 3 * h)
                    at = pl.ds((1 if h else 3) * 96 + y * 48, 48)
                    yield own, y, h, at, rows16(48 * ((7 - mm) if y else mm), 48)

        def out_corners(self):
            for y in range(2):
                for m, x, right, at in ((3, 1, 0, 32), (3, 2, 1, 48), (4, 3, 0, 80), (4, 0, 1, 0), (7, 2, 0, 32), (7, 1, 1, 48)):
                    yield m, y, x, 2 * y + right, pl.ds(2 * y * 96 + at, 16)
                for h in range(2):
                    yield 7, y, 3 * h, 2 * (1 - y) + h, pl.ds((1 if h else 3) * 96 + (32 if y else 48), 16)

        def second_sends(self):
            sb = self.sb
            for own, y, x, at, to in self.out_rows():
                yield jnp.logical_not(own), sb.at[at], self.rg_v.at[y, to], 8 + kk, dev(y, x)
            for own, y, h, at, to in self.out_columns():
                yield jnp.logical_not(own), sb.at[at], self.rg_h.at[h, to], 12 + mm, dev(y, 3 * h)
            for m, y, x, spot, at in self.out_corners():
                if home(m) != (y, x):
                    yield mm == m, sb.at[at], self.rg_c.at[spot], 20 + spot, dev(y, x)

        def second_moves(self):
            for own, y, x, at, to in self.out_rows():
                self.move(own, self.rg_v, (y, to), self.sb, (at,))
            for own, y, h, at, to in self.out_columns():
                self.move(own, self.rg_h, (h, to), self.sb, (at,))
            for m, y, x, spot, at in self.out_corners():
                if home(m) == (y, x):
                    self.move(mm == m, self.rg_c, (spot,), self.sb, (at,))

        def finish(self):
            self.get(None, self.rg_v.at[1 - ty], 24)
            self.get(tx > 0, self.rg_h.at[0], 25)
            self.get(tx < 3, self.rg_h.at[1], 26)
            for k in range(4):
                self.get(kk != k, self.rg_v.at[ty, rows16(flip48(hx == 1, k, 4), 48)], 8 + k)
            for m in range(8):
                self.get(at_end & (mm != m), self.rg_h.at[hx, rows16(flip48(ty == 1, m, 8), 48)], 12 + m)
            for spot in range(4):
                y, right = spot // 2, spot % 2
                face_corner = (ty == y) & (tx == 3 * right)
                if spot == 2:
                    own = (ty == 1) & (tx == 2)
                    skip = face_corner | own
                else:
                    skip = face_corner
                self.get(jnp.logical_not(skip), self.rg_c.at[spot], 20 + spot)

    class Backward(Exchange):
        row_pieces, column_pieces = Forward.row_pieces, Forward.column_pieces
        out_rows, out_columns = Forward.out_rows, Forward.out_columns

        def corners(self):
            for right in range(2):
                away = (tx < 3) if right else (tx > 0)
                if right:
                    x, y = jnp.where(tx == 0, 1, jnp.where(tx == 1, 2, 3)), jnp.where(tx == 0, 0, 1)
                else:
                    x, y = jnp.where(tx == 1, 3, jnp.where(tx == 2, 2, 1)), jnp.where(tx == 3, 0, 1)
                own = away & (ty == y) & (tx == x)
                yield right, away, own, x, y, 2 * ty + right

        def first_sends(self):
            rg_v, rg_h, rg_c, sb, xw, xd = self.rg_v, self.rg_h, self.rg_c, self.sb, self.xw, self.xd
            for k, at, to in self.row_pieces():
                yield kk != k, rg_v.at[ty, at], sb.at[to], (2 * ty) * 2 + hx, dev(*home_class(k))
            for m, at, to in self.column_pieces():
                yield at_end & (mm != m), rg_h.at[hx, at], sb.at[to], jnp.where(hx == 1, 2, 6) + ty, dev(*home(m))
            for right, away, own, x, y, slot in self.corners():
                yield away & jnp.logical_not(own), rg_c.at[slot], xw.at[slot], 8 + slot, dev(y, x)
                inner = 2 * (1 - ty) + right
                edge = (tx == 3) if right else (tx == 0)
                yield edge, rg_c.at[inner], xw.at[4 + slot], 12 + slot, dev(1, 2)
                yield away, rg_c.at[inner], xd.at[1 - right], 17 - right, dev(1 - ty, tx + (1 if right else -1))
            ed_v, ed_h = self.ed_v, self.ed_h
            yield None, rg_v.at[1 - ty], ed_v.at[ty], 30, dev(1 - ty, tx)
            yield tx < 3, rg_h.at[1], ed_h.at[0], 31, dev(ty, tx + 1)
            yield tx > 0, rg_h.at[0], ed_h.at[1], 32, dev(ty, tx - 1)

        def first_moves(self):
            for k, at, to in self.row_pieces():
                self.move(kk == k, self.sb, (to,), self.rg_v, (ty, at))
            for m, at, to in self.column_pieces():
                self.move(at_end & (mm == m), self.sb, (to,), self.rg_h, (hx, at))
            for right, away, own, x, y, slot in self.corners():
                self.move(own, self.xw, (slot,), self.rg_c, (slot,))

        def relay(self):
            sb, db, xw = self.sb, self.db, self.xw
            for s in range(4):
                for h in range(2):
                    if s % 2 == 0:
                        own = (ty == s // 2) & (hx == h)
                    else:
                        own = at_end & (ty == h) & (tx == (0 if s == 3 else 3))
                    self.get(jnp.logical_not(own), sb.at[pl.ds(s * 96 + h * 48, 48)], s * 2 + h)
            for y in range(2):
                for right in range(2):
                    slot = 2 * y + right
                    wants = (mm == 3) | (mm == 4) | (mm == 7)
                    if slot == 2:
                        wants = (mm == 3) | (mm == 4)
                    self.get(wants, xw.at[slot], 8 + slot)
                    self.get(mm == 7, xw.at[4 + slot], 12 + slot)
                    for m, at in ((3, 48 if right else 32), (4, 0 if right else 80), (7, 48 if right else 32)):
                        @pl.when(mm == m)
                        def _(spot=2 * y * 96 + at, slot=slot):
                            here = pl.ds(spot, 16)
                            sb[here] = (sb[here].astype(f32) + xw[slot].astype(f32)).astype(bf)

                    @pl.when(mm == 7)
                    def _(spot=(1 if right else 3) * 96 + (32 if y else 48), slot=4 + slot):
                        here = pl.ds(spot, 16)
                        sb[here] = (sb[here].astype(f32) + xw[slot].astype(f32)).astype(bf)
            db[...] = dot(sel_t[...], sb[...]).astype(bf)

        def second_sends(self):
            for own, y, x, at, to in self.out_rows():
                yield jnp.logical_not(own), self.db.at[at], self.ed_v.at[y, to], 18 + kk, dev(y, x)
            for own, y, h, at, to in self.out_columns():
                yield jnp.logical_not(own), self.db.at[at], self.ed_h.at[h, to], 22 + mm, dev(y, 3 * h)

        def second_moves(self):
            for own, y, x, at, to in self.out_rows():
                self.move(own, self.ed_v, (y, to), self.db, (at,))
            for own, y, h, at, to in self.out_columns():
                self.move(own, self.ed_h, (h, to), self.db, (at,))

        def finish(self):
            self.get(None, self.ed_v.at[1 - ty], 30)
            self.get(tx > 0, self.ed_h.at[0], 31)
            self.get(tx < 3, self.ed_h.at[1], 32)
            self.get(tx > 0, self.xd.at[0], 16)
            self.get(tx < 3, self.xd.at[1], 17)
            for k in range(4):
                self.get(kk != k, self.ed_v.at[ty, rows16(flip48(hx == 1, k, 4), 48)], 18 + k)
            for m in range(8):
                self.get(at_end & (mm != m), self.ed_h.at[hx, rows16(flip48(ty == 1, m, 8), 48)], 22 + m)

        def stage(self, blocks):
            for j in range(blocks):
                lanes = slice(128 * j, 128 * j + 128)
                for s in range(2):
                    evf[j, s] = self.ed_v[s, :, lanes].astype(f32)
                    ehf[j, s] = self.ed_h[s, :, lanes].astype(f32)

                @pl.when(tx > 0)
                def _(j=j, lanes=lanes):
                    evf[j, 1 - ty, pl.ds(0, 16)] += self.xd[0, :, lanes].astype(f32)

                @pl.when(tx < 3)
                def _(j=j, lanes=lanes):
                    evf[j, 1 - ty, pl.ds(176, 16)] += self.xd[1, :, lanes].astype(f32)

    class Total:
        def __init__(self, index, acc, acc0, out, out0, land, land0, count, order):
            self.index, self.acc, self.out, self.land = index, acc, out, land
            self.acc0, self.out0, self.land0, self.count = acc0, out0, land0, count
            axes = {
                "core": (2, core, lambda k: {"dp": core_mate}),
                "x": (2, xx, lambda k: {"dp": x_mate}),
                "y": (2, ty, lambda k: {"ty": 1 - ty}),
                "z": (4, tx, lambda k: {"tx": k}),
                "yz": (8, place, lambda k: {"ty": k // 4, "tx": k % 4}),
            }
            self.stages = []
            start, size, land_at, sem = 0, count, 0, 0
            for name in order:
                n, me, target = axes[name]
                chunk = size // n
                self.stages.append((n, me, target, start, chunk, land_at, sem))
                land_at += chunk * (1 if n == 2 else n)
                sem += 1 if n == 2 else n
                start, size = start + me * chunk, chunk
            self.unit, self.sems, self.last = size, sem, len(order) - 1
            self.near = []
            for n, me, *_ in self.stages:
                if n == 2:
                    self.near.append([(1 - me, None, 0, 0)])
                else:
                    self.near.append([(k, me != k, k, me) for k in range(n)])

        def at(self, base, start, size):
            return rows16(base + start, size)

        def copy(self, src, dst, slot, rslot, target):
            return pltpu.make_async_remote_copy(
                src_ref=src, dst_ref=dst, send_sem=sum_ssem.at[self.index, slot],
                recv_sem=sum_rsem.at[self.index, rslot], device_id=target, device_id_type=pl.DeviceIdType.MESH,
            )

        def rs_copy(self, s, k, mine, theirs):
            n, me, target, start, chunk, land_at, sem = self.stages[s]
            return self.copy(
                self.out.at[self.at(self.out0, start + k * chunk, chunk)],
                self.land.at[self.at(self.land0, land_at + chunk * theirs, chunk)],
                sem + mine, sem + theirs, target(k))

        def send_rs(self, s):
            n, me, target, start, chunk, land_at, sem = self.stages[s]
            for k, cond, mine, theirs in self.near[s]:
                def go(k=k, mine=mine, theirs=theirs):
                    self.cast(start + k * chunk, chunk)
                    self.rs_copy(s, k, mine, theirs).start()
                maybe(cond, go)

        def recv_rs(self, s):
            n, me, target, start, chunk, land_at, sem = self.stages[s]
            for k, cond, mine, theirs in self.near[s]:
                def get(k=k, mine=mine):
                    here = self.land.at[self.at(self.land0, land_at + chunk * mine, chunk)]
                    self.copy(here, here, sem + mine, sem + mine, target(k)).wait_recv()

                    @pl.loop(0, chunk // self.unit)
                    def _(i):
                        self.acc[self.at(self.acc0, start + me * chunk + i * self.unit, self.unit)] += self.land[
                            self.at(self.land0, land_at + chunk * mine + i * self.unit, self.unit)].astype(f32)

                maybe(cond, get)

        def done_rs(self, s):
            target = self.stages[s][2]
            for k, cond, mine, theirs in self.near[s]:
                def done(k=k, mine=mine, theirs=theirs):
                    self.rs_copy(s, k, mine, theirs).wait_send()
                    pl.semaphore_signal(
                        ack.at[self.index, s], inc=1, device_id=target(k), device_id_type=pl.DeviceIdType.MESH)
                maybe(cond, done)

        def ag_copy(self, s, k, mine, theirs):
            n, me, target, start, chunk, land_at, sem = self.stages[s]
            here = self.out.at[self.at(self.out0, start + me * chunk, chunk)]
            return self.copy(here, here, self.sems + sem + mine, self.sems + sem + theirs, target(k))

        def send_ag(self, s):
            pl.semaphore_wait(ack.at[self.index, s], self.stages[s][0] - 1)
            for k, cond, mine, theirs in self.near[s]:
                maybe(cond, lambda k=k, mine=mine, theirs=theirs: self.ag_copy(s, k, mine, theirs).start())

        def recv_ag(self, s):
            n, me, target, start, chunk, land_at, sem = self.stages[s]
            for k, cond, mine, theirs in self.near[s]:
                def get(k=k, mine=mine):
                    here = self.out.at[self.at(self.out0, start + k * chunk, chunk)]
                    slot = self.sems + sem + mine
                    self.copy(here, here, slot, slot, target(k)).wait_recv()
                maybe(cond, get)

        def cast(self, start, size):
            @pl.loop(0, size // self.unit)
            def _(i):
                at = start + i * self.unit
                self.out[self.at(self.out0, at, self.unit)] = self.acc[self.at(self.acc0, at, self.unit)].astype(bf)

        def step(self, k):
            last = self.last
            if k == 0:
                self.send_rs(0)
            elif k <= last:
                self.recv_rs(k - 1)
                self.send_rs(k)
                self.done_rs(k - 1)
            elif k == last + 1:
                self.recv_rs(last)
                n, me, target, start, chunk, land_at, sem = self.stages[last]
                self.cast(start + me * chunk, chunk)
                self.done_rs(last)
                self.send_ag(last)
            elif k <= 2 * last + 1:
                self.recv_ag(2 * last + 2 - k)
                self.send_ag(2 * last + 1 - k)
            else:
                self.recv_ag(0)
                for s in range(last + 1):
                    for k, cond, mine, theirs in self.near[s]:
                        maybe(cond, lambda s=s, k=k, mine=mine, theirs=theirs: self.ag_copy(s, k, mine, theirs).wait_send())

    def sums(where, at=None):
        for (spot, spot_at), steps in SUM_PLAN.items():
            if spot == where:
                def go(steps=steps):
                    for name, k in steps:
                        totals[name].step(k)
                        if name == "a" and k == 2 * totals[name].last + 2:
                            pltpu.make_async_copy(outa, suma_ref, lsem.at[8]).start()
                if at is None:
                    go()
                else:
                    pl.when(at == spot_at)(go)

    def dot(a, b):
        return jnp.dot(a, b, preferred_element_type=f32)

    def dot_nt(a, b):
        return lax.dot_general(a, b, (((1,), (1,)), ((), ())), preferred_element_type=f32)

    def dot_tn(a, b):
        return lax.dot_general(a, b, (((0,), (0,)), ((), ())), preferred_element_type=f32)

    def cat(parts, axis=-1):
        return jnp.concatenate(parts, axis=axis)

    def face_rows(f):
        return pl.ds(pl.multiple_of(f * area, area), area)

    def top(f, s):
        return pl.ds(f * area + (area - cols if s else 0), cols)

    def side(f, s):
        return pl.ds(f * area + (cols - 1 if s else 0), rows, stride=cols)

    def ring_v(f):
        return pl.ds(f, cols, stride=faces)

    def ring_h(f):
        return pl.ds(f, rows, stride=faces)

    def shifts(v):
        zero = jnp.zeros((rows, 1, v.shape[-1]), v.dtype)
        return cat([zero, v[:, : cols - 1]], 1), cat([v[:, 1:], zero], 1)

    def fill(ref, v):
        left, right = shifts(v)
        wide = v.shape[-1]
        ref[1 : rows + 1, :, 0:wide] = left
        ref[1 : rows + 1, :, wide : 2 * wide] = v
        ref[1 : rows + 1, :, 2 * wide : 3 * wide] = right

    def windows(ref):
        return [ref[a : a + rows].reshape(area, ref.shape[-1]) for a in range(3)]

    def split(ref, at, v):
        for h in range(2):
            ref[(h,) + at] = v[:, 128 * h : 128 * h + 128]

    def join(ref, at, blocks=2):
        return cat([ref[(h,) + at] for h in range(blocks)])

    def gelu_slope(u):
        phi = 0.5 + 0.5 * lax.erf(u * 0.7071067811865476)
        return u * phi, phi + u * (0.3989422804014327 * jnp.exp(-0.5 * u * u))

    lane = lax.broadcasted_iota(jnp.int32, (1, LANES), 1)

    first, second = Forward(0), Forward(1)
    third, fourth = Backward(2), Backward(3)
    def load(src, dst, sem):
        copy = pltpu.make_async_copy(src, dst, lsem.at[sem])
        copy.start()
        return copy

    eload, hotload, xload = load(ext_in, ev, 1), load(hot_in, slope.at[0:1152], 11), load(x_in, xv, 0)
    w1load, skipload = load(w1_in, w1, 5), load(skip_in, wskip, 6)
    cload, w2load = load(cot_in, cv, 2), load(w2_in, w2, 7)
    barrier = pltpu.get_barrier_semaphore()
    for e in (0, 1):
        bufs[e][6][...] = jnp.zeros_like(bufs[e][6])
    for y in range(2):
        for x in range(4):
            @pl.when((ty != y) | (tx != x))
            def _(y=y, x=x):
                pl.semaphore_signal(barrier, inc=1, device_id=dev(y, x), device_id_type=pl.DeviceIdType.MESH)
    for mate in (core_mate, x_mate):
        pl.semaphore_signal(barrier, inc=1, device_id={"dp": mate}, device_id_type=pl.DeviceIdType.MESH)
    pl.semaphore_wait(barrier, 9)

    for ref in (xc[0], xc[1]):
        ref[0] = jnp.zeros(ref.shape[1:], bf)
        ref[rows + 1] = jnp.zeros(ref.shape[1:], bf)

    @pl.loop(0, faces)
    def _(f):
        hc[f, 0] = jnp.zeros(hc.shape[2:], bf)
        hc[f, rows + 1] = jnp.zeros(hc.shape[2:], bf)
        t27[f, 0] = jnp.zeros(t27.shape[2:], bf)
        t27[f, rows + 1] = jnp.zeros(t27.shape[2:], bf)

    eload.wait()
    turned = cat([ev[f].astype(f32).reshape(9 * cols, rows).T for f in range(faces)], 0).astype(bf)
    hotload.wait()
    for k in range(8):
        flat = dot(turned, slope[144 * k : 144 * k + 144])
        for c in range(2):
            pre[0, pl.ds((2 * k + c) * faces * rows, faces * rows)] = flat[:, c * LANES : c * LANES + LANES]
    xload.wait()

    @pl.loop(0, faces)
    def _(f):
        for c in range(cols):
            ff[2, pl.ds(c, rows, stride=cols)] = pre[0, pl.ds(c * faces * rows + f * rows, rows)]
        packed = ff[2] + jnp.where(lane == ONE, 1.0, 0.0)
        t27[f, 1 : rows + 1] = packed.astype(bf).reshape(rows, cols, LANES)
        ff[2] = jnp.where(lane < 9, pltpu.roll(packed, LANES - 9, axis=1), 0.0)
        for h in range(2):
            ff[h] = xv[f, :, :, 128 * h : 128 * h + 128].astype(f32).reshape(area, LANES)
        for j in range(3):
            for s in range(2):
                evf[j, s, ring_v(f)] = ff[j, pl.ds(area - cols if s else 0, cols)]
                ehf[j, s, ring_h(f)] = ff[j, pl.ds(cols - 1 if s else 0, rows, stride=cols)]

    def edges_out(ex, blocks):
        for s in range(2):
            ex.ed_v[s] = join(evf, (s,), blocks).astype(bf)
            ex.ed_h[s] = join(ehf, (s,), blocks).astype(bf)

    edges_out(first, 3)
    first.start()

    acca[...] = jnp.zeros_like(acca)
    accb[...] = jnp.zeros_like(accb)
    w1load.wait()
    skipload.wait()
    ff[...] = jnp.zeros_like(ff)
    for h in range(2):
        lanes = slice(128 * h, 128 * h + 128)
        for a in range(3):
            for b in range(3):
                ff[h, pl.ds(128 * a + 9 * b, 9)] = w1[3 * a + b, 256:265, lanes].astype(f32)
        ff[h, pl.ds(128 + ONE, 1)] = bias_one[...].astype(f32).reshape(1, 256)[:, lanes]
        ff[h, pl.ds(384 + 9, 9)] = wskip[256:265, lanes].astype(f32)
        ff[h, pl.ds(384 + ONE, 1)] = bias_skip[...].astype(f32).reshape(1, 256)[:, lanes]
        for a in range(3):
            we[a, :, lanes] = ff[h, pl.ds(128 * a, 128)].astype(bf)
        wse[:, lanes] = ff[h, pl.ds(384, 128)].astype(bf)
        ff[h, pl.ds(0, 256)] = jnp.zeros((256, LANES), f32)
        for t in range(TAPS):
            ff[h, pl.ds(9 * t, 9)] = w1[t, 256:265, lanes].astype(f32)
        ff[h, pl.ds(128 + 36, 9)] = wskip[256:265, lanes].astype(f32)
        for k in range(2):
            we81[k, :, lanes] = ff[h, pl.ds(128 * k, 128)].astype(bf)
    total = 32 * faces
    spread = jnp.where(
        lax.broadcasted_iota(jnp.int32, (faces, total), 1) % faces
        == lax.broadcasted_iota(jnp.int32, (faces, total), 0), 1.0, 0.0)
    spot = lax.broadcasted_iota(jnp.int32, (1, total), 1)
    side_of, step_of = spot // (8 * faces), (spot // faces % 8).astype(f32)
    source = jnp.zeros((1, total), f32)
    for s in range(4):
        entry = dot(table[s].astype(f32), spread)
        step = jnp.where(entry[2:3] > 0.5, 7.0 - step_of, step_of)
        source = source + jnp.where(side_of == s, (entry[1:2] * 8.0 + step) * faces + entry[0:1], 0.0)
    sel_t[...] = jnp.where(
        lax.broadcasted_iota(jnp.int32, (total, total), 0) == source.astype(jnp.int32), 1.0, 0.0).astype(bf)
    same = jnp.where(
        lax.broadcasted_iota(jnp.int32, (faces, faces), 1) == lax.broadcasted_iota(jnp.int32, (faces, faces), 0), 1.0, 0.0)
    for spot_index, k in enumerate((0, 1, 3, 2)):
        column = jnp.sum(same * table[k, 3:4].astype(f32), axis=1, keepdims=True)
        rule[spot_index, 0:faces] = jnp.broadcast_to(1.0 - column, (faces, LANES))

    def ring_in(ex, blocks):
        for j in range(blocks):
            lanes = slice(128 * j, 128 * j + 128)
            for s in range(2):
                rvf[j, s, pl.ds(12, 192)] = ex.rg_v[s, :, lanes].astype(f32)
                rhf[j, s, pl.ds(12, 384)] = ex.rg_h[s, :, lanes].astype(f32)
            for spot in range(4):
                s, right = spot // 2, spot % 2
                win = ex.rg_c[spot, :, lanes].astype(f32)
                edge = (tx == 3) if right else (tx == 0)
                late = jnp.where(edge, ty == 1, right == 0)
                got = jnp.where(late, win[4:16], win[0:12])
                from_v = rvf[j, s, pl.ds(192 if right else 12, 12)]
                from_h = rhf[j, right, pl.ds(384 if s else 12, 12)]
                local = jnp.where(rule[spot, 0:12] > 0.0, from_v, from_h)
                rvf[j, s, pl.ds(204 if right else 0, 12)] = jnp.where((ty == s) & edge, local, got)

    def ring_cat(rcv, rch, blocks):
        for s in range(2):
            for b in range(3):
                for j in range(2):
                    at = slice(256 * b + 128 * j, 256 * b + 128 * j + 128)
                    rcv[s, :, at] = rvf[j, s, pl.ds(12 * b, 192)].astype(bf)
                    rch[s, :, at] = rhf[j, s, pl.ds(12 * b, 384)].astype(bf)
            if blocks == 3:
                total = rvf[2, s, pl.ds(0, 192)]
                for b in (1, 2):
                    total = total + pltpu.roll(rvf[2, s, pl.ds(12 * b, 192)], 9 * b, axis=1)
                rcv[s, :, 768:896] = total.astype(bf)
                for a in range(3):
                    line = rhf[2, s, pl.ds(12 * a, 384)]
                    line = pltpu.roll(line, 18, axis=1) if s else line
                    rch[s, :, 768 + 128 * a : 896 + 128 * a] = line.astype(bf)

    def zero_h_ends(blocks):
        for j in range(blocks):
            for s in range(2):
                rhf[j, s, pl.ds(0, 12)] = jnp.zeros((12, LANES), f32)
                rhf[j, s, pl.ds(396, 12)] = jnp.zeros((12, LANES), f32)

    zero_h_ends(3)

    def add_to_edges(source_v, source_h):
        @pl.loop(0, faces)
        def _(f):
            for h in range(2):
                for s in range(2):
                    pre[h, top(f, s)] += source_v[h, s, ring_v(f)]
            for h in range(2):
                for s in range(2):
                    pre[h, side(f, s)] += source_h[h, s, ring_h(f)]
            for h in range(2):
                for s in range(2):
                    evf[h, s, ring_v(f)] = pre[h, top(f, s)]
                    ehf[h, s, ring_h(f)] = pre[h, side(f, s)]

    def w_first(t):
        return w1[t, 0:256]

    def conv_first(f, ref):
        lhs = cat(windows(ref) + windows(t27.at[f]))
        rhs = cat([w_first(t) for t in range(TAPS)] + [we[a] for a in range(3)], 0)
        split(pre, (face_rows(f),), dot(lhs, rhs))

    def first_part():
        @pl.loop(0, faces // 2)
        def _(i):
            pl.when(i == 3)(first.middle)
            for u in range(2):
                fill(xc[u], xv[2 * i + u])
            for u in range(2):
                conv_first(2 * i + u, xc[u])

    first_part()
    cload.wait()

    @pl.loop(0, faces // 2)
    def _(i):
        pair = [2 * i, 2 * i + 1]
        field = cat([cat([xv[f].reshape(area, 256), t27[f, 1 : rows + 1].reshape(area, LANES)]) for f in pair], 0)
        fresh = dot_tn(field, cat([cv[f] for f in pair], 0))
        acca[2304:2560] += fresh[0:256]
        accb[864:896] += fresh[256:288]

    @pl.loop(0, faces)
    def _(f):
        for h in range(2):
            ff[h] = cv[f, :, 128 * h : 128 * h + 128].astype(f32)
            for s in range(2):
                cvf[h, s, ring_v(f)] = ff[h, pl.ds(area - cols if s else 0, cols)]
                chf[h, s, ring_h(f)] = ff[h, pl.ds(cols - 1 if s else 0, rows, stride=cols)]

    for s in range(2):
        cev[s] = join(cvf, (s,)).astype(bf)
        ceh[s] = join(chf, (s,)).astype(bf)
    first.finish()
    ring_in(first, 3)
    ring_cat(rc1v, rc1h, 3)
    for s in range(2):
        rhs = cat([w_first(6 * s + b) for b in range(3)] + [we[2 * s]], 0)
        split(cvf, (s,), dot(rc1v[s], rhs))
        rhs = cat([w_first(3 * a + 2 * s) for a in range(3)] + [we[a] for a in range(3)], 0)
        split(chf, (s,), dot(rc1h[s], rhs))
    add_to_edges(cvf, chf)
    for h in range(2):
        for s in range(2):
            evf[h, s], slev[h, s] = gelu_slope(evf[h, s])
            ehf[h, s], sleh[h, s] = gelu_slope(ehf[h, s])
    edges_out(second, 2)
    second.start()

    def conv_second(f):
        lhs = cat(windows(hc.at[f]))
        rhs = cat([w2[t] for t in range(TAPS)], 0)
        split(pre, (face_rows(f),), dot(lhs, rhs))

    def second_part():
        @pl.loop(0, faces // 2)
        def _(i):
            pl.when(i == 3)(second.middle)
            for u in range(2):
                f = 2 * i + u
                act, sl = gelu_slope(join(pre, (face_rows(f),)))
                slope[face_rows(f)] = sl.astype(bf)
                fill(hc.at[f], act.astype(bf).reshape(rows, cols, 256))
            for u in range(2):
                conv_second(2 * i + u)

    w2load.wait()
    second_part()
    second.finish()
    ring_in(second, 2)
    ring_cat(rc2v, rc2h, 2)
    for s in range(2):
        split(cvf, (s,), dot(rc2v[s], cat([w2[6 * s + b] for b in range(3)], 0)))
        split(chf, (s,), dot(rc2h[s], cat([w2[3 * a + 2 * s] for a in range(3)], 0)))
    add_to_edges(cvf, chf)

    def ring_grads(ex, taps, blocks):
        for s in range(2):
            lhs = cat([cat([rvf[j, s, pl.ds(12 * b, 216)] for j in range(2)]).astype(bf) for b in range(3)])
            base = 0 if s else 6
            rhs = cat([taps(8 - (base + b)) for b in range(3)], 1)
            out = dot_nt(lhs, rhs)
            if blocks == 3:
                mid = dot_nt(gev[s], we[2 * s])
                pad = jnp.zeros((24, LANES), f32)
                mid = cat([pad, mid, pad], 0)
                tail = mid[24:240]
                for b in (1, 2):
                    tail = tail + pltpu.roll(mid[24 - 12 * b : 240 - 12 * b], LANES - 9 * b, axis=1)
                out = cat([out, jnp.where(lane < 9, tail, 0.0)])
            for j in range(blocks):
                cvf[j, s] = out[12:204, 128 * j : 128 * j + 128]
                ff[j, pl.ds(256 * s, 12)] = out[0:12, 128 * j : 128 * j + 128]
                ff[j, pl.ds(256 * s + 128, 12)] = out[204:216, 128 * j : 128 * j + 128]
            lhs = cat([cat([rhf[j, s, pl.ds(12 * a, 384)] for j in range(2)]).astype(bf) for a in range(3)])
            base = 0 if s else 2
            rhs = cat([taps(8 - (base + 3 * a)) for a in range(3)], 1)
            out = dot_nt(lhs, rhs)
            if blocks == 3:
                tail = dot_nt(lhs, cat([we[2 - a] for a in range(3)], 1))
                tail = pltpu.roll(tail, LANES - 18, axis=1) if s else tail
                out = cat([out, jnp.where(lane < 9, tail, 0.0)])
            for j in range(blocks):
                chf[j, s] = out[:, 128 * j : 128 * j + 128]
        for j in range(blocks):
            lanes = slice(128 * j, 128 * j + 128)
            for spot in range(4):
                s, right = spot // 2, spot % 2
                v = ff[j, pl.ds(256 * s + 128 * right, 12)]
                edge = (tx == 3) if right else (tx == 0)
                late = jnp.where(edge, ty == 1, right == 0)
                zero = jnp.zeros((4, LANES), f32)
                ex.rg_c[spot, :, lanes] = jnp.where(late, cat([zero, v], 0), cat([v, zero], 0)).astype(bf)

                @pl.when((ty == s) & edge)
                def _(j=j, s=s, right=right, spot=spot, v=v):
                    take = rule[spot, 0:12] > 0.0
                    cvf[j, s, pl.ds(180 if right else 0, 12)] += jnp.where(take, v, 0.0)
                    chf[j, right, pl.ds(372 if s else 0, 12)] += jnp.where(take, 0.0, v)
        for s in range(2):
            ex.rg_v[s] = join(cvf, (s,), blocks).astype(bf)
            ex.rg_h[s] = join(chf, (s,), blocks).astype(bf)

    def edge_grads(make_v, make_h):
        for s in range(2):
            for h in range(2):
                lanes = slice(128 * h, 128 * h + 128)
                v = make_v(h, s).astype(bf)
                gev[s, :, lanes] = v
                rvf[h, s, pl.ds(0, 24)] = jnp.zeros((24, LANES), f32)
                rvf[h, s, pl.ds(216, 24)] = jnp.zeros((24, LANES), f32)
                rvf[h, s, pl.ds(24, 192)] = v.astype(f32)
                v = make_h(h, s).astype(bf)
                geh[s, :, lanes] = v
                rhf[h, s, pl.ds(12, 384)] = v.astype(f32)

    def slope_two(u, h):
        return gelu_slope(u + bias_two[...].astype(f32).reshape(1, 256)[:, 128 * h : 128 * h + 128])[1]

    edge_grads(
        lambda h, s: slope_two(evf[h, s], h) * cev[s, :, 128 * h : 128 * h + 128].astype(f32),
        lambda h, s: slope_two(ehf[h, s], h) * ceh[s, :, 128 * h : 128 * h + 128].astype(f32),
    )
    ring_grads(third, lambda t: w2[t], 2)
    third.start()

    def out_copy(u, f):
        return pltpu.make_async_copy(ost.at[u], out_ref.at[f], lsem.at[3 + u])

    def third_part():
        @pl.loop(0, faces // 2)
        def _(i):
            pl.when(i == 4)(third.middle)
            for u in range(2):
                out_copy(u, 0).wait()
            grads, ready = [], []
            for u in range(2):
                f = 2 * i + u
                act, sl = gelu_slope(join(pre, (face_rows(f),)) + bias_two[...].astype(f32).reshape(1, 256))
                grad = (cv[f].astype(f32) * sl).astype(bf)
                accb[896:897] += jnp.sum(grad.astype(f32), axis=0, keepdims=True)
                field = cat([xv[f].reshape(area, 256), t27[f, 1 : rows + 1].reshape(area, LANES)])
                skip = dot(field, cat([wskip[0:256], wse[...]], 0))
                ready.append((act + skip).astype(bf))
                grads.append(grad)
            for u in range(2):
                cv[2 * i + u] = grads[u]
                ost[u] = ready[u]
            pair = cat(grads, 0)
            for a in range(3):
                field = cat([hc[2 * i + u, a : a + rows].reshape(area, 768) for u in range(2)], 0)
                acca[768 * a : 768 * a + 768] += dot_tn(field, pair)
            for u in range(2):
                out_copy(u, 2 * i + u).start()

    def third_back():
        @pl.loop(0, faces // 2)
        def _(i):
            sums("back", i)
            for u in range(2):
                fill(xc[u], cv[2 * i + u].reshape(rows, cols, 256))
            rhs = cat([w2[8 - t] for t in range(TAPS)], 1)
            for u in range(2):
                split(pre, (face_rows(2 * i + u),), dot_nt(cat(windows(xc[u])), rhs))

    def ring_kernel_grads(grad_ref, extra, rcv, rch):
        for s in range(2):
            fresh = dot_tn(rcv[s], gev[s])
            for b in range(3):
                at = BLOCKS[b] + 512 * s if extra else 1536 * s + 256 * b
                grad_ref[at : at + 256] += fresh[256 * b : 256 * b + 256]
            if extra:
                grad_ref[768 + 64 * s : 800 + 64 * s] += fresh[768:800]
            fresh = dot_tn(rch[s], geh[s])
            for a in range(3):
                at = BLOCKS[2 * s] + 256 * a if extra else 768 * a + 512 * s
                grad_ref[at : at + 256] += fresh[256 * a : 256 * a + 256]
                if extra:
                    grad_ref[768 + 32 * a : 800 + 32 * a] += fresh[768 + 128 * a : 800 + 128 * a]

    for u in range(2):
        ost[u] = jnp.zeros(ost.shape[1:], bf)
        out_copy(u, u).start()
    third_part()
    ring_kernel_grads(acca, False, rc2v, rc2h)
    totals = {}
    for index, (name, first_row, count, way) in enumerate(SUMS):
        if name == "a":
            totals[name] = Total(index, acca, first_row, outa, first_row, landa, first_row, count, way)
        else:
            totals[name] = Total(index, accb, first_row, slope, first_row, slope, 2560 + first_row, count, way)
    sums("middle")
    third_back()
    for u in range(2):
        out_copy(u, 0).wait()
    cload = load(cot_in, cv, 2)
    third.finish()
    third.stage(2)

    @pl.loop(0, faces)
    def _(f):
        for h in range(2):
            for s in range(2):
                pre[h, top(f, s)] += evf[h, s, ring_v(f)]
        for h in range(2):
            for s in range(2):
                pre[h, side(f, s)] += ehf[h, s, ring_h(f)]
        for h in range(2):
            for s in range(2):
                evf[h, s, ring_v(f)] = pre[h, top(f, s)]
                ehf[h, s, ring_h(f)] = pre[h, side(f, s)]

    edge_grads(lambda h, s: evf[h, s] * slev[h, s], lambda h, s: ehf[h, s] * sleh[h, s])
    ring_grads(fourth, w_first, 3)
    fourth.start()
    sums("sent")

    def first_grads(f):
        grad = (join(pre, (face_rows(f),)) * slope[face_rows(f)].astype(f32)).astype(bf)
        fill(hc.at[f], grad.reshape(rows, cols, 256))

    def shifted_grads(g, start, choose):
        for u in range(3):
            xc[0][1 : rows + 1, :, 256 * u : 256 * u + 256] = choose(xv[3 * g + u])
        grads = cat([hc[3 * g + u, 1 : rows + 1, :, 256:512].reshape(area, 256) for u in range(3)], 0)
        field = cat([
            cat([xc[0][a : a + rows, :, 256 * u : 256 * u + 256].reshape(area, 256) for a in range(3)])
            for u in range(3)], 0)
        accb[pl.ds(start, 768)] += dot_tn(field, grads)
        return grads

    def fourth_start():
        @pl.loop(0, faces // 3)
        def _(g):
            pl.when(g == 2)(fourth.middle)
            for u in range(3):
                first_grads(3 * g + u)
            grads = shifted_grads(g, 0, lambda v: shifts(v)[0])
            extra = cat([
                cat([t27[3 * g + u, a : a + rows].reshape(area, LANES) for a in range(3)]) for u in range(3)], 0)
            fresh = dot_tn(extra, grads)
            for a in range(3):
                accb[768 + 32 * a : 800 + 32 * a] += fresh[128 * a : 128 * a + 32]

    def free_slopes():
        for target in ({"dp": core_mate}, {"dp": x_mate}):
            pl.semaphore_signal(credit, inc=1, device_id=target, device_id_type=pl.DeviceIdType.MESH)
        for q in range(8):
            @pl.when(place != q)
            def _(q=q):
                pl.semaphore_signal(credit, inc=1, device_id=dev(q // 4, q % 4), device_id_type=pl.DeviceIdType.MESH)

    def fourth_rest():
        @pl.loop(0, 2 * faces // 3)
        def _(i):
            b = 1 + i // 4
            sums("more", i)
            shifted_grads(i % 4, pl.multiple_of(256 + 768 * b, 256), lambda v: jnp.where(b == 1, v, shifts(v)[1]))

    ring_kernel_grads(accb, True, rc1v, rc1h)
    fourth_start()
    free_slopes()
    pl.semaphore_wait(credit, 9)
    sums("first")
    fourth_rest()
    hot = landa.at[0:1152]
    hotload = load(hot_back_in, hot, 11)
    sums("third")
    fourth.finish()
    fourth.stage(3)

    def part(u, j, start=0, size=area, stride=1):
        return pl.ds((3 * u + j) * area + start, size, stride=stride)

    def gx_copy(u, f):
        return pltpu.make_async_copy(ost.at[u], gx_ref.at[f], lsem.at[3 + u])

    def last_part():
        @pl.loop(0, faces // 2)
        def _(i):
            sums("last", i)
            for u in range(2):
                gx_copy(u, 0).wait()
            col = lax.broadcasted_iota(jnp.int32, (area, 1), 0) % cols
            for u in range(2):
                f = 2 * i + u
                cot = cv[f]
                rhs = cat([w_first(8 - t) for t in range(TAPS)] + [wskip[0:256]], 1)
                main = dot_nt(cat(windows(hc.at[f]) + [cot]), rhs)
                for h in range(2):
                    pre[0, part(u, h)] = main[:, 128 * h : 128 * h + 128]
                taps = dot_nt(cat([hc[f, 1 : rows + 1, :, 256:512].reshape(area, 256), cot]), cat([we81[0], we81[1]], 1))
                edge = jnp.zeros((cols, LANES), f32)
                lines = (
                    cat([taps[cols:], edge], 0)
                    + pltpu.roll(taps, LANES - 27, axis=1)
                    + cat([edge, pltpu.roll(taps, LANES - 54, axis=1)[: area - cols]], 0))
                after = jnp.where(col == cols - 1, 0.0, pltpu.roll(lines, area - 1, axis=0))
                before = jnp.where(col == 0, 0.0, pltpu.roll(lines, 1, axis=0))
                pre[0, part(u, 2)] = after + pltpu.roll(lines, LANES - 9, axis=1) + pltpu.roll(before, LANES - 18, axis=1)
            for u in range(2):
                f = 2 * i + u
                for j in range(3):
                    for s in range(2):
                        pre[0, part(u, j, area - cols if s else 0, cols)] += evf[j, s, ring_v(f)]
                for j in range(3):
                    for s in range(2):
                        pre[0, part(u, j, cols - 1 if s else 0, rows, cols)] += ehf[j, s, ring_h(f)]
                for c in range(cols):
                    here = pre[0, part(u, 2, c, rows, cols)].astype(bf)
                    rc1h[c // 8, rows16(f * rows, rows), c % 8 * LANES : c % 8 * LANES + LANES] = here
                ost[u] = cat([pre[0, part(u, 0)], pre[0, part(u, 1)]]).astype(bf)
            for u in range(2):
                gx_copy(u, 2 * i + u).start()

    cload.wait()
    for u in range(2):
        gx_copy(u, u).start()
    last_part()
    sums("end")
    hotload.wait()
    back = sum(
        dot_nt(rc1h[k // 4, :, k % 4 * 256 : k % 4 * 256 + 256], hot[144 * k : 144 * k + 144]) for k in range(8))
    for f in range(faces):
        ev[f] = back[f * rows : f * rows + rows].T.astype(bf).reshape(9, cols, rows)
    eout = pltpu.make_async_copy(ev, gext_ref, lsem.at[1])
    eout.start()
    sums("rest")
    stores = []
    for a in range(3):
        for b in range(3):
            stores.append(pltpu.make_async_copy(
                slope.at[pl.ds(BLOCKS[b] + 256 * a, 256)], sumb_ref.at[pl.ds(256 * (3 * a + b), 256)], lsem.at[9]))
            stores[-1].start()
    tail = slope[768:1024].astype(f32)
    for t in range(TAPS):
        tails[t] = tail[32 * (t // 3) + 9 * (t % 3) : 32 * (t // 3) + 9 * (t % 3) + 9]
    tails[TAPS] = tail[96 + 9 : 96 + 18]
    rests[0:1] = tail[32 + ONE : 32 + ONE + 1]
    rests[1:2] = tail[128:129]
    rests[2:3] = tail[96 + ONE : 96 + ONE + 1]
    for u in range(2):
        gx_copy(u, 0).wait()
    eout.wait()
    pltpu.make_async_copy(outa, suma_ref, lsem.at[8]).wait()
    pltpu.make_async_copy(slope.at[0:2304], sumb_ref, lsem.at[9]).wait()
    for ex in (first, second, third, fourth):
        ex.drain()


def packing(extra, cols, moves):
    hot = np.zeros((extra, cols, cols, LANES), ml_dtypes.bfloat16)
    for start, step in moves:
        for channel in range(extra):
            for column in range(cols):
                if 0 <= column - step < cols:
                    hot[channel, column, column - step, start + channel] = 1
    hot = hot.reshape(extra * cols, cols * LANES // 256, 256)
    return hot.transpose(1, 0, 2).reshape(-1, 256)


def fast_device(
    features, extra_inputs, first_kernel, first_bias, second_kernel, second_bias,
    skip_kernel, skip_bias, seam_table, cotangent,
):
    f32, bf = jnp.float32, jnp.bfloat16
    _, faces, rows, cols, ch = features.shape
    area = rows * cols
    extra = extra_inputs.shape[-1]
    vm, hbm = pl.BlockSpec(memory_space=pltpu.VMEM), pl.BlockSpec(memory_space=pl.ANY)
    shape = jax.ShapeDtypeStruct

    def exchange_bufs(lanes, windows):
        return [
            pltpu.VMEM((2, 192, lanes), bf), pltpu.VMEM((2, 384, lanes), bf), pltpu.VMEM((384, lanes), bf),
            pltpu.VMEM((384, lanes), bf), pltpu.VMEM((2, 192, lanes), bf), pltpu.VMEM((2, 384, lanes), bf),
            pltpu.VMEM((4, 16, lanes), bf), pltpu.VMEM((8 * windows, 16, lanes), bf),
            pltpu.VMEM((2 * windows, 16, lanes), bf),
        ]

    cat_shape = (rows + 2, cols, 3 * ch)
    sums = (SUM_ROWS, ch)
    scratch = [
        pltpu.VMEM((TAPS, ch + extra, ch), bf), pltpu.VMEM((TAPS, ch, ch), bf), pltpu.VMEM((ch + extra, ch), bf),
        pltpu.VMEM((3, LANES, ch), bf), pltpu.VMEM((LANES, ch), bf), pltpu.VMEM((2, LANES, ch), bf),
        pltpu.VMEM((384, 384), bf),
        pltpu.VMEM((4, 16, LANES), f32),
        pltpu.VMEM((faces, rows, cols, ch), bf), pltpu.VMEM((faces, extra, cols, rows), bf),
        pltpu.VMEM((faces, area, ch), bf), pltpu.VMEM((faces, rows + 2, cols, LANES), bf),
        [pltpu.VMEM(cat_shape, bf)] * 2, pltpu.VMEM((faces,) + cat_shape, bf),
        pltpu.VMEM((2, faces * area, LANES), f32), pltpu.VMEM((faces * area, ch), bf),
        pltpu.VMEM((2, 2, 192, LANES), f32), pltpu.VMEM((2, 2, 384, LANES), f32),
        pltpu.VMEM((2, 192, ch), bf), pltpu.VMEM((2, 384, ch), bf),
        pltpu.VMEM((2, area, ch), bf),
        pltpu.VMEM((3, area, LANES), f32),
        pltpu.VMEM((3, 2, 192, LANES), f32), pltpu.VMEM((3, 2, 384, LANES), f32),
        pltpu.VMEM((3, 2, 240, LANES), f32), pltpu.VMEM((3, 2, 408, LANES), f32),
        pltpu.VMEM((3, 2, 192, LANES), f32), pltpu.VMEM((3, 2, 384, LANES), f32),
        pltpu.VMEM((2, 192, 896), bf), pltpu.VMEM((2, 384, 1152), bf),
        pltpu.VMEM((2, 192, 768), bf), pltpu.VMEM((2, 384, 768), bf),
        pltpu.VMEM((2, 192, ch), bf), pltpu.VMEM((2, 384, ch), bf),
        pltpu.VMEM(sums, f32), pltpu.VMEM(sums, f32), pltpu.VMEM(sums, bf), pltpu.VMEM(sums, bf),
        [exchange_bufs(384, 0 + 1), exchange_bufs(256, 1), exchange_bufs(256, 1), exchange_bufs(384, 1)],
        pltpu.SemaphoreType.DMA((4, 48)), pltpu.SemaphoreType.DMA((4, 33)),
        pltpu.SemaphoreType.DMA((len(SUMS), 20)), pltpu.SemaphoreType.DMA((len(SUMS), 20)),
        pltpu.SemaphoreType.REGULAR, pltpu.SemaphoreType.REGULAR((len(SUMS), 4)), pltpu.SemaphoreType.DMA((12,)),
    ]
    out = pl.pallas_call(
        whole_block,
        out_shape=(
            shape((faces, area, ch), bf), shape((faces, area, ch), bf), shape((faces, extra, cols, rows), bf),
            shape(sums, bf), shape((TAPS * ch, ch), bf), shape((TAPS + 1, extra, ch), f32), shape((8, ch), f32),
        ),
        in_specs=[hbm] * 5 + [vm] * 4 + [hbm] * 3,
        out_specs=[hbm] * 5 + [vm] * 2,
        scratch_shapes=scratch,
        compiler_params=pltpu.CompilerParams(
            collective_id=0, has_side_effects=True, vmem_limit_bytes=65400 * 1024),
    )(
        features[0], extra_inputs[0].transpose(0, 3, 2, 1), first_kernel.reshape(TAPS, ch + extra, ch),
        second_kernel.reshape(TAPS, ch, ch), skip_kernel, first_bias, second_bias, skip_bias,
        seam_table.transpose(1, 2, 0), cotangent.reshape(faces, area, ch),
        packing(extra, cols, ((0, -1), (extra, 0), (2 * extra, 1))), packing(extra, cols, ((0, 0),)),
    )
    block_output, grad_features, grad_extra, suma, sumb, tails, rests = out
    tall = TAPS * ch
    first_grad = jnp.concatenate(
        [sumb.reshape(3, 3, ch, ch).astype(f32), tails[:TAPS].reshape(3, 3, extra, ch)], 2)
    return (
        block_output.reshape(features.shape),
        grad_features.reshape(features.shape),
        grad_extra.transpose(0, 3, 2, 1)[None],
        first_grad,
        rests[0],
        suma[:tall].astype(f32).reshape(second_kernel.shape),
        rests[1],
        jnp.concatenate([suma[tall:].astype(f32), tails[TAPS]], 0),
        rests[2],
    )


def solution(mesh):
    fits = mesh.shape["ty"] == 2 and mesh.shape["tx"] == 4

    def block(*args):
        tile = args[0].shape
        if fits and tile[1:] == (12, 32, 16, 256) and args[1].shape[-1] == 9:
            return fast_device(*args)
        return per_device(*args)

    return jax.shard_map(
        block,
        mesh=mesh,
        in_specs=(
            P("dp", None, "ty", "tx", None),
            P("dp", None, "ty", "tx", None),
            P(),
            P(),
            P(),
            P(),
            P(),
            P(),
            P(),
            P("dp", None, "ty", "tx", None),
        ),
        out_specs=(
            P("dp", None, "ty", "tx", None),
            P("dp", None, "ty", "tx", None),
            P("dp", None, "ty", "tx", None),
            P(),
            P(),
            P(),
            P(),
            P(),
            P(),
        ),
        check_vma=False,
    )
```

```python
from functools import partial

import jax
import jax.numpy as jnp
import ml_dtypes
import numpy as np
from jax import lax
from jax.experimental import pallas as pl
from jax.experimental.pallas import tpu as pltpu
from jax.sharding import PartitionSpec as P


def extended(value, sides, width):
    for axis, dim in sides:
        size, length = (lax.axis_size(axis), value.shape[dim])
        up = [(i, (i + 1) % size) for i in range(size - 1)]
        down = [(j, i) for i, j in up]
        last = lax.slice_in_dim(value, length - width, length, axis=dim)
        leading = lax.slice_in_dim(value, 0, width, axis=dim)
        before = lax.ppermute(last, axis, up)
        after = lax.ppermute(leading, axis, down)
        value = jnp.concatenate([before, value, after], axis=dim)
    return value


def face_lines(edge_rows, seam_table):
    face_hot = (
        seam_table[:, :, 0][:, :, None]
        == jnp.arange(edge_rows.shape[1], dtype=jnp.int32)[None, None, :]
    ).astype(edge_rows.dtype)
    side_hot = (
        seam_table[:, :, 1][:, :, None] == jnp.arange(4, dtype=jnp.int32)[None, None, :]
    ).astype(edge_rows.dtype)
    chooser = face_hot[:, :, :, None] * side_hot[:, :, None, :]
    side_lines = jnp.einsum(
        "fsgt,bgtnc->bfsnc",
        chooser,
        edge_rows,
        precision=lax.Precision.HIGHEST,
        preferred_element_type=jnp.float32,
    ).astype(edge_rows.dtype)
    flipped = seam_table[:, :, 2][None, :, :, None, None] == 1
    side_lines = jnp.where(flipped, side_lines[:, :, :, ::-1, :], side_lines)
    corner_rule = seam_table[:, :, 3][None, :, :, None] == 0
    upper_line = side_lines[:, :, 0]
    right_line = side_lines[:, :, 1]
    lower_line = side_lines[:, :, 2]
    left_line = side_lines[:, :, 3]
    upper_left = jnp.where(corner_rule[:, :, 0], upper_line[:, :, 0], left_line[:, :, 0])
    upper_right = jnp.where(corner_rule[:, :, 1], upper_line[:, :, -1], right_line[:, :, 0])
    lower_right = jnp.where(corner_rule[:, :, 2], lower_line[:, :, -1], right_line[:, :, -1])
    lower_left = jnp.where(corner_rule[:, :, 3], lower_line[:, :, 0], left_line[:, :, -1])
    upper_full = jnp.concatenate(
        [upper_left[:, :, None], upper_line, upper_right[:, :, None]], axis=2
    )
    right_full = jnp.concatenate(
        [upper_right[:, :, None], right_line, lower_right[:, :, None]], axis=2
    )
    lower_full = jnp.concatenate(
        [lower_left[:, :, None], lower_line, lower_right[:, :, None]], axis=2
    )
    left_full = jnp.concatenate([upper_left[:, :, None], left_line, lower_left[:, :, None]], axis=2)
    return (upper_full, right_full, lower_full, left_full)


def seam_layer(edge_rows, seam_table, place):
    row_index, column_index, row_count, column_count, tile_rows, tile_columns = place
    upper_full, right_full, lower_full, left_full = face_lines(edge_rows, seam_table)
    upper_piece = lax.dynamic_slice_in_dim(
        upper_full, column_index * tile_columns, tile_columns + 2, 2
    )
    lower_piece = lax.dynamic_slice_in_dim(
        lower_full, column_index * tile_columns, tile_columns + 2, 2
    )
    left_piece = lax.dynamic_slice_in_dim(left_full, row_index * tile_rows, tile_rows + 2, 2)
    right_piece = lax.dynamic_slice_in_dim(right_full, row_index * tile_rows, tile_rows + 2, 2)
    grid_rows = lax.broadcasted_iota(jnp.int32, (tile_rows + 2, tile_columns + 2, 1), 0)
    grid_columns = lax.broadcasted_iota(jnp.int32, (tile_rows + 2, tile_columns + 2, 1), 1)
    seam_cells = jnp.zeros(
        upper_piece.shape[:2] + (tile_rows + 2, tile_columns + 2, upper_piece.shape[-1]),
        edge_rows.dtype,
    )
    seam_cells = jnp.where((grid_rows == 0) & (row_index == 0), upper_piece[:, :, None], seam_cells)
    seam_cells = jnp.where(
        (grid_rows == tile_rows + 1) & (row_index == row_count - 1),
        lower_piece[:, :, None],
        seam_cells,
    )
    seam_cells = jnp.where(
        (grid_columns == 0) & (column_index == 0), left_piece[:, :, :, None], seam_cells
    )
    seam_cells = jnp.where(
        (grid_columns == tile_columns + 1) & (column_index == column_count - 1),
        right_piece[:, :, :, None],
        seam_cells,
    )
    return seam_cells


def join_tiles(tile_parts):
    moved = jnp.moveaxis(tile_parts, 0, 2)
    return moved.reshape(
        tile_parts.shape[1],
        tile_parts.shape[2],
        tile_parts.shape[0] * tile_parts.shape[3],
        tile_parts.shape[4],
    )


def face_edges(field):
    row_count = lax.axis_size("ty")
    column_count = lax.axis_size("tx")
    row_edges = jnp.stack([field[:, :, 0], field[:, :, -1]], axis=2)
    column_edges = jnp.stack([field[:, :, :, -1], field[:, :, :, 0]], axis=2)
    row_gathered, column_gathered = (
        lax.all_gather(row_edges[None], ("ty", "tx"), axis=0, tiled=True),
        lax.all_gather(column_edges[None], ("ty", "tx"), axis=0, tiled=True),
    )
    row_grid = row_gathered.reshape((row_count, column_count) + row_edges.shape)
    column_grid = column_gathered.reshape((row_count, column_count) + column_edges.shape)
    upper_edge = join_tiles(row_grid[0, :, :, :, 0])
    lower_edge = join_tiles(row_grid[row_count - 1, :, :, :, 1])
    right_edge = join_tiles(column_grid[:, column_count - 1, :, :, 0])
    left_edge = join_tiles(column_grid[:, 0, :, :, 1])
    return jnp.stack([upper_edge, right_edge, lower_edge, left_edge], axis=2)


def extend(field, seam_table, place):
    rimmed = extended(field, (("ty", 2), ("tx", 3)), 1)
    return rimmed + seam_layer(face_edges(field), seam_table, place)


def collect(grad_padded, seam_table, place):
    row_index, column_index, row_count, column_count, tile_rows, tile_columns = place
    widened = extended(grad_padded.astype(jnp.bfloat16), (("ty", 2), ("tx", 3)), 1).astype(
        grad_padded.dtype
    )
    inside = grad_padded[:, :, 1:-1, 1:-1]
    inside = inside.at[:, :, 0].add(widened[:, :, 0, 2 : tile_columns + 2])
    inside = inside.at[:, :, -1].add(widened[:, :, tile_rows + 3, 2 : tile_columns + 2])
    inside = inside.at[:, :, :, 0].add(widened[:, :, 2 : tile_rows + 2, 0])
    inside = inside.at[:, :, :, -1].add(widened[:, :, 2 : tile_rows + 2, tile_columns + 3])
    inside = inside.at[:, :, 0, 0].add(widened[:, :, 0, 0])
    inside = inside.at[:, :, 0, -1].add(widened[:, :, 0, tile_columns + 3])
    inside = inside.at[:, :, -1, 0].add(widened[:, :, tile_rows + 3, 0])
    inside = inside.at[:, :, -1, -1].add(widened[:, :, tile_rows + 3, tile_columns + 3])
    blank = jnp.zeros(
        grad_padded.shape[:2] + (4, tile_rows * row_count, grad_padded.shape[-1]), jnp.float32
    )
    unused, seam_pull = jax.vjp(
        lambda edge_values: seam_layer(edge_values, seam_table, place), blank
    )
    (edge_grads,) = seam_pull(grad_padded)
    edge_grads = lax.psum(edge_grads, ("ty", "tx"))
    upper_part = lax.dynamic_slice_in_dim(
        edge_grads[:, :, 0], column_index * tile_columns, tile_columns, 2
    )
    right_part = lax.dynamic_slice_in_dim(edge_grads[:, :, 1], row_index * tile_rows, tile_rows, 2)
    lower_part = lax.dynamic_slice_in_dim(
        edge_grads[:, :, 2], column_index * tile_columns, tile_columns, 2
    )
    left_part = lax.dynamic_slice_in_dim(edge_grads[:, :, 3], row_index * tile_rows, tile_rows, 2)
    inside = inside.at[:, :, 0].add(jnp.where(row_index == 0, upper_part, 0.0))
    inside = inside.at[:, :, -1].add(jnp.where(row_index == row_count - 1, lower_part, 0.0))
    inside = inside.at[:, :, :, 0].add(jnp.where(column_index == 0, left_part, 0.0))
    inside = inside.at[:, :, :, -1].add(
        jnp.where(column_index == column_count - 1, right_part, 0.0)
    )
    return inside


def conv_valid(padded, kernel):
    shape_in = padded.shape
    merged = padded.reshape(shape_in[0] * shape_in[1], shape_in[2], shape_in[3], shape_in[4])
    result = lax.conv_general_dilated(
        merged,
        kernel,
        (1, 1),
        "VALID",
        dimension_numbers=("NHWC", "HWIO", "NHWC"),
        preferred_element_type=jnp.float32,
    )
    return result.reshape(
        shape_in[0], shape_in[1], shape_in[2] - 2, shape_in[3] - 2, kernel.shape[-1]
    )


def conv_back(grad_pre, kernel):
    flipped = jnp.transpose(kernel[::-1, ::-1], (0, 1, 3, 2))
    surround = jnp.pad(grad_pre, ((0, 0), (0, 0), (2, 2), (2, 2), (0, 0)))
    return conv_valid(surround, flipped)


def kernel_grad(padded, grad_pre):
    tile_rows = grad_pre.shape[2]
    tile_columns = grad_pre.shape[3]
    pieces = []
    for offset_row in range(3):
        for offset_column in range(3):
            window = padded[
                :,
                :,
                offset_row : offset_row + tile_rows,
                offset_column : offset_column + tile_columns,
            ]
            pieces.append(
                jnp.einsum("sfhwc,sfhwd->cd", window, grad_pre, preferred_element_type=jnp.float32)
            )
    return jnp.stack(pieces).reshape(3, 3, padded.shape[-1], grad_pre.shape[-1])


def per_device(
    features,
    extra_inputs,
    first_kernel,
    first_bias,
    second_kernel,
    second_bias,
    skip_kernel,
    skip_bias,
    seam_table,
    cotangent,
):
    place = (
        lax.axis_index("ty"),
        lax.axis_index("tx"),
        lax.axis_size("ty"),
        lax.axis_size("tx"),
        features.shape[2],
        features.shape[3],
    )
    gelu_exact = partial(jax.nn.gelu, approximate=False)
    joined = jnp.concatenate([features, extra_inputs], axis=-1)
    padded_one = extend(joined, seam_table, place)
    pre_one = conv_valid(padded_one, first_kernel) + first_bias
    active_one, slope_one = jax.vjp(gelu_exact, pre_one)
    hidden = active_one.astype(jnp.bfloat16)
    padded_two = extend(hidden, seam_table, place)
    pre_two = conv_valid(padded_two, second_kernel) + second_bias
    active_two, slope_two = jax.vjp(gelu_exact, pre_two)
    skipped = (
        jnp.einsum("sfhwc,cd->sfhwd", joined, skip_kernel, preferred_element_type=jnp.float32)
        + skip_bias
    )
    block_output = (active_two + skipped).astype(jnp.bfloat16)
    (grad_two,) = slope_two(cotangent.astype(jnp.float32))
    grad_two = grad_two.astype(jnp.bfloat16)
    second_kernel_grad = kernel_grad(padded_two, grad_two)
    second_bias_grad = jnp.sum(grad_two, axis=(0, 1, 2, 3), dtype=jnp.float32)
    grad_hidden = collect(conv_back(grad_two, second_kernel), seam_table, place)
    (grad_one,) = slope_one(grad_hidden)
    grad_one = grad_one.astype(jnp.bfloat16)
    first_kernel_grad = kernel_grad(padded_one, grad_one)
    first_bias_grad = jnp.sum(grad_one, axis=(0, 1, 2, 3), dtype=jnp.float32)
    grad_joined = collect(conv_back(grad_one, first_kernel), seam_table, place)
    grad_joined = grad_joined + jnp.einsum(
        "sfhwd,cd->sfhwc", cotangent, skip_kernel, preferred_element_type=jnp.float32
    )
    skip_kernel_grad = jnp.einsum(
        "sfhwc,sfhwd->cd", joined, cotangent, preferred_element_type=jnp.float32
    )
    skip_bias_grad = jnp.sum(cotangent, axis=(0, 1, 2, 3), dtype=jnp.float32)
    summed = lax.psum(
        (
            first_kernel_grad,
            first_bias_grad,
            second_kernel_grad,
            second_bias_grad,
            skip_kernel_grad,
            skip_bias_grad,
        ),
        ("dp", "ty", "tx"),
    )
    grad_joined = grad_joined.astype(jnp.bfloat16)
    channels = features.shape[-1]
    return (
        block_output,
        grad_joined[..., :channels],
        grad_joined[..., channels:],
        summed[0],
        summed[1],
        summed[2],
        summed[3],
        summed[4],
        summed[5],
    )


TAPS = 9
SUM_ROWS = 2560
LANES = 128
PACK = 27
ONE = 27
FOUR = ("core", "x", "y", "z")
FOURY = ("core", "y", "x", "z")
SUMS = (("a", 0, 2560, FOUR), ("b", 0, 1024, FOUR), ("c", 1024, 512, FOURY), ("d", 1536, 1024, FOURY))
BLOCKS = (0, 1024, 1792)
SUM_PLAN = {
    ('middle', 0): (('a', 0),),
    ('back', 4): (('a', 1),),
    ('sent', 0): (('a', 2),),
    ('first', 0): (('b', 0),),
    ('more', 4): (('b', 1), ('c', 0)),
    ('third', 0): (('a', 3), ('c', 1), ('d', 0)),
    ('out', 2): (('b', 2),),
    ('out', 3): (('d', 1),),
    ('out', 5): (('c', 2),),
    ('last', 0): (('a', 4), ('b', 3), ('d', 2)),
    ('last', 1): (('c', 3), ('d', 3)),
    ('last', 2): (('a', 5), ('b', 4), ('c', 4), ('d', 4)),
    ('last', 3): (('b', 5), ('c', 5), ('d', 5)),
    ('last', 4): (('a', 6), ('b', 6), ('c', 6)),
    ('last', 5): (('c', 7), ('d', 6)),
    ('end', 0): (('a', 7), ('b', 7), ('c', 8), ('d', 7)),
    ('rest', 0): (('a', 8), ('b', 8), ('d', 8)),
}


def whole_block(
    x_in, ext_in, w1_in, w2_in, skip_in, bias_one, bias_two, bias_skip, table, cot_in, hot_in, hot_back_in,
    out_ref, gx_ref, gext_ref, second_ref, first_ref, kept, skip_ref, one_ref, two_ref, three_ref,
    w1, w2, wskip, we, wse, we81, sel_t, rule, tails,
    xv, ev, cv, t27, xc, hc, pre, slope, slev, sleh, cev, ceh,
    ff, evf, ehf, rvf, rhf, cvf, chf, rc1v, rc1h, rc2v, rc2h, gev, geh,
    acca, accb, outa, landa, bufs, ssem, rsem, sum_ssem, sum_rsem, credit, ack, lsem,
):
    f32, bf = jnp.float32, jnp.bfloat16
    dp, ty, tx = lax.axis_index("dp"), lax.axis_index("ty"), lax.axis_index("tx")
    core, xx, place = dp % 2, dp // 2, ty * 4 + tx
    core_mate, x_mate = dp + 1 - 2 * core, dp + 2 - 4 * xx
    faces, rows, cols = x_in.shape[0], x_in.shape[1], x_in.shape[2]
    area = rows * cols
    is_mid = jnp.where((tx == 0) | (tx == 3), 0, 1)
    hx = jnp.where(tx >= 2, 1, 0)
    kk = ty + 2 * hx
    mm = kk + 4 * is_mid
    at_end = is_mid == 0

    def dev(y, x):
        return {"ty": y, "tx": x}

    def rows16(start, size):
        return pl.ds(pl.multiple_of(start, 16), size)

    def home(m):
        half = (m // 2) % 2
        return m % 2, (3 * half if m // 4 == 0 else 1 + half)

    def home_class(k):
        half = k // 2
        return k % 2, jnp.where(at_end, 3 * half, 1 + half)

    def flip48(flag, k, n):
        return 48 * jnp.where(flag, n - 1 - k, k)

    def maybe(cond, call):
        if cond is None:
            call()
        else:
            pl.when(cond)(call)

    class Exchange:
        def __init__(self, index):
            self.index = index
            self.ed_v, self.ed_h, self.db, self.sb, self.rg_v, self.rg_h, self.rg_c, self.xw, self.xd = bufs[index]

        def copies(self, sends, first_slot):
            for n, (cond, src, dst, rs, target) in enumerate(sends):
                yield cond, pltpu.make_async_remote_copy(
                    src_ref=src, dst_ref=dst, send_sem=ssem.at[self.index, first_slot + n],
                    recv_sem=rsem.at[self.index, rs], device_id=target, device_id_type=pl.DeviceIdType.MESH,
                )

        def start(self):
            for cond, copy in self.copies(self.first_sends(), 0):
                maybe(cond, copy.start)
            self.first_moves()

        def middle(self):
            self.relay()
            for cond, copy in self.copies(self.second_sends(), 24):
                maybe(cond, copy.start)
            self.second_moves()

        def drain(self):
            for cond, copy in self.copies(self.first_sends(), 0):
                maybe(cond, copy.wait_send)
            for cond, copy in self.copies(self.second_sends(), 24):
                maybe(cond, copy.wait_send)

        def get(self, cond, dst, rs):
            copy = pltpu.make_async_remote_copy(
                src_ref=dst, dst_ref=dst, send_sem=ssem.at[self.index, 0],
                recv_sem=rsem.at[self.index, rs], device_id=dev(1 - ty, tx), device_id_type=pl.DeviceIdType.MESH,
            )
            maybe(cond, copy.wait_recv)

        def move(self, cond, dst, dst_at, src, src_at):
            @pl.when(cond)
            def _():
                dst[dst_at] = src[src_at]

    class Forward(Exchange):
        def row_pieces(self):
            to = rows16((2 * ty) * 96 + hx * 48, 48)
            for k in range(4):
                yield k, rows16(flip48(hx == 1, k, 4), 48), to

        def column_pieces(self):
            to = rows16(jnp.where(hx == 1, 1, 3) * 96 + ty * 48, 48)
            for m in range(8):
                yield m, rows16(flip48(ty == 1, m, 8), 48), to

        def first_sends(self):
            ed_v, ed_h, db, rg_v, rg_h, rg_c = self.ed_v, self.ed_h, self.db, self.rg_v, self.rg_h, self.rg_c
            for k, at, to in self.row_pieces():
                yield kk != k, ed_v.at[ty, at], db.at[to], (2 * ty) * 2 + hx, dev(*home_class(k))
            for m, at, to in self.column_pieces():
                yield at_end & (mm != m), ed_h.at[hx, at], db.at[to], jnp.where(hx == 1, 2, 6) + ty, dev(*home(m))
            yield None, ed_v.at[1 - ty], rg_v.at[ty], 24, dev(1 - ty, tx)
            yield tx < 3, ed_h.at[1], rg_h.at[0], 25, dev(ty, tx + 1)
            yield tx > 0, ed_h.at[0], rg_h.at[1], 26, dev(ty, tx - 1)
            yield tx < 3, ed_v.at[1 - ty, pl.ds(176, 16)], rg_c.at[2 * ty], 20 + 2 * ty, dev(1 - ty, tx + 1)
            yield tx > 0, ed_v.at[1 - ty, pl.ds(0, 16)], rg_c.at[2 * ty + 1], 21 + 2 * ty, dev(1 - ty, tx - 1)

        def first_moves(self):
            for k, at, to in self.row_pieces():
                self.move(kk == k, self.db, (to,), self.ed_v, (ty, at))
            for m, at, to in self.column_pieces():
                self.move(at_end & (mm == m), self.db, (to,), self.ed_h, (hx, at))

        def relay(self):
            db, sb = self.db, self.sb
            for t in range(4):
                for h in range(2):
                    if t % 2 == 0:
                        own = (ty == t // 2) & (hx == h)
                    else:
                        own = at_end & (ty == h) & (tx == (0 if t == 3 else 3))
                    self.get(jnp.logical_not(own), db.at[pl.ds(t * 96 + h * 48, 48)], t * 2 + h)
            sb[...] = dot_tn(sel_t[...], db[...]).astype(bf)

        def out_rows(self):
            for y in range(2):
                for h in range(2):
                    x = jnp.where(at_end, 3 * h, 1 + h)
                    own = (ty == y) & (tx == x)
                    yield own, y, x, pl.ds(2 * y * 96 + h * 48, 48), rows16(48 * ((3 - kk) if h else kk), 48)

        def out_columns(self):
            for y in range(2):
                for h in range(2):
                    own = (ty == y) & (tx == 3 * h)
                    at = pl.ds((1 if h else 3) * 96 + y * 48, 48)
                    yield own, y, h, at, rows16(48 * ((7 - mm) if y else mm), 48)

        def out_corners(self):
            for y in range(2):
                for m, x, right, at in ((3, 1, 0, 32), (3, 2, 1, 48), (4, 3, 0, 80), (4, 0, 1, 0), (7, 2, 0, 32), (7, 1, 1, 48)):
                    yield m, y, x, 2 * y + right, pl.ds(2 * y * 96 + at, 16)
                for h in range(2):
                    yield 7, y, 3 * h, 2 * (1 - y) + h, pl.ds((1 if h else 3) * 96 + (32 if y else 48), 16)

        def second_sends(self):
            sb = self.sb
            for own, y, x, at, to in self.out_rows():
                yield jnp.logical_not(own), sb.at[at], self.rg_v.at[y, to], 8 + kk, dev(y, x)
            for own, y, h, at, to in self.out_columns():
                yield jnp.logical_not(own), sb.at[at], self.rg_h.at[h, to], 12 + mm, dev(y, 3 * h)
            for m, y, x, spot, at in self.out_corners():
                if home(m) != (y, x):
                    yield mm == m, sb.at[at], self.rg_c.at[spot], 20 + spot, dev(y, x)

        def second_moves(self):
            for own, y, x, at, to in self.out_rows():
                self.move(own, self.rg_v, (y, to), self.sb, (at,))
            for own, y, h, at, to in self.out_columns():
                self.move(own, self.rg_h, (h, to), self.sb, (at,))
            for m, y, x, spot, at in self.out_corners():
                if home(m) == (y, x):
                    self.move(mm == m, self.rg_c, (spot,), self.sb, (at,))

        def finish(self):
            self.get(None, self.rg_v.at[1 - ty], 24)
            self.get(tx > 0, self.rg_h.at[0], 25)
            self.get(tx < 3, self.rg_h.at[1], 26)
            for k in range(4):
                self.get(kk != k, self.rg_v.at[ty, rows16(flip48(hx == 1, k, 4), 48)], 8 + k)
            for m in range(8):
                self.get(at_end & (mm != m), self.rg_h.at[hx, rows16(flip48(ty == 1, m, 8), 48)], 12 + m)
            for spot in range(4):
                y, right = spot // 2, spot % 2
                face_corner = (ty == y) & (tx == 3 * right)
                if spot == 2:
                    own = (ty == 1) & (tx == 2)
                    skip = face_corner | own
                else:
                    skip = face_corner
                self.get(jnp.logical_not(skip), self.rg_c.at[spot], 20 + spot)

    class Backward(Exchange):
        row_pieces, column_pieces = Forward.row_pieces, Forward.column_pieces
        out_rows, out_columns = Forward.out_rows, Forward.out_columns

        def corners(self):
            for right in range(2):
                away = (tx < 3) if right else (tx > 0)
                if right:
                    x, y = jnp.where(tx == 0, 1, jnp.where(tx == 1, 2, 3)), jnp.where(tx == 0, 0, 1)
                else:
                    x, y = jnp.where(tx == 1, 3, jnp.where(tx == 2, 2, 1)), jnp.where(tx == 3, 0, 1)
                own = away & (ty == y) & (tx == x)
                yield right, away, own, x, y, 2 * ty + right

        def first_sends(self):
            rg_v, rg_h, rg_c, sb, xw, xd = self.rg_v, self.rg_h, self.rg_c, self.sb, self.xw, self.xd
            for k, at, to in self.row_pieces():
                yield kk != k, rg_v.at[ty, at], sb.at[to], (2 * ty) * 2 + hx, dev(*home_class(k))
            for m, at, to in self.column_pieces():
                yield at_end & (mm != m), rg_h.at[hx, at], sb.at[to], jnp.where(hx == 1, 2, 6) + ty, dev(*home(m))
            for right, away, own, x, y, slot in self.corners():
                yield away & jnp.logical_not(own), rg_c.at[slot], xw.at[slot], 8 + slot, dev(y, x)
                inner = 2 * (1 - ty) + right
                edge = (tx == 3) if right else (tx == 0)
                yield edge, rg_c.at[inner], xw.at[4 + slot], 12 + slot, dev(1, 2)
                yield away, rg_c.at[inner], xd.at[1 - right], 17 - right, dev(1 - ty, tx + (1 if right else -1))
            ed_v, ed_h = self.ed_v, self.ed_h
            yield None, rg_v.at[1 - ty], ed_v.at[ty], 30, dev(1 - ty, tx)
            yield tx < 3, rg_h.at[1], ed_h.at[0], 31, dev(ty, tx + 1)
            yield tx > 0, rg_h.at[0], ed_h.at[1], 32, dev(ty, tx - 1)

        def first_moves(self):
            for k, at, to in self.row_pieces():
                self.move(kk == k, self.sb, (to,), self.rg_v, (ty, at))
            for m, at, to in self.column_pieces():
                self.move(at_end & (mm == m), self.sb, (to,), self.rg_h, (hx, at))
            for right, away, own, x, y, slot in self.corners():
                self.move(own, self.xw, (slot,), self.rg_c, (slot,))

        def relay(self):
            sb, db, xw = self.sb, self.db, self.xw
            for s in range(4):
                for h in range(2):
                    if s % 2 == 0:
                        own = (ty == s // 2) & (hx == h)
                    else:
                        own = at_end & (ty == h) & (tx == (0 if s == 3 else 3))
                    self.get(jnp.logical_not(own), sb.at[pl.ds(s * 96 + h * 48, 48)], s * 2 + h)
            for y in range(2):
                for right in range(2):
                    slot = 2 * y + right
                    wants = (mm == 3) | (mm == 4) | (mm == 7)
                    if slot == 2:
                        wants = (mm == 3) | (mm == 4)
                    self.get(wants, xw.at[slot], 8 + slot)
                    self.get(mm == 7, xw.at[4 + slot], 12 + slot)
                    for m, at in ((3, 48 if right else 32), (4, 0 if right else 80), (7, 48 if right else 32)):
                        @pl.when(mm == m)
                        def _(spot=2 * y * 96 + at, slot=slot):
                            here = pl.ds(spot, 16)
                            sb[here] = (sb[here].astype(f32) + xw[slot].astype(f32)).astype(bf)

                    @pl.when(mm == 7)
                    def _(spot=(1 if right else 3) * 96 + (32 if y else 48), slot=4 + slot):
                        here = pl.ds(spot, 16)
                        sb[here] = (sb[here].astype(f32) + xw[slot].astype(f32)).astype(bf)
            db[...] = dot(sel_t[...], sb[...]).astype(bf)

        def second_sends(self):
            for own, y, x, at, to in self.out_rows():
                yield jnp.logical_not(own), self.db.at[at], self.ed_v.at[y, to], 18 + kk, dev(y, x)
            for own, y, h, at, to in self.out_columns():
                yield jnp.logical_not(own), self.db.at[at], self.ed_h.at[h, to], 22 + mm, dev(y, 3 * h)

        def second_moves(self):
            for own, y, x, at, to in self.out_rows():
                self.move(own, self.ed_v, (y, to), self.db, (at,))
            for own, y, h, at, to in self.out_columns():
                self.move(own, self.ed_h, (h, to), self.db, (at,))

        def finish(self):
            self.get(None, self.ed_v.at[1 - ty], 30)
            self.get(tx > 0, self.ed_h.at[0], 31)
            self.get(tx < 3, self.ed_h.at[1], 32)
            self.get(tx > 0, self.xd.at[0], 16)
            self.get(tx < 3, self.xd.at[1], 17)
            for k in range(4):
                self.get(kk != k, self.ed_v.at[ty, rows16(flip48(hx == 1, k, 4), 48)], 18 + k)
            for m in range(8):
                self.get(at_end & (mm != m), self.ed_h.at[hx, rows16(flip48(ty == 1, m, 8), 48)], 22 + m)

        def stage(self, blocks):
            for j in range(blocks):
                lanes = slice(128 * j, 128 * j + 128)
                for s in range(2):
                    evf[j, s] = self.ed_v[s, :, lanes].astype(f32)
                    ehf[j, s] = self.ed_h[s, :, lanes].astype(f32)

                @pl.when(tx > 0)
                def _(j=j, lanes=lanes):
                    evf[j, 1 - ty, pl.ds(0, 16)] += self.xd[0, :, lanes].astype(f32)

                @pl.when(tx < 3)
                def _(j=j, lanes=lanes):
                    evf[j, 1 - ty, pl.ds(176, 16)] += self.xd[1, :, lanes].astype(f32)

    class Total:
        def __init__(self, index, acc, acc0, out, out0, land, land0, count, order):
            self.index, self.acc, self.out, self.land = index, acc, out, land
            self.acc0, self.out0, self.land0, self.count = acc0, out0, land0, count
            axes = {
                "core": (2, core, lambda k: {"dp": core_mate}),
                "x": (2, xx, lambda k: {"dp": x_mate}),
                "y": (2, ty, lambda k: {"ty": 1 - ty}),
                "z": (4, tx, lambda k: {"tx": k}),
                "yz": (8, place, lambda k: {"ty": k // 4, "tx": k % 4}),
            }
            self.stages = []
            start, size, land_at, sem = 0, count, 0, 0
            for name in order:
                n, me, target = axes[name]
                chunk = size // n
                self.stages.append((n, me, target, start, chunk, land_at, sem))
                land_at += chunk * (1 if n == 2 else n)
                sem += 1 if n == 2 else n
                start, size = start + me * chunk, chunk
            self.unit, self.sems, self.last = size, sem, len(order) - 1
            self.near = []
            for n, me, *_ in self.stages:
                if n == 2:
                    self.near.append([(1 - me, None, 0, 0)])
                else:
                    self.near.append([(k, me != k, k, me) for k in range(n)])

        def at(self, base, start, size):
            return rows16(base + start, size)

        def copy(self, src, dst, slot, rslot, target):
            return pltpu.make_async_remote_copy(
                src_ref=src, dst_ref=dst, send_sem=sum_ssem.at[self.index, slot],
                recv_sem=sum_rsem.at[self.index, rslot], device_id=target, device_id_type=pl.DeviceIdType.MESH,
            )

        def rs_copy(self, s, k, mine, theirs):
            n, me, target, start, chunk, land_at, sem = self.stages[s]
            return self.copy(
                self.out.at[self.at(self.out0, start + k * chunk, chunk)],
                self.land.at[self.at(self.land0, land_at + chunk * theirs, chunk)],
                sem + mine, sem + theirs, target(k))

        def send_rs(self, s):
            n, me, target, start, chunk, land_at, sem = self.stages[s]
            for k, cond, mine, theirs in self.near[s]:
                def go(k=k, mine=mine, theirs=theirs):
                    self.cast(start + k * chunk, chunk)
                    self.rs_copy(s, k, mine, theirs).start()
                maybe(cond, go)

        def recv_rs(self, s):
            n, me, target, start, chunk, land_at, sem = self.stages[s]
            for k, cond, mine, theirs in self.near[s]:
                def get(k=k, mine=mine):
                    here = self.land.at[self.at(self.land0, land_at + chunk * mine, chunk)]
                    self.copy(here, here, sem + mine, sem + mine, target(k)).wait_recv()

                    @pl.loop(0, chunk // self.unit)
                    def _(i):
                        self.acc[self.at(self.acc0, start + me * chunk + i * self.unit, self.unit)] += self.land[
                            self.at(self.land0, land_at + chunk * mine + i * self.unit, self.unit)].astype(f32)

                maybe(cond, get)

        def done_rs(self, s):
            target = self.stages[s][2]
            for k, cond, mine, theirs in self.near[s]:
                def done(k=k, mine=mine, theirs=theirs):
                    self.rs_copy(s, k, mine, theirs).wait_send()
                    pl.semaphore_signal(
                        ack.at[self.index, s], inc=1, device_id=target(k), device_id_type=pl.DeviceIdType.MESH)
                maybe(cond, done)

        def ag_copy(self, s, k, mine, theirs):
            n, me, target, start, chunk, land_at, sem = self.stages[s]
            here = self.out.at[self.at(self.out0, start + me * chunk, chunk)]
            return self.copy(here, here, self.sems + sem + mine, self.sems + sem + theirs, target(k))

        def send_ag(self, s):
            pl.semaphore_wait(ack.at[self.index, s], self.stages[s][0] - 1)
            for k, cond, mine, theirs in self.near[s]:
                maybe(cond, lambda k=k, mine=mine, theirs=theirs: self.ag_copy(s, k, mine, theirs).start())

        def recv_ag(self, s):
            n, me, target, start, chunk, land_at, sem = self.stages[s]
            for k, cond, mine, theirs in self.near[s]:
                def get(k=k, mine=mine):
                    here = self.out.at[self.at(self.out0, start + k * chunk, chunk)]
                    slot = self.sems + sem + mine
                    self.copy(here, here, slot, slot, target(k)).wait_recv()
                maybe(cond, get)

        def cast(self, start, size):
            @pl.loop(0, size // self.unit)
            def _(i):
                at = start + i * self.unit
                self.out[self.at(self.out0, at, self.unit)] = self.acc[self.at(self.acc0, at, self.unit)].astype(bf)

        def step(self, k):
            last = self.last
            if k == 0:
                self.send_rs(0)
            elif k <= last:
                self.recv_rs(k - 1)
                self.send_rs(k)
                self.done_rs(k - 1)
            elif k == last + 1:
                self.recv_rs(last)
                n, me, target, start, chunk, land_at, sem = self.stages[last]
                self.cast(start + me * chunk, chunk)
                self.done_rs(last)
                self.send_ag(last)
            elif k <= 2 * last + 1:
                self.recv_ag(2 * last + 2 - k)
                self.send_ag(2 * last + 1 - k)
            else:
                self.recv_ag(0)
                for s in range(last + 1):
                    for k, cond, mine, theirs in self.near[s]:
                        maybe(cond, lambda s=s, k=k, mine=mine, theirs=theirs: self.ag_copy(s, k, mine, theirs).wait_send())

    def sums(where, at=None):
        for (spot, spot_at), steps in SUM_PLAN.items():
            if spot == where:
                def go(steps=steps):
                    for name, k in steps:
                        totals[name].step(k)
                if at is None:
                    go()
                else:
                    pl.when(at == spot_at)(go)

    def dot(a, b):
        return jnp.dot(a, b, preferred_element_type=f32)

    def dot_nt(a, b):
        return lax.dot_general(a, b, (((1,), (1,)), ((), ())), preferred_element_type=f32)

    def dot_tn(a, b):
        return lax.dot_general(a, b, (((0,), (0,)), ((), ())), preferred_element_type=f32)

    def cat(parts, axis=-1):
        return jnp.concatenate(parts, axis=axis)

    def face_rows(f):
        return pl.ds(pl.multiple_of(f * area, area), area)

    def top(f, s):
        return pl.ds(f * area + (area - cols if s else 0), cols)

    def side(f, s):
        return pl.ds(f * area + (cols - 1 if s else 0), rows, stride=cols)

    def ring_v(f):
        return pl.ds(f, cols, stride=faces)

    def ring_h(f):
        return pl.ds(f, rows, stride=faces)

    def shifts(v):
        zero = jnp.zeros((rows, 1, v.shape[-1]), v.dtype)
        return cat([zero, v[:, : cols - 1]], 1), cat([v[:, 1:], zero], 1)

    def fill(ref, v):
        left, right = shifts(v)
        wide = v.shape[-1]
        ref[1 : rows + 1, :, 0:wide] = left
        ref[1 : rows + 1, :, wide : 2 * wide] = v
        ref[1 : rows + 1, :, 2 * wide : 3 * wide] = right

    def windows(ref):
        return [ref[a : a + rows].reshape(area, ref.shape[-1]) for a in range(3)]

    def split(ref, at, v):
        for h in range(2):
            ref[(h,) + at] = v[:, 128 * h : 128 * h + 128]

    def join(ref, at, blocks=2):
        return cat([ref[(h,) + at] for h in range(blocks)])

    def gelu_slope(u):
        phi = 0.5 + 0.5 * lax.erf(u * 0.7071067811865476)
        return u * phi, phi + u * (0.3989422804014327 * jnp.exp(-0.5 * u * u))

    lane = lax.broadcasted_iota(jnp.int32, (1, LANES), 1)

    first, second = Forward(0), Forward(1)
    third, fourth = Backward(2), Backward(3)
    def load(src, dst, sem):
        copy = pltpu.make_async_copy(src, dst, lsem.at[sem])
        copy.start()
        return copy

    eload, hotload, xload = load(ext_in, ev, 1), load(hot_in, slope.at[0:1152], 11), load(x_in, xv, 0)
    w1load, skipload = load(w1_in, w1, 5), load(skip_in, wskip, 6)
    cload, w2load = load(cot_in, cv, 2), load(w2_in, w2, 7)
    barrier = pltpu.get_barrier_semaphore()
    for e in (0, 1):
        bufs[e][6][...] = jnp.zeros_like(bufs[e][6])
    for y in range(2):
        for x in range(4):
            @pl.when((ty != y) | (tx != x))
            def _(y=y, x=x):
                pl.semaphore_signal(barrier, inc=1, device_id=dev(y, x), device_id_type=pl.DeviceIdType.MESH)
    for mate in (core_mate, x_mate):
        pl.semaphore_signal(barrier, inc=1, device_id={"dp": mate}, device_id_type=pl.DeviceIdType.MESH)
    pl.semaphore_wait(barrier, 9)

    for ref in (xc[0], xc[1]):
        ref[0] = jnp.zeros(ref.shape[1:], bf)
        ref[rows + 1] = jnp.zeros(ref.shape[1:], bf)

    @pl.loop(0, faces)
    def _(f):
        hc[f, 0] = jnp.zeros(hc.shape[2:], bf)
        hc[f, rows + 1] = jnp.zeros(hc.shape[2:], bf)
        t27[f, 0] = jnp.zeros(t27.shape[2:], bf)
        t27[f, rows + 1] = jnp.zeros(t27.shape[2:], bf)

    eload.wait()
    turned = cat([ev[f].astype(f32).reshape(9 * cols, rows).T for f in range(faces)], 0).astype(bf)
    hotload.wait()
    for k in range(8):
        flat = dot(turned, slope[144 * k : 144 * k + 144])
        for c in range(2):
            pre[0, pl.ds((2 * k + c) * faces * rows, faces * rows)] = flat[:, c * LANES : c * LANES + LANES]
    xload.wait()

    @pl.loop(0, faces)
    def _(f):
        for c in range(cols):
            ff[2, pl.ds(c, rows, stride=cols)] = pre[0, pl.ds(c * faces * rows + f * rows, rows)]
        packed = ff[2] + jnp.where(lane == ONE, 1.0, 0.0)
        t27[f, 1 : rows + 1] = packed.astype(bf).reshape(rows, cols, LANES)
        ff[2] = jnp.where(lane < 9, pltpu.roll(packed, LANES - 9, axis=1), 0.0)
        for h in range(2):
            ff[h] = xv[f, :, :, 128 * h : 128 * h + 128].astype(f32).reshape(area, LANES)
        for j in range(3):
            for s in range(2):
                evf[j, s, ring_v(f)] = ff[j, pl.ds(area - cols if s else 0, cols)]
                ehf[j, s, ring_h(f)] = ff[j, pl.ds(cols - 1 if s else 0, rows, stride=cols)]

    def edges_out(ex, blocks):
        for s in range(2):
            ex.ed_v[s] = join(evf, (s,), blocks).astype(bf)
            ex.ed_h[s] = join(ehf, (s,), blocks).astype(bf)

    edges_out(first, 3)
    first.start()

    acca[...] = jnp.zeros_like(acca)
    accb[...] = jnp.zeros_like(accb)
    w1load.wait()
    skipload.wait()
    ff[...] = jnp.zeros_like(ff)
    for h in range(2):
        lanes = slice(128 * h, 128 * h + 128)
        for a in range(3):
            for b in range(3):
                ff[h, pl.ds(128 * a + 9 * b, 9)] = w1[3 * a + b, 256:265, lanes].astype(f32)
        ff[h, pl.ds(128 + ONE, 1)] = bias_one[...].astype(f32).reshape(1, 256)[:, lanes]
        ff[h, pl.ds(384 + 9, 9)] = wskip[256:265, lanes].astype(f32)
        ff[h, pl.ds(384 + ONE, 1)] = bias_skip[...].astype(f32).reshape(1, 256)[:, lanes]
        for a in range(3):
            we[a, :, lanes] = ff[h, pl.ds(128 * a, 128)].astype(bf)
        wse[:, lanes] = ff[h, pl.ds(384, 128)].astype(bf)
        ff[h, pl.ds(0, 256)] = jnp.zeros((256, LANES), f32)
        for t in range(TAPS):
            ff[h, pl.ds(9 * t, 9)] = w1[t, 256:265, lanes].astype(f32)
        ff[h, pl.ds(128 + 36, 9)] = wskip[256:265, lanes].astype(f32)
        for k in range(2):
            we81[k, :, lanes] = ff[h, pl.ds(128 * k, 128)].astype(bf)
    total = 32 * faces
    spread = jnp.where(
        lax.broadcasted_iota(jnp.int32, (faces, total), 1) % faces
        == lax.broadcasted_iota(jnp.int32, (faces, total), 0), 1.0, 0.0)
    spot = lax.broadcasted_iota(jnp.int32, (1, total), 1)
    side_of, step_of = spot // (8 * faces), (spot // faces % 8).astype(f32)
    source = jnp.zeros((1, total), f32)
    for s in range(4):
        entry = dot(table[s].astype(f32), spread)
        step = jnp.where(entry[2:3] > 0.5, 7.0 - step_of, step_of)
        source = source + jnp.where(side_of == s, (entry[1:2] * 8.0 + step) * faces + entry[0:1], 0.0)
    sel_t[...] = jnp.where(
        lax.broadcasted_iota(jnp.int32, (total, total), 0) == source.astype(jnp.int32), 1.0, 0.0).astype(bf)
    same = jnp.where(
        lax.broadcasted_iota(jnp.int32, (faces, faces), 1) == lax.broadcasted_iota(jnp.int32, (faces, faces), 0), 1.0, 0.0)
    for spot_index, k in enumerate((0, 1, 3, 2)):
        column = jnp.sum(same * table[k, 3:4].astype(f32), axis=1, keepdims=True)
        rule[spot_index, 0:faces] = jnp.broadcast_to(1.0 - column, (faces, LANES))

    def ring_in(ex, blocks):
        for j in range(blocks):
            lanes = slice(128 * j, 128 * j + 128)
            for s in range(2):
                rvf[j, s, pl.ds(12, 192)] = ex.rg_v[s, :, lanes].astype(f32)
                rhf[j, s, pl.ds(12, 384)] = ex.rg_h[s, :, lanes].astype(f32)
            for spot in range(4):
                s, right = spot // 2, spot % 2
                win = ex.rg_c[spot, :, lanes].astype(f32)
                edge = (tx == 3) if right else (tx == 0)
                late = jnp.where(edge, ty == 1, right == 0)
                got = jnp.where(late, win[4:16], win[0:12])
                from_v = rvf[j, s, pl.ds(192 if right else 12, 12)]
                from_h = rhf[j, right, pl.ds(384 if s else 12, 12)]
                local = jnp.where(rule[spot, 0:12] > 0.0, from_v, from_h)
                rvf[j, s, pl.ds(204 if right else 0, 12)] = jnp.where((ty == s) & edge, local, got)

    def ring_cat(rcv, rch, blocks):
        for s in range(2):
            for b in range(3):
                for j in range(2):
                    at = slice(256 * b + 128 * j, 256 * b + 128 * j + 128)
                    rcv[s, :, at] = rvf[j, s, pl.ds(12 * b, 192)].astype(bf)
                    rch[s, :, at] = rhf[j, s, pl.ds(12 * b, 384)].astype(bf)
            if blocks == 3:
                total = rvf[2, s, pl.ds(0, 192)]
                for b in (1, 2):
                    total = total + pltpu.roll(rvf[2, s, pl.ds(12 * b, 192)], 9 * b, axis=1)
                rcv[s, :, 768:896] = total.astype(bf)
                for a in range(3):
                    line = rhf[2, s, pl.ds(12 * a, 384)]
                    line = pltpu.roll(line, 18, axis=1) if s else line
                    rch[s, :, 768 + 128 * a : 896 + 128 * a] = line.astype(bf)

    def zero_h_ends(blocks):
        for j in range(blocks):
            for s in range(2):
                rhf[j, s, pl.ds(0, 12)] = jnp.zeros((12, LANES), f32)
                rhf[j, s, pl.ds(396, 12)] = jnp.zeros((12, LANES), f32)

    zero_h_ends(3)

    def add_to_edges(source_v, source_h):
        @pl.loop(0, faces)
        def _(f):
            for h in range(2):
                for s in range(2):
                    pre[h, top(f, s)] += source_v[h, s, ring_v(f)]
            for h in range(2):
                for s in range(2):
                    pre[h, side(f, s)] += source_h[h, s, ring_h(f)]
            for h in range(2):
                for s in range(2):
                    evf[h, s, ring_v(f)] = pre[h, top(f, s)]
                    ehf[h, s, ring_h(f)] = pre[h, side(f, s)]

    def w_first(t):
        return w1[t, 0:256]

    def conv_first(f, ref):
        lhs = cat(windows(ref) + windows(t27.at[f]))
        rhs = cat([w_first(t) for t in range(TAPS)] + [we[a] for a in range(3)], 0)
        split(pre, (face_rows(f),), dot(lhs, rhs))

    def first_part():
        @pl.loop(0, faces // 2)
        def _(i):
            pl.when(i == 2)(first.middle)
            for u in range(2):
                fill(xc[u], xv[2 * i + u])
            for u in range(2):
                conv_first(2 * i + u, xc[u])

    cload.wait()

    @pl.loop(0, faces // 2)
    def _(i):
        pair = [2 * i, 2 * i + 1]
        field = cat([cat([xv[f].reshape(area, 256), t27[f, 1 : rows + 1].reshape(area, LANES)]) for f in pair], 0)
        fresh = dot_tn(field, cat([cv[f] for f in pair], 0))
        acca[2304:2560] += fresh[0:256]
        accb[864:896] += fresh[256:288]

    @pl.loop(0, faces)
    def _(f):
        for h in range(2):
            ff[h] = cv[f, :, 128 * h : 128 * h + 128].astype(f32)
            for s in range(2):
                cvf[h, s, ring_v(f)] = ff[h, pl.ds(area - cols if s else 0, cols)]
                chf[h, s, ring_h(f)] = ff[h, pl.ds(cols - 1 if s else 0, rows, stride=cols)]

    for s in range(2):
        cev[s] = join(cvf, (s,)).astype(bf)
        ceh[s] = join(chf, (s,)).astype(bf)
    first_part()
    first.finish()
    ring_in(first, 3)
    ring_cat(rc1v, rc1h, 3)
    for s in range(2):
        rhs = cat([w_first(6 * s + b) for b in range(3)] + [we[2 * s]], 0)
        split(cvf, (s,), dot(rc1v[s], rhs))
        rhs = cat([w_first(3 * a + 2 * s) for a in range(3)] + [we[a] for a in range(3)], 0)
        split(chf, (s,), dot(rc1h[s], rhs))
    add_to_edges(cvf, chf)
    for h in range(2):
        for s in range(2):
            evf[h, s], slev[h, s] = gelu_slope(evf[h, s])
            ehf[h, s], sleh[h, s] = gelu_slope(ehf[h, s])
    edges_out(second, 2)
    second.start()

    def conv_second(f):
        lhs = cat(windows(hc.at[f]))
        rhs = cat([w2[t] for t in range(TAPS)], 0)
        split(pre, (face_rows(f),), dot(lhs, rhs))

    def second_part():
        @pl.loop(0, faces // 2)
        def _(i):
            pl.when(i == 3)(second.middle)
            for u in range(2):
                f = 2 * i + u
                act, sl = gelu_slope(join(pre, (face_rows(f),)))
                slope[face_rows(f)] = sl.astype(bf)
                fill(hc.at[f], act.astype(bf).reshape(rows, cols, 256))
            for u in range(2):
                conv_second(2 * i + u)

    w2load.wait()
    second_part()
    second.finish()
    ring_in(second, 2)
    ring_cat(rc2v, rc2h, 2)
    for s in range(2):
        split(cvf, (s,), dot(rc2v[s], cat([w2[6 * s + b] for b in range(3)], 0)))
        split(chf, (s,), dot(rc2h[s], cat([w2[3 * a + 2 * s] for a in range(3)], 0)))
    add_to_edges(cvf, chf)

    def ring_grads(ex, taps, blocks):
        for s in range(2):
            lhs = cat([cat([rvf[j, s, pl.ds(12 * b, 216)] for j in range(2)]).astype(bf) for b in range(3)])
            base = 0 if s else 6
            rhs = cat([taps(8 - (base + b)) for b in range(3)], 1)
            out = dot_nt(lhs, rhs)
            if blocks == 3:
                mid = dot_nt(gev[s], we[2 * s])
                pad = jnp.zeros((24, LANES), f32)
                mid = cat([pad, mid, pad], 0)
                tail = mid[24:240]
                for b in (1, 2):
                    tail = tail + pltpu.roll(mid[24 - 12 * b : 240 - 12 * b], LANES - 9 * b, axis=1)
                out = cat([out, jnp.where(lane < 9, tail, 0.0)])
            for j in range(blocks):
                cvf[j, s] = out[12:204, 128 * j : 128 * j + 128]
                ff[j, pl.ds(256 * s, 12)] = out[0:12, 128 * j : 128 * j + 128]
                ff[j, pl.ds(256 * s + 128, 12)] = out[204:216, 128 * j : 128 * j + 128]
            lhs = cat([cat([rhf[j, s, pl.ds(12 * a, 384)] for j in range(2)]).astype(bf) for a in range(3)])
            base = 0 if s else 2
            rhs = cat([taps(8 - (base + 3 * a)) for a in range(3)], 1)
            out = dot_nt(lhs, rhs)
            if blocks == 3:
                tail = dot_nt(lhs, cat([we[2 - a] for a in range(3)], 1))
                tail = pltpu.roll(tail, LANES - 18, axis=1) if s else tail
                out = cat([out, jnp.where(lane < 9, tail, 0.0)])
            for j in range(blocks):
                chf[j, s] = out[:, 128 * j : 128 * j + 128]
        for j in range(blocks):
            lanes = slice(128 * j, 128 * j + 128)
            for spot in range(4):
                s, right = spot // 2, spot % 2
                v = ff[j, pl.ds(256 * s + 128 * right, 12)]
                edge = (tx == 3) if right else (tx == 0)
                late = jnp.where(edge, ty == 1, right == 0)
                zero = jnp.zeros((4, LANES), f32)
                ex.rg_c[spot, :, lanes] = jnp.where(late, cat([zero, v], 0), cat([v, zero], 0)).astype(bf)

                @pl.when((ty == s) & edge)
                def _(j=j, s=s, right=right, spot=spot, v=v):
                    take = rule[spot, 0:12] > 0.0
                    cvf[j, s, pl.ds(180 if right else 0, 12)] += jnp.where(take, v, 0.0)
                    chf[j, right, pl.ds(372 if s else 0, 12)] += jnp.where(take, 0.0, v)
        for s in range(2):
            ex.rg_v[s] = join(cvf, (s,), blocks).astype(bf)
            ex.rg_h[s] = join(chf, (s,), blocks).astype(bf)

    def edge_grads(make_v, make_h):
        for s in range(2):
            for h in range(2):
                lanes = slice(128 * h, 128 * h + 128)
                v = make_v(h, s).astype(bf)
                gev[s, :, lanes] = v
                rvf[h, s, pl.ds(0, 24)] = jnp.zeros((24, LANES), f32)
                rvf[h, s, pl.ds(216, 24)] = jnp.zeros((24, LANES), f32)
                rvf[h, s, pl.ds(24, 192)] = v.astype(f32)
                v = make_h(h, s).astype(bf)
                geh[s, :, lanes] = v
                rhf[h, s, pl.ds(12, 384)] = v.astype(f32)

    def slope_two(u, h):
        return gelu_slope(u + bias_two[...].astype(f32).reshape(1, 256)[:, 128 * h : 128 * h + 128])[1]

    edge_grads(
        lambda h, s: slope_two(evf[h, s], h) * cev[s, :, 128 * h : 128 * h + 128].astype(f32),
        lambda h, s: slope_two(ehf[h, s], h) * ceh[s, :, 128 * h : 128 * h + 128].astype(f32),
    )
    ring_grads(third, lambda t: w2[t], 2)
    third.start()

    def out_copy(f):
        return pltpu.make_async_copy(hc.at[f, pl.ds(1, rows), :, pl.ds(0, 256)], out_ref.at[f], lsem.at[3])

    def gx_copy(f):
        return pltpu.make_async_copy(hc.at[f, pl.ds(1, rows), :, pl.ds(512, 256)], gx_ref.at[f], lsem.at[4])

    def second_bias():
        return bias_two[...].astype(f32).reshape(1, 256)

    def third_part():
        @pl.loop(0, faces // 2)
        def _(i):
            pl.when(i == 4)(third.middle)
            grads = []
            for u in range(2):
                f = 2 * i + u
                sl = gelu_slope(join(pre, (face_rows(f),)) + second_bias())[1]
                grad = (cv[f].astype(f32) * sl).astype(bf)
                accb[896:897] += jnp.sum(grad.astype(f32), axis=0, keepdims=True)
                grads.append(grad)
            for u in range(2):
                cv[2 * i + u] = grads[u]
            pair = cat(grads, 0)
            for a in range(3):
                field = cat([hc[2 * i + u, a : a + rows].reshape(area, 768) for u in range(2)], 0)
                acca[768 * a : 768 * a + 768] += dot_tn(field, pair)

    def output_part():
        @pl.loop(0, faces // 2)
        def _(i):
            sums("out", i)
            for u in range(2):
                f = 2 * i + u
                act = gelu_slope(join(pre, (face_rows(f),)) + second_bias())[0]
                field = cat([xv[f].reshape(area, 256), t27[f, 1 : rows + 1].reshape(area, LANES)])
                whole = (act + dot(field, cat([wskip[0:256], wse[...]], 0))).astype(bf)
                hc[f, 1 : rows + 1, :, 0:256] = whole.reshape(rows, cols, 256)
            for u in range(2):
                out_copy(2 * i + u).start()

    def third_back():
        @pl.loop(0, faces // 2)
        def _(i):
            sums("back", i)
            for u in range(2):
                fill(xc[u], cv[2 * i + u].reshape(rows, cols, 256))
            rhs = cat([w2[8 - t] for t in range(TAPS)], 1)
            for u in range(2):
                split(pre, (face_rows(2 * i + u),), dot_nt(cat(windows(xc[u])), rhs))

    def ring_kernel_grads(grad_ref, extra, rcv, rch):
        for s in range(2):
            fresh = dot_tn(rcv[s], gev[s])
            for b in range(3):
                at = BLOCKS[b] + 512 * s if extra else 1536 * s + 256 * b
                grad_ref[at : at + 256] += fresh[256 * b : 256 * b + 256]
            if extra:
                grad_ref[768 + 64 * s : 800 + 64 * s] += fresh[768:800]
            fresh = dot_tn(rch[s], geh[s])
            for a in range(3):
                at = BLOCKS[2 * s] + 256 * a if extra else 768 * a + 512 * s
                grad_ref[at : at + 256] += fresh[256 * a : 256 * a + 256]
                if extra:
                    grad_ref[768 + 32 * a : 800 + 32 * a] += fresh[768 + 128 * a : 800 + 128 * a]

    keep = load(pre, kept, 12)
    third_part()
    keep.wait()
    ring_kernel_grads(acca, False, rc2v, rc2h)
    totals = {}
    for index, (name, first_row, count, way) in enumerate(SUMS):
        if name[0] == "a":
            totals[name] = Total(index, acca, first_row, outa, first_row, landa, first_row, count, way)
        else:
            totals[name] = Total(index, accb, first_row, slope, first_row, slope, 2560 + first_row, count, way)
    sums("middle")
    third_back()
    cload = load(cot_in, cv, 2)
    third.finish()
    third.stage(2)

    @pl.loop(0, faces)
    def _(f):
        for h in range(2):
            for s in range(2):
                pre[h, top(f, s)] += evf[h, s, ring_v(f)]
        for h in range(2):
            for s in range(2):
                pre[h, side(f, s)] += ehf[h, s, ring_h(f)]
        for h in range(2):
            for s in range(2):
                evf[h, s, ring_v(f)] = pre[h, top(f, s)]
                ehf[h, s, ring_h(f)] = pre[h, side(f, s)]

    edge_grads(lambda h, s: evf[h, s] * slev[h, s], lambda h, s: ehf[h, s] * sleh[h, s])
    ring_grads(fourth, w_first, 3)
    fourth.start()
    sums("sent")

    def first_grads(f):
        grad = (join(pre, (face_rows(f),)) * slope[face_rows(f)].astype(f32)).astype(bf)
        hc[f, 1 : rows + 1, :, 256:512] = grad.reshape(rows, cols, 256)

    def shifted_grads(g, start, choose):
        for u in range(3):
            xc[0][1 : rows + 1, :, 256 * u : 256 * u + 256] = choose(xv[3 * g + u])
        grads = cat([hc[3 * g + u, 1 : rows + 1, :, 256:512].reshape(area, 256) for u in range(3)], 0)
        field = cat([
            cat([xc[0][a : a + rows, :, 256 * u : 256 * u + 256].reshape(area, 256) for a in range(3)])
            for u in range(3)], 0)
        accb[pl.ds(start, 768)] += dot_tn(field, grads)
        return grads

    def fourth_start():
        @pl.loop(0, faces // 3)
        def _(g):
            for u in range(3):
                first_grads(3 * g + u)
            grads = shifted_grads(g, 0, lambda v: shifts(v)[0])
            extra = cat([
                cat([t27[3 * g + u, a : a + rows].reshape(area, LANES) for a in range(3)]) for u in range(3)], 0)
            fresh = dot_tn(extra, grads)
            for a in range(3):
                accb[768 + 32 * a : 800 + 32 * a] += fresh[128 * a : 128 * a + 32]

    def free_slopes():
        for target in ({"dp": core_mate}, {"dp": x_mate}):
            pl.semaphore_signal(credit, inc=1, device_id=target, device_id_type=pl.DeviceIdType.MESH)
        for q in range(8):
            @pl.when(place != q)
            def _(q=q):
                pl.semaphore_signal(credit, inc=1, device_id=dev(q // 4, q % 4), device_id_type=pl.DeviceIdType.MESH)

    def fourth_rest():
        @pl.loop(0, 2 * faces // 3)
        def _(i):
            b = 1 + i // 4
            pl.when(i == 2)(fourth.middle)
            sums("more", i)
            shifted_grads(i % 4, pl.multiple_of(256 + 768 * b, 256), lambda v: jnp.where(b == 1, v, shifts(v)[1]))

    ring_kernel_grads(accb, True, rc1v, rc1h)
    fourth_start()
    free_slopes()
    pl.semaphore_wait(credit, 9)
    sums("first")
    keep = load(kept, pre, 12)
    fourth_rest()
    hot = landa.at[0:1152]
    hotload = load(hot_back_in, hot, 11)
    sums("third")
    keep.wait()
    output_part()
    fourth.finish()
    fourth.stage(3)

    def part(u, j, start=0, size=area, stride=1):
        return pl.ds((3 * u + j) * area + start, size, stride=stride)

    def last_part():
        @pl.loop(0, faces // 2)
        def _(i):
            sums("last", i)
            col = lax.broadcasted_iota(jnp.int32, (area, 1), 0) % cols
            for u in range(2):
                f = 2 * i + u
                cot = cv[f]
                rhs = cat([w_first(8 - t) for t in range(TAPS)] + [wskip[0:256]], 1)
                fill(xc[u], hc[f, 1 : rows + 1, :, 256:512])
                main = dot_nt(cat(windows(xc[u]) + [cot]), rhs)
                for h in range(2):
                    pre[0, part(u, h)] = main[:, 128 * h : 128 * h + 128]
                taps = dot_nt(cat([hc[f, 1 : rows + 1, :, 256:512].reshape(area, 256), cot]), cat([we81[0], we81[1]], 1))
                edge = jnp.zeros((cols, LANES), f32)
                lines = (
                    cat([taps[cols:], edge], 0)
                    + pltpu.roll(taps, LANES - 27, axis=1)
                    + cat([edge, pltpu.roll(taps, LANES - 54, axis=1)[: area - cols]], 0))
                after = jnp.where(col == cols - 1, 0.0, pltpu.roll(lines, area - 1, axis=0))
                before = jnp.where(col == 0, 0.0, pltpu.roll(lines, 1, axis=0))
                pre[0, part(u, 2)] = after + pltpu.roll(lines, LANES - 9, axis=1) + pltpu.roll(before, LANES - 18, axis=1)
            for u in range(2):
                f = 2 * i + u
                for j in range(3):
                    for s in range(2):
                        pre[0, part(u, j, area - cols if s else 0, cols)] += evf[j, s, ring_v(f)]
                for j in range(3):
                    for s in range(2):
                        pre[0, part(u, j, cols - 1 if s else 0, rows, cols)] += ehf[j, s, ring_h(f)]
                for c in range(cols):
                    here = pre[0, part(u, 2, c, rows, cols)].astype(bf)
                    rc1h[c // 8, rows16(f * rows, rows), c % 8 * LANES : c % 8 * LANES + LANES] = here
                whole = cat([pre[0, part(u, 0)], pre[0, part(u, 1)]]).astype(bf)
                hc[f, 1 : rows + 1, :, 512:768] = whole.reshape(rows, cols, 256)
            for u in range(2):
                gx_copy(2 * i + u).start()

    cload.wait()
    last_part()
    sums("end")
    hotload.wait()
    back = sum(
        dot_nt(rc1h[k // 4, :, k % 4 * 256 : k % 4 * 256 + 256], hot[144 * k : 144 * k + 144]) for k in range(8))
    for f in range(faces):
        ev[f] = back[f * rows : f * rows + rows].T.astype(bf).reshape(9, cols, rows)
    eout = pltpu.make_async_copy(ev, gext_ref, lsem.at[1])
    eout.start()
    sums("rest")
    tail = slope[768:1024].astype(f32)
    for h in range(2):
        for t in range(TAPS):
            at = 32 * (t // 3) + 9 * (t % 3)
            tails[t, :, 128 * h : 128 * h + 128] = tail[at : at + 9, 128 * h : 128 * h + 128]
    for t in range(TAPS):
        pltpu.make_async_copy(tails.at[t], first_ref.at[t, pl.ds(256, 9)], lsem.at[10]).start()
    for b in range(3):
        @pl.loop(0, 3)
        def _(a):
            accb[pl.ds(pl.multiple_of(BLOCKS[b] + 256 * a, 256), 256)] = slope[
                pl.ds(pl.multiple_of(BLOCKS[b] + 256 * a, 256), 256)].astype(f32)
            pltpu.make_async_copy(
                accb.at[pl.ds(pl.multiple_of(BLOCKS[b] + 256 * a, 256), 256)], first_ref.at[3 * a + b, pl.ds(0, 256)],
                lsem.at[9]).start()
    @pl.loop(0, TAPS)
    def _(t):
        here = pl.ds(pl.multiple_of(256 * t, 256), 256)
        acca[here] = outa[here].astype(f32)
        pltpu.make_async_copy(acca.at[here], second_ref.at[here], lsem.at[8]).start()

    skip_ref[0:256] = outa[2304:2560].astype(f32)
    skip_ref[256:265] = tail[96 + 9 : 96 + 18]
    one_ref[...] = tail[32 + ONE : 32 + ONE + 1]
    two_ref[...] = tail[128:129]
    three_ref[...] = tail[96 + ONE : 96 + ONE + 1]
    pltpu.make_async_copy(out_ref, out_ref, lsem.at[3]).wait()
    pltpu.make_async_copy(gx_ref, gx_ref, lsem.at[4]).wait()
    eout.wait()
    pltpu.make_async_copy(acca.at[0:2304], second_ref, lsem.at[8]).wait()
    pltpu.make_async_copy(accb.at[0:2304], accb.at[0:2304], lsem.at[9]).wait()
    pltpu.make_async_copy(tails, tails, lsem.at[10]).wait()
    for ex in (first, second, third, fourth):
        ex.drain()


def packing(extra, cols, moves):
    hot = np.zeros((extra, cols, cols, LANES), ml_dtypes.bfloat16)
    for start, step in moves:
        for channel in range(extra):
            for column in range(cols):
                if 0 <= column - step < cols:
                    hot[channel, column, column - step, start + channel] = 1
    hot = hot.reshape(extra * cols, cols * LANES // 256, 256)
    return hot.transpose(1, 0, 2).reshape(-1, 256)


def fast_device(
    features, extra_inputs, first_kernel, first_bias, second_kernel, second_bias,
    skip_kernel, skip_bias, seam_table, cotangent,
):
    f32, bf = jnp.float32, jnp.bfloat16
    _, faces, rows, cols, ch = features.shape
    area = rows * cols
    extra = extra_inputs.shape[-1]
    vm, hbm = pl.BlockSpec(memory_space=pltpu.VMEM), pl.BlockSpec(memory_space=pl.ANY)
    shape = jax.ShapeDtypeStruct

    def exchange_bufs(lanes, windows):
        return [
            pltpu.VMEM((2, 192, lanes), bf), pltpu.VMEM((2, 384, lanes), bf), pltpu.VMEM((384, lanes), bf),
            pltpu.VMEM((384, lanes), bf), pltpu.VMEM((2, 192, lanes), bf), pltpu.VMEM((2, 384, lanes), bf),
            pltpu.VMEM((4, 16, lanes), bf), pltpu.VMEM((8 * windows, 16, lanes), bf),
            pltpu.VMEM((2 * windows, 16, lanes), bf),
        ]

    cat_shape = (rows + 2, cols, 3 * ch)
    sums = (SUM_ROWS, ch)
    scratch = [
        pltpu.VMEM((TAPS, ch + extra, ch), bf), pltpu.VMEM((TAPS, ch, ch), bf), pltpu.VMEM((ch + extra, ch), bf),
        pltpu.VMEM((3, LANES, ch), bf), pltpu.VMEM((LANES, ch), bf), pltpu.VMEM((2, LANES, ch), bf),
        pltpu.VMEM((384, 384), bf),
        pltpu.VMEM((4, 16, LANES), f32), pltpu.VMEM((TAPS, extra, ch), f32),
        pltpu.VMEM((faces, rows, cols, ch), bf), pltpu.VMEM((faces, extra, cols, rows), bf),
        pltpu.VMEM((faces, area, ch), bf), pltpu.VMEM((faces, rows + 2, cols, LANES), bf),
        [pltpu.VMEM(cat_shape, bf)] * 2, pltpu.VMEM((faces,) + cat_shape, bf),
        pltpu.VMEM((2, faces * area, LANES), f32), pltpu.VMEM((faces * area, ch), bf),
        pltpu.VMEM((2, 2, 192, LANES), f32), pltpu.VMEM((2, 2, 384, LANES), f32),
        pltpu.VMEM((2, 192, ch), bf), pltpu.VMEM((2, 384, ch), bf),
        pltpu.VMEM((3, area, LANES), f32),
        pltpu.VMEM((3, 2, 192, LANES), f32), pltpu.VMEM((3, 2, 384, LANES), f32),
        pltpu.VMEM((3, 2, 240, LANES), f32), pltpu.VMEM((3, 2, 408, LANES), f32),
        pltpu.VMEM((3, 2, 192, LANES), f32), pltpu.VMEM((3, 2, 384, LANES), f32),
        pltpu.VMEM((2, 192, 896), bf), pltpu.VMEM((2, 384, 1152), bf),
        pltpu.VMEM((2, 192, 768), bf), pltpu.VMEM((2, 384, 768), bf),
        pltpu.VMEM((2, 192, ch), bf), pltpu.VMEM((2, 384, ch), bf),
        pltpu.VMEM(sums, f32), pltpu.VMEM(sums, f32), pltpu.VMEM(sums, bf), pltpu.VMEM(sums, bf),
        [exchange_bufs(384, 0 + 1), exchange_bufs(256, 1), exchange_bufs(256, 1), exchange_bufs(384, 1)],
        pltpu.SemaphoreType.DMA((4, 48)), pltpu.SemaphoreType.DMA((4, 33)),
        pltpu.SemaphoreType.DMA((len(SUMS), 20)), pltpu.SemaphoreType.DMA((len(SUMS), 20)),
        pltpu.SemaphoreType.REGULAR, pltpu.SemaphoreType.REGULAR((len(SUMS), 4)), pltpu.SemaphoreType.DMA((13,)),
    ]
    out = pl.pallas_call(
        whole_block,
        out_shape=(
            shape((faces, rows, cols, ch), bf), shape((faces, rows, cols, ch), bf), shape((faces, extra, cols, rows), bf),
            shape((TAPS * ch, ch), f32), shape((TAPS, ch + extra, ch), f32),
            shape((2, faces * area, LANES), f32), shape((ch + extra, ch), f32),
            shape((1, ch), f32), shape((1, ch), f32), shape((1, ch), f32),
        ),
        in_specs=[hbm] * 5 + [vm] * 4 + [hbm] * 3,
        out_specs=[hbm] * 6 + [vm] * 4,
        scratch_shapes=scratch,
        compiler_params=pltpu.CompilerParams(
            collective_id=0, has_side_effects=True, vmem_limit_bytes=65400 * 1024),
    )(
        features[0], extra_inputs[0].transpose(0, 3, 2, 1), first_kernel.reshape(TAPS, ch + extra, ch),
        second_kernel.reshape(TAPS, ch, ch), skip_kernel, first_bias, second_bias, skip_bias,
        seam_table.transpose(1, 2, 0), cotangent.reshape(faces, area, ch),
        packing(extra, cols, ((0, -1), (extra, 0), (2 * extra, 1))), packing(extra, cols, ((0, 0),)),
    )
    block_output, grad_features, grad_extra, second_grad, first_grad, _, skip_grad, one, two, three = out
    return (
        block_output.reshape(features.shape),
        grad_features.reshape(features.shape),
        grad_extra.transpose(0, 3, 2, 1)[None],
        first_grad.reshape(first_kernel.shape),
        one[0],
        second_grad.reshape(second_kernel.shape),
        two[0],
        skip_grad,
        three[0],
    )


def solution(mesh):
    fits = mesh.shape["ty"] == 2 and mesh.shape["tx"] == 4

    def block(*args):
        tile = args[0].shape
        if fits and tile[1:] == (12, 32, 16, 256) and args[1].shape[-1] == 9:
            return fast_device(*args)
        return per_device(*args)

    return jax.shard_map(
        block,
        mesh=mesh,
        in_specs=(
            P("dp", None, "ty", "tx", None),
            P("dp", None, "ty", "tx", None),
            P(),
            P(),
            P(),
            P(),
            P(),
            P(),
            P(),
            P("dp", None, "ty", "tx", None),
        ),
        out_specs=(
            P("dp", None, "ty", "tx", None),
            P("dp", None, "ty", "tx", None),
            P("dp", None, "ty", "tx", None),
            P(),
            P(),
            P(),
            P(),
            P(),
            P(),
        ),
        check_vma=False,
    )
```

```python
from functools import partial

import jax
import jax.numpy as jnp
import ml_dtypes
import numpy as np
from jax import lax
from jax.experimental import pallas as pl
from jax.experimental.pallas import tpu as pltpu
from jax.sharding import PartitionSpec as P


def extended(value, sides, width):
    for axis, dim in sides:
        size, length = (lax.axis_size(axis), value.shape[dim])
        up = [(i, (i + 1) % size) for i in range(size - 1)]
        down = [(j, i) for i, j in up]
        last = lax.slice_in_dim(value, length - width, length, axis=dim)
        leading = lax.slice_in_dim(value, 0, width, axis=dim)
        before = lax.ppermute(last, axis, up)
        after = lax.ppermute(leading, axis, down)
        value = jnp.concatenate([before, value, after], axis=dim)
    return value


def face_lines(edge_rows, seam_table):
    face_hot = (
        seam_table[:, :, 0][:, :, None]
        == jnp.arange(edge_rows.shape[1], dtype=jnp.int32)[None, None, :]
    ).astype(edge_rows.dtype)
    side_hot = (
        seam_table[:, :, 1][:, :, None] == jnp.arange(4, dtype=jnp.int32)[None, None, :]
    ).astype(edge_rows.dtype)
    chooser = face_hot[:, :, :, None] * side_hot[:, :, None, :]
    side_lines = jnp.einsum(
        "fsgt,bgtnc->bfsnc",
        chooser,
        edge_rows,
        precision=lax.Precision.HIGHEST,
        preferred_element_type=jnp.float32,
    ).astype(edge_rows.dtype)
    flipped = seam_table[:, :, 2][None, :, :, None, None] == 1
    side_lines = jnp.where(flipped, side_lines[:, :, :, ::-1, :], side_lines)
    corner_rule = seam_table[:, :, 3][None, :, :, None] == 0
    upper_line = side_lines[:, :, 0]
    right_line = side_lines[:, :, 1]
    lower_line = side_lines[:, :, 2]
    left_line = side_lines[:, :, 3]
    upper_left = jnp.where(corner_rule[:, :, 0], upper_line[:, :, 0], left_line[:, :, 0])
    upper_right = jnp.where(corner_rule[:, :, 1], upper_line[:, :, -1], right_line[:, :, 0])
    lower_right = jnp.where(corner_rule[:, :, 2], lower_line[:, :, -1], right_line[:, :, -1])
    lower_left = jnp.where(corner_rule[:, :, 3], lower_line[:, :, 0], left_line[:, :, -1])
    upper_full = jnp.concatenate(
        [upper_left[:, :, None], upper_line, upper_right[:, :, None]], axis=2
    )
    right_full = jnp.concatenate(
        [upper_right[:, :, None], right_line, lower_right[:, :, None]], axis=2
    )
    lower_full = jnp.concatenate(
        [lower_left[:, :, None], lower_line, lower_right[:, :, None]], axis=2
    )
    left_full = jnp.concatenate([upper_left[:, :, None], left_line, lower_left[:, :, None]], axis=2)
    return (upper_full, right_full, lower_full, left_full)


def seam_layer(edge_rows, seam_table, place):
    row_index, column_index, row_count, column_count, tile_rows, tile_columns = place
    upper_full, right_full, lower_full, left_full = face_lines(edge_rows, seam_table)
    upper_piece = lax.dynamic_slice_in_dim(
        upper_full, column_index * tile_columns, tile_columns + 2, 2
    )
    lower_piece = lax.dynamic_slice_in_dim(
        lower_full, column_index * tile_columns, tile_columns + 2, 2
    )
    left_piece = lax.dynamic_slice_in_dim(left_full, row_index * tile_rows, tile_rows + 2, 2)
    right_piece = lax.dynamic_slice_in_dim(right_full, row_index * tile_rows, tile_rows + 2, 2)
    grid_rows = lax.broadcasted_iota(jnp.int32, (tile_rows + 2, tile_columns + 2, 1), 0)
    grid_columns = lax.broadcasted_iota(jnp.int32, (tile_rows + 2, tile_columns + 2, 1), 1)
    seam_cells = jnp.zeros(
        upper_piece.shape[:2] + (tile_rows + 2, tile_columns + 2, upper_piece.shape[-1]),
        edge_rows.dtype,
    )
    seam_cells = jnp.where((grid_rows == 0) & (row_index == 0), upper_piece[:, :, None], seam_cells)
    seam_cells = jnp.where(
        (grid_rows == tile_rows + 1) & (row_index == row_count - 1),
        lower_piece[:, :, None],
        seam_cells,
    )
    seam_cells = jnp.where(
        (grid_columns == 0) & (column_index == 0), left_piece[:, :, :, None], seam_cells
    )
    seam_cells = jnp.where(
        (grid_columns == tile_columns + 1) & (column_index == column_count - 1),
        right_piece[:, :, :, None],
        seam_cells,
    )
    return seam_cells


def join_tiles(tile_parts):
    moved = jnp.moveaxis(tile_parts, 0, 2)
    return moved.reshape(
        tile_parts.shape[1],
        tile_parts.shape[2],
        tile_parts.shape[0] * tile_parts.shape[3],
        tile_parts.shape[4],
    )


def face_edges(field):
    row_count = lax.axis_size("ty")
    column_count = lax.axis_size("tx")
    row_edges = jnp.stack([field[:, :, 0], field[:, :, -1]], axis=2)
    column_edges = jnp.stack([field[:, :, :, -1], field[:, :, :, 0]], axis=2)
    row_gathered, column_gathered = (
        lax.all_gather(row_edges[None], ("ty", "tx"), axis=0, tiled=True),
        lax.all_gather(column_edges[None], ("ty", "tx"), axis=0, tiled=True),
    )
    row_grid = row_gathered.reshape((row_count, column_count) + row_edges.shape)
    column_grid = column_gathered.reshape((row_count, column_count) + column_edges.shape)
    upper_edge = join_tiles(row_grid[0, :, :, :, 0])
    lower_edge = join_tiles(row_grid[row_count - 1, :, :, :, 1])
    right_edge = join_tiles(column_grid[:, column_count - 1, :, :, 0])
    left_edge = join_tiles(column_grid[:, 0, :, :, 1])
    return jnp.stack([upper_edge, right_edge, lower_edge, left_edge], axis=2)


def extend(field, seam_table, place):
    rimmed = extended(field, (("ty", 2), ("tx", 3)), 1)
    return rimmed + seam_layer(face_edges(field), seam_table, place)


def collect(grad_padded, seam_table, place):
    row_index, column_index, row_count, column_count, tile_rows, tile_columns = place
    widened = extended(grad_padded.astype(jnp.bfloat16), (("ty", 2), ("tx", 3)), 1).astype(
        grad_padded.dtype
    )
    inside = grad_padded[:, :, 1:-1, 1:-1]
    inside = inside.at[:, :, 0].add(widened[:, :, 0, 2 : tile_columns + 2])
    inside = inside.at[:, :, -1].add(widened[:, :, tile_rows + 3, 2 : tile_columns + 2])
    inside = inside.at[:, :, :, 0].add(widened[:, :, 2 : tile_rows + 2, 0])
    inside = inside.at[:, :, :, -1].add(widened[:, :, 2 : tile_rows + 2, tile_columns + 3])
    inside = inside.at[:, :, 0, 0].add(widened[:, :, 0, 0])
    inside = inside.at[:, :, 0, -1].add(widened[:, :, 0, tile_columns + 3])
    inside = inside.at[:, :, -1, 0].add(widened[:, :, tile_rows + 3, 0])
    inside = inside.at[:, :, -1, -1].add(widened[:, :, tile_rows + 3, tile_columns + 3])
    blank = jnp.zeros(
        grad_padded.shape[:2] + (4, tile_rows * row_count, grad_padded.shape[-1]), jnp.float32
    )
    unused, seam_pull = jax.vjp(
        lambda edge_values: seam_layer(edge_values, seam_table, place), blank
    )
    (edge_grads,) = seam_pull(grad_padded)
    edge_grads = lax.psum(edge_grads, ("ty", "tx"))
    upper_part = lax.dynamic_slice_in_dim(
        edge_grads[:, :, 0], column_index * tile_columns, tile_columns, 2
    )
    right_part = lax.dynamic_slice_in_dim(edge_grads[:, :, 1], row_index * tile_rows, tile_rows, 2)
    lower_part = lax.dynamic_slice_in_dim(
        edge_grads[:, :, 2], column_index * tile_columns, tile_columns, 2
    )
    left_part = lax.dynamic_slice_in_dim(edge_grads[:, :, 3], row_index * tile_rows, tile_rows, 2)
    inside = inside.at[:, :, 0].add(jnp.where(row_index == 0, upper_part, 0.0))
    inside = inside.at[:, :, -1].add(jnp.where(row_index == row_count - 1, lower_part, 0.0))
    inside = inside.at[:, :, :, 0].add(jnp.where(column_index == 0, left_part, 0.0))
    inside = inside.at[:, :, :, -1].add(
        jnp.where(column_index == column_count - 1, right_part, 0.0)
    )
    return inside


def conv_valid(padded, kernel):
    shape_in = padded.shape
    merged = padded.reshape(shape_in[0] * shape_in[1], shape_in[2], shape_in[3], shape_in[4])
    result = lax.conv_general_dilated(
        merged,
        kernel,
        (1, 1),
        "VALID",
        dimension_numbers=("NHWC", "HWIO", "NHWC"),
        preferred_element_type=jnp.float32,
    )
    return result.reshape(
        shape_in[0], shape_in[1], shape_in[2] - 2, shape_in[3] - 2, kernel.shape[-1]
    )


def conv_back(grad_pre, kernel):
    flipped = jnp.transpose(kernel[::-1, ::-1], (0, 1, 3, 2))
    surround = jnp.pad(grad_pre, ((0, 0), (0, 0), (2, 2), (2, 2), (0, 0)))
    return conv_valid(surround, flipped)


def kernel_grad(padded, grad_pre):
    tile_rows = grad_pre.shape[2]
    tile_columns = grad_pre.shape[3]
    pieces = []
    for offset_row in range(3):
        for offset_column in range(3):
            window = padded[
                :,
                :,
                offset_row : offset_row + tile_rows,
                offset_column : offset_column + tile_columns,
            ]
            pieces.append(
                jnp.einsum("sfhwc,sfhwd->cd", window, grad_pre, preferred_element_type=jnp.float32)
            )
    return jnp.stack(pieces).reshape(3, 3, padded.shape[-1], grad_pre.shape[-1])


def per_device(
    features,
    extra_inputs,
    first_kernel,
    first_bias,
    second_kernel,
    second_bias,
    skip_kernel,
    skip_bias,
    seam_table,
    cotangent,
):
    place = (
        lax.axis_index("ty"),
        lax.axis_index("tx"),
        lax.axis_size("ty"),
        lax.axis_size("tx"),
        features.shape[2],
        features.shape[3],
    )
    gelu_exact = partial(jax.nn.gelu, approximate=False)
    joined = jnp.concatenate([features, extra_inputs], axis=-1)
    padded_one = extend(joined, seam_table, place)
    pre_one = conv_valid(padded_one, first_kernel) + first_bias
    active_one, slope_one = jax.vjp(gelu_exact, pre_one)
    hidden = active_one.astype(jnp.bfloat16)
    padded_two = extend(hidden, seam_table, place)
    pre_two = conv_valid(padded_two, second_kernel) + second_bias
    active_two, slope_two = jax.vjp(gelu_exact, pre_two)
    skipped = (
        jnp.einsum("sfhwc,cd->sfhwd", joined, skip_kernel, preferred_element_type=jnp.float32)
        + skip_bias
    )
    block_output = (active_two + skipped).astype(jnp.bfloat16)
    (grad_two,) = slope_two(cotangent.astype(jnp.float32))
    grad_two = grad_two.astype(jnp.bfloat16)
    second_kernel_grad = kernel_grad(padded_two, grad_two)
    second_bias_grad = jnp.sum(grad_two, axis=(0, 1, 2, 3), dtype=jnp.float32)
    grad_hidden = collect(conv_back(grad_two, second_kernel), seam_table, place)
    (grad_one,) = slope_one(grad_hidden)
    grad_one = grad_one.astype(jnp.bfloat16)
    first_kernel_grad = kernel_grad(padded_one, grad_one)
    first_bias_grad = jnp.sum(grad_one, axis=(0, 1, 2, 3), dtype=jnp.float32)
    grad_joined = collect(conv_back(grad_one, first_kernel), seam_table, place)
    grad_joined = grad_joined + jnp.einsum(
        "sfhwd,cd->sfhwc", cotangent, skip_kernel, preferred_element_type=jnp.float32
    )
    skip_kernel_grad = jnp.einsum(
        "sfhwc,sfhwd->cd", joined, cotangent, preferred_element_type=jnp.float32
    )
    skip_bias_grad = jnp.sum(cotangent, axis=(0, 1, 2, 3), dtype=jnp.float32)
    summed = lax.psum(
        (
            first_kernel_grad,
            first_bias_grad,
            second_kernel_grad,
            second_bias_grad,
            skip_kernel_grad,
            skip_bias_grad,
        ),
        ("dp", "ty", "tx"),
    )
    grad_joined = grad_joined.astype(jnp.bfloat16)
    channels = features.shape[-1]
    return (
        block_output,
        grad_joined[..., :channels],
        grad_joined[..., channels:],
        summed[0],
        summed[1],
        summed[2],
        summed[3],
        summed[4],
        summed[5],
    )


TAPS = 9
SUM_ROWS = 2560
LANES = 128
PACK = 27
ONE = 27
FOUR = ("core", "x", "y", "z")
FOURY = ("core", "y", "x", "z")
SUMS = (("a", 0, 2560, FOUR), ("b", 0, 1024, FOUR), ("c", 1024, 512, FOURY), ("d", 1536, 1024, FOURY))
BLOCKS = (0, 1024, 1792)
SUM_PLAN = {
    ('middle', 0): (('a', 0),),
    ('back', 4): (('a', 1),),
    ('sent', 0): (('a', 2),),
    ('first', 0): (('b', 0),),
    ('more', 4): (('c', 0), ('b', 1)),
    ('third', 0): (('d', 0), ('c', 1), ('a', 3)),
    ('out', 2): (('b', 2),),
    ('out', 3): (('d', 1),),
    ('out', 5): (('c', 2),),
    ('last', 0): (('d', 2), ('b', 3), ('a', 4)),
    ('last', 1): (('d', 3), ('c', 3)),
    ('last', 2): (('d', 4), ('c', 4), ('b', 4), ('a', 5)),
    ('last', 3): (('d', 5), ('c', 5), ('b', 5)),
    ('last', 4): (('c', 6), ('b', 6), ('a', 6)),
    ('last', 5): (('d', 6), ('c', 7)),
    ('end', 0): (('d', 7), ('c', 8), ('b', 7), ('a', 7)),
    ('rest', 0): (('d', 8), ('b', 8), ('a', 8)),
}


def whole_block(
    x_in, ext_in, w1_in, w2_in, skip_in, bias_one, bias_two, bias_skip, table, cot_in, hot_in, hot_back_in,
    out_ref, gx_ref, gext_ref, second_ref, first_ref, kept, skip_ref, one_ref, two_ref, three_ref,
    w1, w2, wskip, we, wse, we81, sel_t, rule, tails,
    xv, ev, cv, t27, xc, hc, pre, slope, slev, sleh, cev, ceh,
    ff, evf, ehf, rvf, rhf, cvf, chf, rc1v, rc1h, rc2v, rc2h, gev, geh,
    acca, accb, outa, landa, bufs, ssem, rsem, sum_ssem, sum_rsem, credit, ack, lsem,
):
    f32, bf = jnp.float32, jnp.bfloat16
    dp, ty, tx = lax.axis_index("dp"), lax.axis_index("ty"), lax.axis_index("tx")
    core, xx, place = dp % 2, dp // 2, ty * 4 + tx
    core_mate, x_mate = dp + 1 - 2 * core, dp + 2 - 4 * xx
    faces, rows, cols = x_in.shape[0], x_in.shape[1], x_in.shape[2]
    area = rows * cols
    is_mid = jnp.where((tx == 0) | (tx == 3), 0, 1)
    hx = jnp.where(tx >= 2, 1, 0)
    kk = ty + 2 * hx
    mm = kk + 4 * is_mid
    at_end = is_mid == 0

    def dev(y, x):
        return {"ty": y, "tx": x}

    def rows16(start, size):
        return pl.ds(pl.multiple_of(start, 16), size)

    def home(m):
        half = (m // 2) % 2
        return m % 2, (3 * half if m // 4 == 0 else 1 + half)

    def home_class(k):
        half = k // 2
        return k % 2, jnp.where(at_end, 3 * half, 1 + half)

    def flip48(flag, k, n):
        return 48 * jnp.where(flag, n - 1 - k, k)

    def maybe(cond, call):
        if cond is None:
            call()
        else:
            pl.when(cond)(call)

    class Exchange:
        def __init__(self, index):
            self.index = index
            self.ed_v, self.ed_h, self.db, self.sb, self.rg_v, self.rg_h, self.rg_c, self.xw, self.xd = bufs[index]

        def copies(self, sends, first_slot):
            for n, (cond, src, dst, rs, target) in enumerate(sends):
                yield cond, pltpu.make_async_remote_copy(
                    src_ref=src, dst_ref=dst, send_sem=ssem.at[self.index, first_slot + n],
                    recv_sem=rsem.at[self.index, rs], device_id=target, device_id_type=pl.DeviceIdType.MESH,
                )

        def start(self):
            for cond, copy in self.copies(self.first_sends(), 0):
                maybe(cond, copy.start)
            self.first_moves()

        def middle(self):
            self.relay()
            for cond, copy in self.copies(self.second_sends(), 24):
                maybe(cond, copy.start)
            self.second_moves()

        def drain(self):
            for cond, copy in self.copies(self.first_sends(), 0):
                maybe(cond, copy.wait_send)
            for cond, copy in self.copies(self.second_sends(), 24):
                maybe(cond, copy.wait_send)

        def get(self, cond, dst, rs):
            copy = pltpu.make_async_remote_copy(
                src_ref=dst, dst_ref=dst, send_sem=ssem.at[self.index, 0],
                recv_sem=rsem.at[self.index, rs], device_id=dev(1 - ty, tx), device_id_type=pl.DeviceIdType.MESH,
            )
            maybe(cond, copy.wait_recv)

        def move(self, cond, dst, dst_at, src, src_at):
            @pl.when(cond)
            def _():
                dst[dst_at] = src[src_at]

    class Forward(Exchange):
        def row_pieces(self):
            to = rows16((2 * ty) * 96 + hx * 48, 48)
            for k in range(4):
                yield k, rows16(flip48(hx == 1, k, 4), 48), to

        def column_pieces(self):
            to = rows16(jnp.where(hx == 1, 1, 3) * 96 + ty * 48, 48)
            for m in range(8):
                yield m, rows16(flip48(ty == 1, m, 8), 48), to

        def first_sends(self):
            ed_v, ed_h, db, rg_v, rg_h, rg_c = self.ed_v, self.ed_h, self.db, self.rg_v, self.rg_h, self.rg_c
            for k, at, to in self.row_pieces():
                yield kk != k, ed_v.at[ty, at], db.at[to], (2 * ty) * 2 + hx, dev(*home_class(k))
            for m, at, to in self.column_pieces():
                yield at_end & (mm != m), ed_h.at[hx, at], db.at[to], jnp.where(hx == 1, 2, 6) + ty, dev(*home(m))
            yield None, ed_v.at[1 - ty], rg_v.at[ty], 24, dev(1 - ty, tx)
            yield tx < 3, ed_h.at[1], rg_h.at[0], 25, dev(ty, tx + 1)
            yield tx > 0, ed_h.at[0], rg_h.at[1], 26, dev(ty, tx - 1)
            yield tx < 3, ed_v.at[1 - ty, pl.ds(176, 16)], rg_c.at[2 * ty], 20 + 2 * ty, dev(1 - ty, tx + 1)
            yield tx > 0, ed_v.at[1 - ty, pl.ds(0, 16)], rg_c.at[2 * ty + 1], 21 + 2 * ty, dev(1 - ty, tx - 1)

        def first_moves(self):
            for k, at, to in self.row_pieces():
                self.move(kk == k, self.db, (to,), self.ed_v, (ty, at))
            for m, at, to in self.column_pieces():
                self.move(at_end & (mm == m), self.db, (to,), self.ed_h, (hx, at))

        def relay(self):
            db, sb = self.db, self.sb
            for t in range(4):
                for h in range(2):
                    if t % 2 == 0:
                        own = (ty == t // 2) & (hx == h)
                    else:
                        own = at_end & (ty == h) & (tx == (0 if t == 3 else 3))
                    self.get(jnp.logical_not(own), db.at[pl.ds(t * 96 + h * 48, 48)], t * 2 + h)
            sb[...] = dot_tn(sel_t[...], db[...]).astype(bf)

        def out_rows(self):
            for y in range(2):
                for h in range(2):
                    x = jnp.where(at_end, 3 * h, 1 + h)
                    own = (ty == y) & (tx == x)
                    yield own, y, x, pl.ds(2 * y * 96 + h * 48, 48), rows16(48 * ((3 - kk) if h else kk), 48)

        def out_columns(self):
            for y in range(2):
                for h in range(2):
                    own = (ty == y) & (tx == 3 * h)
                    at = pl.ds((1 if h else 3) * 96 + y * 48, 48)
                    yield own, y, h, at, rows16(48 * ((7 - mm) if y else mm), 48)

        def out_corners(self):
            for y in range(2):
                for m, x, right, at in ((3, 1, 0, 32), (3, 2, 1, 48), (4, 3, 0, 80), (4, 0, 1, 0), (7, 2, 0, 32), (7, 1, 1, 48)):
                    yield m, y, x, 2 * y + right, pl.ds(2 * y * 96 + at, 16)
                for h in range(2):
                    yield 7, y, 3 * h, 2 * (1 - y) + h, pl.ds((1 if h else 3) * 96 + (32 if y else 48), 16)

        def second_sends(self):
            sb = self.sb
            for own, y, x, at, to in self.out_rows():
                yield jnp.logical_not(own), sb.at[at], self.rg_v.at[y, to], 8 + kk, dev(y, x)
            for own, y, h, at, to in self.out_columns():
                yield jnp.logical_not(own), sb.at[at], self.rg_h.at[h, to], 12 + mm, dev(y, 3 * h)
            for m, y, x, spot, at in self.out_corners():
                if home(m) != (y, x):
                    yield mm == m, sb.at[at], self.rg_c.at[spot], 20 + spot, dev(y, x)

        def second_moves(self):
            for own, y, x, at, to in self.out_rows():
                self.move(own, self.rg_v, (y, to), self.sb, (at,))
            for own, y, h, at, to in self.out_columns():
                self.move(own, self.rg_h, (h, to), self.sb, (at,))
            for m, y, x, spot, at in self.out_corners():
                if home(m) == (y, x):
                    self.move(mm == m, self.rg_c, (spot,), self.sb, (at,))

        def finish(self):
            self.get(None, self.rg_v.at[1 - ty], 24)
            self.get(tx > 0, self.rg_h.at[0], 25)
            self.get(tx < 3, self.rg_h.at[1], 26)
            for k in range(4):
                self.get(kk != k, self.rg_v.at[ty, rows16(flip48(hx == 1, k, 4), 48)], 8 + k)
            for m in range(8):
                self.get(at_end & (mm != m), self.rg_h.at[hx, rows16(flip48(ty == 1, m, 8), 48)], 12 + m)
            for spot in range(4):
                y, right = spot // 2, spot % 2
                face_corner = (ty == y) & (tx == 3 * right)
                if spot == 2:
                    own = (ty == 1) & (tx == 2)
                    skip = face_corner | own
                else:
                    skip = face_corner
                self.get(jnp.logical_not(skip), self.rg_c.at[spot], 20 + spot)

    class Backward(Exchange):
        row_pieces, column_pieces = Forward.row_pieces, Forward.column_pieces
        out_rows, out_columns = Forward.out_rows, Forward.out_columns

        def corners(self):
            for right in range(2):
                away = (tx < 3) if right else (tx > 0)
                if right:
                    x, y = jnp.where(tx == 0, 1, jnp.where(tx == 1, 2, 3)), jnp.where(tx == 0, 0, 1)
                else:
                    x, y = jnp.where(tx == 1, 3, jnp.where(tx == 2, 2, 1)), jnp.where(tx == 3, 0, 1)
                own = away & (ty == y) & (tx == x)
                yield right, away, own, x, y, 2 * ty + right

        def first_sends(self):
            rg_v, rg_h, rg_c, sb, xw, xd = self.rg_v, self.rg_h, self.rg_c, self.sb, self.xw, self.xd
            for k, at, to in self.row_pieces():
                yield kk != k, rg_v.at[ty, at], sb.at[to], (2 * ty) * 2 + hx, dev(*home_class(k))
            for m, at, to in self.column_pieces():
                yield at_end & (mm != m), rg_h.at[hx, at], sb.at[to], jnp.where(hx == 1, 2, 6) + ty, dev(*home(m))
            for right, away, own, x, y, slot in self.corners():
                yield away & jnp.logical_not(own), rg_c.at[slot], xw.at[slot], 8 + slot, dev(y, x)
                inner = 2 * (1 - ty) + right
                edge = (tx == 3) if right else (tx == 0)
                yield edge, rg_c.at[inner], xw.at[4 + slot], 12 + slot, dev(1, 2)
                yield away, rg_c.at[inner], xd.at[1 - right], 17 - right, dev(1 - ty, tx + (1 if right else -1))
            ed_v, ed_h = self.ed_v, self.ed_h
            yield None, rg_v.at[1 - ty], ed_v.at[ty], 30, dev(1 - ty, tx)
            yield tx < 3, rg_h.at[1], ed_h.at[0], 31, dev(ty, tx + 1)
            yield tx > 0, rg_h.at[0], ed_h.at[1], 32, dev(ty, tx - 1)

        def first_moves(self):
            for k, at, to in self.row_pieces():
                self.move(kk == k, self.sb, (to,), self.rg_v, (ty, at))
            for m, at, to in self.column_pieces():
                self.move(at_end & (mm == m), self.sb, (to,), self.rg_h, (hx, at))
            for right, away, own, x, y, slot in self.corners():
                self.move(own, self.xw, (slot,), self.rg_c, (slot,))

        def relay(self):
            sb, db, xw = self.sb, self.db, self.xw
            for s in range(4):
                for h in range(2):
                    if s % 2 == 0:
                        own = (ty == s // 2) & (hx == h)
                    else:
                        own = at_end & (ty == h) & (tx == (0 if s == 3 else 3))
                    self.get(jnp.logical_not(own), sb.at[pl.ds(s * 96 + h * 48, 48)], s * 2 + h)
            for y in range(2):
                for right in range(2):
                    slot = 2 * y + right
                    wants = (mm == 3) | (mm == 4) | (mm == 7)
                    if slot == 2:
                        wants = (mm == 3) | (mm == 4)
                    self.get(wants, xw.at[slot], 8 + slot)
                    self.get(mm == 7, xw.at[4 + slot], 12 + slot)
                    for m, at in ((3, 48 if right else 32), (4, 0 if right else 80), (7, 48 if right else 32)):
                        @pl.when(mm == m)
                        def _(spot=2 * y * 96 + at, slot=slot):
                            here = pl.ds(spot, 16)
                            sb[here] = (sb[here].astype(f32) + xw[slot].astype(f32)).astype(bf)

                    @pl.when(mm == 7)
                    def _(spot=(1 if right else 3) * 96 + (32 if y else 48), slot=4 + slot):
                        here = pl.ds(spot, 16)
                        sb[here] = (sb[here].astype(f32) + xw[slot].astype(f32)).astype(bf)
            db[...] = dot(sel_t[...], sb[...]).astype(bf)

        def second_sends(self):
            for own, y, x, at, to in self.out_rows():
                yield jnp.logical_not(own), self.db.at[at], self.ed_v.at[y, to], 18 + kk, dev(y, x)
            for own, y, h, at, to in self.out_columns():
                yield jnp.logical_not(own), self.db.at[at], self.ed_h.at[h, to], 22 + mm, dev(y, 3 * h)

        def second_moves(self):
            for own, y, x, at, to in self.out_rows():
                self.move(own, self.ed_v, (y, to), self.db, (at,))
            for own, y, h, at, to in self.out_columns():
                self.move(own, self.ed_h, (h, to), self.db, (at,))

        def finish(self):
            self.get(None, self.ed_v.at[1 - ty], 30)
            self.get(tx > 0, self.ed_h.at[0], 31)
            self.get(tx < 3, self.ed_h.at[1], 32)
            self.get(tx > 0, self.xd.at[0], 16)
            self.get(tx < 3, self.xd.at[1], 17)
            for k in range(4):
                self.get(kk != k, self.ed_v.at[ty, rows16(flip48(hx == 1, k, 4), 48)], 18 + k)
            for m in range(8):
                self.get(at_end & (mm != m), self.ed_h.at[hx, rows16(flip48(ty == 1, m, 8), 48)], 22 + m)

        def stage(self, blocks):
            for j in range(blocks):
                lanes = slice(128 * j, 128 * j + 128)
                for s in range(2):
                    evf[j, s] = self.ed_v[s, :, lanes].astype(f32)
                    ehf[j, s] = self.ed_h[s, :, lanes].astype(f32)

                @pl.when(tx > 0)
                def _(j=j, lanes=lanes):
                    evf[j, 1 - ty, pl.ds(0, 16)] += self.xd[0, :, lanes].astype(f32)

                @pl.when(tx < 3)
                def _(j=j, lanes=lanes):
                    evf[j, 1 - ty, pl.ds(176, 16)] += self.xd[1, :, lanes].astype(f32)

    class Total:
        def __init__(self, index, acc, acc0, out, out0, land, land0, count, order):
            self.index, self.acc, self.out, self.land = index, acc, out, land
            self.acc0, self.out0, self.land0, self.count = acc0, out0, land0, count
            axes = {
                "core": (2, core, lambda k: {"dp": core_mate}),
                "x": (2, xx, lambda k: {"dp": x_mate}),
                "y": (2, ty, lambda k: {"ty": 1 - ty}),
                "z": (4, tx, lambda k: {"tx": k}),
                "yz": (8, place, lambda k: {"ty": k // 4, "tx": k % 4}),
            }
            self.stages = []
            start, size, land_at, sem = 0, count, 0, 0
            for name in order:
                n, me, target = axes[name]
                chunk = size // n
                self.stages.append((n, me, target, start, chunk, land_at, sem))
                land_at += chunk * (1 if n == 2 else n)
                sem += 1 if n == 2 else n
                start, size = start + me * chunk, chunk
            self.unit, self.sems, self.last = size, sem, len(order) - 1
            self.near = []
            for n, me, *_ in self.stages:
                if n == 2:
                    self.near.append([(1 - me, None, 0, 0)])
                else:
                    self.near.append([(k, me != k, k, me) for k in range(n)])

        def at(self, base, start, size):
            return rows16(base + start, size)

        def copy(self, src, dst, slot, rslot, target):
            return pltpu.make_async_remote_copy(
                src_ref=src, dst_ref=dst, send_sem=sum_ssem.at[self.index, slot],
                recv_sem=sum_rsem.at[self.index, rslot], device_id=target, device_id_type=pl.DeviceIdType.MESH,
            )

        def rs_copy(self, s, k, mine, theirs):
            n, me, target, start, chunk, land_at, sem = self.stages[s]
            return self.copy(
                self.out.at[self.at(self.out0, start + k * chunk, chunk)],
                self.land.at[self.at(self.land0, land_at + chunk * theirs, chunk)],
                sem + mine, sem + theirs, target(k))

        def send_rs(self, s):
            n, me, target, start, chunk, land_at, sem = self.stages[s]
            for k, cond, mine, theirs in self.near[s]:
                def go(k=k, mine=mine, theirs=theirs):
                    self.cast(start + k * chunk, chunk)
                    self.rs_copy(s, k, mine, theirs).start()
                maybe(cond, go)

        def recv_rs(self, s):
            n, me, target, start, chunk, land_at, sem = self.stages[s]
            for k, cond, mine, theirs in self.near[s]:
                def get(k=k, mine=mine):
                    here = self.land.at[self.at(self.land0, land_at + chunk * mine, chunk)]
                    self.copy(here, here, sem + mine, sem + mine, target(k)).wait_recv()

                    @pl.loop(0, chunk // self.unit)
                    def _(i):
                        self.acc[self.at(self.acc0, start + me * chunk + i * self.unit, self.unit)] += self.land[
                            self.at(self.land0, land_at + chunk * mine + i * self.unit, self.unit)].astype(f32)

                maybe(cond, get)

        def done_rs(self, s):
            target = self.stages[s][2]
            for k, cond, mine, theirs in self.near[s]:
                def done(k=k, mine=mine, theirs=theirs):
                    self.rs_copy(s, k, mine, theirs).wait_send()
                    pl.semaphore_signal(
                        ack.at[self.index, s], inc=1, device_id=target(k), device_id_type=pl.DeviceIdType.MESH)
                maybe(cond, done)

        def ag_copy(self, s, k, mine, theirs):
            n, me, target, start, chunk, land_at, sem = self.stages[s]
            here = self.out.at[self.at(self.out0, start + me * chunk, chunk)]
            return self.copy(here, here, self.sems + sem + mine, self.sems + sem + theirs, target(k))

        def send_ag(self, s):
            pl.semaphore_wait(ack.at[self.index, s], self.stages[s][0] - 1)
            for k, cond, mine, theirs in self.near[s]:
                maybe(cond, lambda k=k, mine=mine, theirs=theirs: self.ag_copy(s, k, mine, theirs).start())

        def recv_ag(self, s):
            n, me, target, start, chunk, land_at, sem = self.stages[s]
            for k, cond, mine, theirs in self.near[s]:
                def get(k=k, mine=mine):
                    here = self.out.at[self.at(self.out0, start + k * chunk, chunk)]
                    slot = self.sems + sem + mine
                    self.copy(here, here, slot, slot, target(k)).wait_recv()
                maybe(cond, get)

        def cast(self, start, size):
            @pl.loop(0, size // self.unit)
            def _(i):
                at = start + i * self.unit
                self.out[self.at(self.out0, at, self.unit)] = self.acc[self.at(self.acc0, at, self.unit)].astype(bf)

        def step(self, k):
            last = self.last
            if k == 0:
                self.send_rs(0)
            elif k <= last:
                self.recv_rs(k - 1)
                self.send_rs(k)
                self.done_rs(k - 1)
            elif k == last + 1:
                self.recv_rs(last)
                n, me, target, start, chunk, land_at, sem = self.stages[last]
                self.cast(start + me * chunk, chunk)
                self.done_rs(last)
                self.send_ag(last)
            elif k <= 2 * last + 1:
                self.recv_ag(2 * last + 2 - k)
                self.send_ag(2 * last + 1 - k)
            else:
                self.recv_ag(0)
                for s in range(last + 1):
                    for k, cond, mine, theirs in self.near[s]:
                        maybe(cond, lambda s=s, k=k, mine=mine, theirs=theirs: self.ag_copy(s, k, mine, theirs).wait_send())

    def sums(where, at=None):
        for (spot, spot_at), steps in SUM_PLAN.items():
            if spot == where:
                def go(steps=steps):
                    for name, k in steps:
                        totals[name].step(k)
                if at is None:
                    go()
                else:
                    pl.when(at == spot_at)(go)

    def dot(a, b):
        return jnp.dot(a, b, preferred_element_type=f32)

    def dot_nt(a, b):
        return lax.dot_general(a, b, (((1,), (1,)), ((), ())), preferred_element_type=f32)

    def dot_tn(a, b):
        return lax.dot_general(a, b, (((0,), (0,)), ((), ())), preferred_element_type=f32)

    def cat(parts, axis=-1):
        return jnp.concatenate(parts, axis=axis)

    def face_rows(f):
        return pl.ds(pl.multiple_of(f * area, area), area)

    def top(f, s):
        return pl.ds(f * area + (area - cols if s else 0), cols)

    def side(f, s):
        return pl.ds(f * area + (cols - 1 if s else 0), rows, stride=cols)

    def ring_v(f):
        return pl.ds(f, cols, stride=faces)

    def ring_h(f):
        return pl.ds(f, rows, stride=faces)

    def shifts(v):
        zero = jnp.zeros((rows, 1, v.shape[-1]), v.dtype)
        return cat([zero, v[:, : cols - 1]], 1), cat([v[:, 1:], zero], 1)

    def fill(ref, v):
        left, right = shifts(v)
        wide = v.shape[-1]
        ref[1 : rows + 1, :, 0:wide] = left
        ref[1 : rows + 1, :, wide : 2 * wide] = v
        ref[1 : rows + 1, :, 2 * wide : 3 * wide] = right

    def windows(ref):
        return [ref[a : a + rows].reshape(area, ref.shape[-1]) for a in range(3)]

    def split(ref, at, v):
        for h in range(2):
            ref[(h,) + at] = v[:, 128 * h : 128 * h + 128]

    def join(ref, at, blocks=2):
        return cat([ref[(h,) + at] for h in range(blocks)])

    def gelu_slope(u):
        phi = 0.5 + 0.5 * lax.erf(u * 0.7071067811865476)
        return u * phi, phi + u * (0.3989422804014327 * jnp.exp(-0.5 * u * u))

    lane = lax.broadcasted_iota(jnp.int32, (1, LANES), 1)

    first, second = Forward(0), Forward(1)
    third, fourth = Backward(2), Backward(3)
    def load(src, dst, sem):
        copy = pltpu.make_async_copy(src, dst, lsem.at[sem])
        copy.start()
        return copy

    eload, hotload, xload = load(ext_in, ev, 1), load(hot_in, slope.at[0:1152], 11), load(x_in, xv, 0)
    w1load, skipload = load(w1_in, w1, 5), load(skip_in, wskip, 6)
    cload, w2load = load(cot_in, cv, 2), load(w2_in, w2, 7)
    barrier = pltpu.get_barrier_semaphore()
    for e in (0, 1):
        bufs[e][6][...] = jnp.zeros_like(bufs[e][6])
    for y in range(2):
        for x in range(4):
            @pl.when((ty != y) | (tx != x))
            def _(y=y, x=x):
                pl.semaphore_signal(barrier, inc=1, device_id=dev(y, x), device_id_type=pl.DeviceIdType.MESH)
    for mate in (core_mate, x_mate):
        pl.semaphore_signal(barrier, inc=1, device_id={"dp": mate}, device_id_type=pl.DeviceIdType.MESH)
    pl.semaphore_wait(barrier, 9)

    for ref in (xc[0], xc[1]):
        ref[0] = jnp.zeros(ref.shape[1:], bf)
        ref[rows + 1] = jnp.zeros(ref.shape[1:], bf)

    @pl.loop(0, faces)
    def _(f):
        hc[f, 0] = jnp.zeros(hc.shape[2:], bf)
        hc[f, rows + 1] = jnp.zeros(hc.shape[2:], bf)
        t27[f, 0] = jnp.zeros(t27.shape[2:], bf)
        t27[f, rows + 1] = jnp.zeros(t27.shape[2:], bf)

    eload.wait()
    turned = cat([ev[f].astype(f32).reshape(9 * cols, rows).T for f in range(faces)], 0).astype(bf)
    hotload.wait()
    for k in range(8):
        flat = dot(turned, slope[144 * k : 144 * k + 144])
        for c in range(2):
            pre[0, pl.ds((2 * k + c) * faces * rows, faces * rows)] = flat[:, c * LANES : c * LANES + LANES]
    xload.wait()

    @pl.loop(0, faces)
    def _(f):
        for c in range(cols):
            ff[2, pl.ds(c, rows, stride=cols)] = pre[0, pl.ds(c * faces * rows + f * rows, rows)]
        packed = ff[2] + jnp.where(lane == ONE, 1.0, 0.0)
        t27[f, 1 : rows + 1] = packed.astype(bf).reshape(rows, cols, LANES)
        ff[2] = jnp.where(lane < 9, pltpu.roll(packed, LANES - 9, axis=1), 0.0)
        for h in range(2):
            ff[h] = xv[f, :, :, 128 * h : 128 * h + 128].astype(f32).reshape(area, LANES)
        for j in range(3):
            for s in range(2):
                evf[j, s, ring_v(f)] = ff[j, pl.ds(area - cols if s else 0, cols)]
                ehf[j, s, ring_h(f)] = ff[j, pl.ds(cols - 1 if s else 0, rows, stride=cols)]

    def edges_out(ex, blocks):
        for s in range(2):
            ex.ed_v[s] = join(evf, (s,), blocks).astype(bf)
            ex.ed_h[s] = join(ehf, (s,), blocks).astype(bf)

    edges_out(first, 3)
    first.start()

    acca[...] = jnp.zeros_like(acca)
    accb[...] = jnp.zeros_like(accb)
    w1load.wait()
    skipload.wait()
    ff[...] = jnp.zeros_like(ff)
    for h in range(2):
        lanes = slice(128 * h, 128 * h + 128)
        for a in range(3):
            for b in range(3):
                ff[h, pl.ds(128 * a + 9 * b, 9)] = w1[3 * a + b, 256:265, lanes].astype(f32)
        ff[h, pl.ds(128 + ONE, 1)] = bias_one[...].astype(f32).reshape(1, 256)[:, lanes]
        ff[h, pl.ds(384 + 9, 9)] = wskip[256:265, lanes].astype(f32)
        ff[h, pl.ds(384 + ONE, 1)] = bias_skip[...].astype(f32).reshape(1, 256)[:, lanes]
        for a in range(3):
            we[a, :, lanes] = ff[h, pl.ds(128 * a, 128)].astype(bf)
        wse[:, lanes] = ff[h, pl.ds(384, 128)].astype(bf)
        ff[h, pl.ds(0, 256)] = jnp.zeros((256, LANES), f32)
        for t in range(TAPS):
            ff[h, pl.ds(9 * t, 9)] = w1[t, 256:265, lanes].astype(f32)
        ff[h, pl.ds(128 + 36, 9)] = wskip[256:265, lanes].astype(f32)
        for k in range(2):
            we81[k, :, lanes] = ff[h, pl.ds(128 * k, 128)].astype(bf)
    total = 32 * faces
    spread = jnp.where(
        lax.broadcasted_iota(jnp.int32, (faces, total), 1) % faces
        == lax.broadcasted_iota(jnp.int32, (faces, total), 0), 1.0, 0.0)
    spot = lax.broadcasted_iota(jnp.int32, (1, total), 1)
    side_of, step_of = spot // (8 * faces), (spot // faces % 8).astype(f32)
    source = jnp.zeros((1, total), f32)
    for s in range(4):
        entry = dot(table[s].astype(f32), spread)
        step = jnp.where(entry[2:3] > 0.5, 7.0 - step_of, step_of)
        source = source + jnp.where(side_of == s, (entry[1:2] * 8.0 + step) * faces + entry[0:1], 0.0)
    sel_t[...] = jnp.where(
        lax.broadcasted_iota(jnp.int32, (total, total), 0) == source.astype(jnp.int32), 1.0, 0.0).astype(bf)
    same = jnp.where(
        lax.broadcasted_iota(jnp.int32, (faces, faces), 1) == lax.broadcasted_iota(jnp.int32, (faces, faces), 0), 1.0, 0.0)
    for spot_index, k in enumerate((0, 1, 3, 2)):
        column = jnp.sum(same * table[k, 3:4].astype(f32), axis=1, keepdims=True)
        rule[spot_index, 0:faces] = jnp.broadcast_to(1.0 - column, (faces, LANES))

    def ring_in(ex, blocks):
        for j in range(blocks):
            lanes = slice(128 * j, 128 * j + 128)
            for s in range(2):
                rvf[j, s, pl.ds(12, 192)] = ex.rg_v[s, :, lanes].astype(f32)
                rhf[j, s, pl.ds(12, 384)] = ex.rg_h[s, :, lanes].astype(f32)
            for spot in range(4):
                s, right = spot // 2, spot % 2
                win = ex.rg_c[spot, :, lanes].astype(f32)
                edge = (tx == 3) if right else (tx == 0)
                late = jnp.where(edge, ty == 1, right == 0)
                got = jnp.where(late, win[4:16], win[0:12])
                from_v = rvf[j, s, pl.ds(192 if right else 12, 12)]
                from_h = rhf[j, right, pl.ds(384 if s else 12, 12)]
                local = jnp.where(rule[spot, 0:12] > 0.0, from_v, from_h)
                rvf[j, s, pl.ds(204 if right else 0, 12)] = jnp.where((ty == s) & edge, local, got)

    def ring_cat(rcv, rch, blocks):
        for s in range(2):
            for b in range(3):
                for j in range(2):
                    at = slice(256 * b + 128 * j, 256 * b + 128 * j + 128)
                    rcv[s, :, at] = rvf[j, s, pl.ds(12 * b, 192)].astype(bf)
                    rch[s, :, at] = rhf[j, s, pl.ds(12 * b, 384)].astype(bf)
            if blocks == 3:
                total = rvf[2, s, pl.ds(0, 192)]
                for b in (1, 2):
                    total = total + pltpu.roll(rvf[2, s, pl.ds(12 * b, 192)], 9 * b, axis=1)
                rcv[s, :, 768:896] = total.astype(bf)
                for a in range(3):
                    line = rhf[2, s, pl.ds(12 * a, 384)]
                    line = pltpu.roll(line, 18, axis=1) if s else line
                    rch[s, :, 768 + 128 * a : 896 + 128 * a] = line.astype(bf)

    def zero_h_ends(blocks):
        for j in range(blocks):
            for s in range(2):
                rhf[j, s, pl.ds(0, 12)] = jnp.zeros((12, LANES), f32)
                rhf[j, s, pl.ds(396, 12)] = jnp.zeros((12, LANES), f32)

    zero_h_ends(3)

    def add_to_edges(source_v, source_h):
        @pl.loop(0, faces)
        def _(f):
            for h in range(2):
                for s in range(2):
                    pre[h, top(f, s)] += source_v[h, s, ring_v(f)]
            for h in range(2):
                for s in range(2):
                    pre[h, side(f, s)] += source_h[h, s, ring_h(f)]
            for h in range(2):
                for s in range(2):
                    evf[h, s, ring_v(f)] = pre[h, top(f, s)]
                    ehf[h, s, ring_h(f)] = pre[h, side(f, s)]

    def w_first(t):
        return w1[t, 0:256]

    def conv_first(f, ref):
        lhs = cat(windows(ref) + windows(t27.at[f]))
        rhs = cat([w_first(t) for t in range(TAPS)] + [we[a] for a in range(3)], 0)
        split(pre, (face_rows(f),), dot(lhs, rhs))

    def first_part():
        @pl.loop(0, faces // 2)
        def _(i):
            pl.when(i == 3)(first.middle)
            for u in range(2):
                fill(xc[u], xv[2 * i + u])
            for u in range(2):
                conv_first(2 * i + u, xc[u])

    cload.wait()

    @pl.loop(0, faces // 2)
    def _(i):
        pair = [2 * i, 2 * i + 1]
        field = cat([cat([xv[f].reshape(area, 256), t27[f, 1 : rows + 1].reshape(area, LANES)]) for f in pair], 0)
        fresh = dot_tn(field, cat([cv[f] for f in pair], 0))
        acca[2304:2560] += fresh[0:256]
        accb[864:896] += fresh[256:288]

    @pl.loop(0, faces)
    def _(f):
        for h in range(2):
            ff[h] = cv[f, :, 128 * h : 128 * h + 128].astype(f32)
            for s in range(2):
                cvf[h, s, ring_v(f)] = ff[h, pl.ds(area - cols if s else 0, cols)]
                chf[h, s, ring_h(f)] = ff[h, pl.ds(cols - 1 if s else 0, rows, stride=cols)]

    for s in range(2):
        cev[s] = join(cvf, (s,)).astype(bf)
        ceh[s] = join(chf, (s,)).astype(bf)
    first_part()
    first.finish()
    ring_in(first, 3)
    ring_cat(rc1v, rc1h, 3)
    for s in range(2):
        rhs = cat([w_first(6 * s + b) for b in range(3)] + [we[2 * s]], 0)
        split(cvf, (s,), dot(rc1v[s], rhs))
        rhs = cat([w_first(3 * a + 2 * s) for a in range(3)] + [we[a] for a in range(3)], 0)
        split(chf, (s,), dot(rc1h[s], rhs))
    add_to_edges(cvf, chf)
    for h in range(2):
        for s in range(2):
            evf[h, s], slev[h, s] = gelu_slope(evf[h, s])
            ehf[h, s], sleh[h, s] = gelu_slope(ehf[h, s])
    edges_out(second, 2)
    second.start()

    def conv_second(f):
        lhs = cat(windows(hc.at[f]))
        rhs = cat([w2[t] for t in range(TAPS)], 0)
        split(pre, (face_rows(f),), dot(lhs, rhs))

    def second_part():
        @pl.loop(0, faces // 2)
        def _(i):
            pl.when(i == 3)(second.middle)
            for u in range(2):
                f = 2 * i + u
                act, sl = gelu_slope(join(pre, (face_rows(f),)))
                slope[face_rows(f)] = sl.astype(bf)
                fill(hc.at[f], act.astype(bf).reshape(rows, cols, 256))
            for u in range(2):
                conv_second(2 * i + u)

    w2load.wait()
    second_part()
    second.finish()
    ring_in(second, 2)
    ring_cat(rc2v, rc2h, 2)
    for s in range(2):
        split(cvf, (s,), dot(rc2v[s], cat([w2[6 * s + b] for b in range(3)], 0)))
        split(chf, (s,), dot(rc2h[s], cat([w2[3 * a + 2 * s] for a in range(3)], 0)))
    add_to_edges(cvf, chf)

    def ring_grads(ex, taps, blocks):
        for s in range(2):
            lhs = cat([cat([rvf[j, s, pl.ds(12 * b, 216)] for j in range(2)]).astype(bf) for b in range(3)])
            base = 0 if s else 6
            rhs = cat([taps(8 - (base + b)) for b in range(3)], 1)
            out = dot_nt(lhs, rhs)
            if blocks == 3:
                mid = dot_nt(gev[s], we[2 * s])
                pad = jnp.zeros((24, LANES), f32)
                mid = cat([pad, mid, pad], 0)
                tail = mid[24:240]
                for b in (1, 2):
                    tail = tail + pltpu.roll(mid[24 - 12 * b : 240 - 12 * b], LANES - 9 * b, axis=1)
                out = cat([out, jnp.where(lane < 9, tail, 0.0)])
            for j in range(blocks):
                cvf[j, s] = out[12:204, 128 * j : 128 * j + 128]
                ff[j, pl.ds(256 * s, 12)] = out[0:12, 128 * j : 128 * j + 128]
                ff[j, pl.ds(256 * s + 128, 12)] = out[204:216, 128 * j : 128 * j + 128]
            lhs = cat([cat([rhf[j, s, pl.ds(12 * a, 384)] for j in range(2)]).astype(bf) for a in range(3)])
            base = 0 if s else 2
            rhs = cat([taps(8 - (base + 3 * a)) for a in range(3)], 1)
            out = dot_nt(lhs, rhs)
            if blocks == 3:
                tail = dot_nt(lhs, cat([we[2 - a] for a in range(3)], 1))
                tail = pltpu.roll(tail, LANES - 18, axis=1) if s else tail
                out = cat([out, jnp.where(lane < 9, tail, 0.0)])
            for j in range(blocks):
                chf[j, s] = out[:, 128 * j : 128 * j + 128]
        for j in range(blocks):
            lanes = slice(128 * j, 128 * j + 128)
            for spot in range(4):
                s, right = spot // 2, spot % 2
                v = ff[j, pl.ds(256 * s + 128 * right, 12)]
                edge = (tx == 3) if right else (tx == 0)
                late = jnp.where(edge, ty == 1, right == 0)
                zero = jnp.zeros((4, LANES), f32)
                ex.rg_c[spot, :, lanes] = jnp.where(late, cat([zero, v], 0), cat([v, zero], 0)).astype(bf)

                @pl.when((ty == s) & edge)
                def _(j=j, s=s, right=right, spot=spot, v=v):
                    take = rule[spot, 0:12] > 0.0
                    cvf[j, s, pl.ds(180 if right else 0, 12)] += jnp.where(take, v, 0.0)
                    chf[j, right, pl.ds(372 if s else 0, 12)] += jnp.where(take, 0.0, v)
        for s in range(2):
            ex.rg_v[s] = join(cvf, (s,), blocks).astype(bf)
            ex.rg_h[s] = join(chf, (s,), blocks).astype(bf)

    def edge_grads(make_v, make_h):
        for s in range(2):
            for h in range(2):
                lanes = slice(128 * h, 128 * h + 128)
                v = make_v(h, s).astype(bf)
                gev[s, :, lanes] = v
                rvf[h, s, pl.ds(0, 24)] = jnp.zeros((24, LANES), f32)
                rvf[h, s, pl.ds(216, 24)] = jnp.zeros((24, LANES), f32)
                rvf[h, s, pl.ds(24, 192)] = v.astype(f32)
                v = make_h(h, s).astype(bf)
                geh[s, :, lanes] = v
                rhf[h, s, pl.ds(12, 384)] = v.astype(f32)

    def slope_two(u, h):
        return gelu_slope(u + bias_two[...].astype(f32).reshape(1, 256)[:, 128 * h : 128 * h + 128])[1]

    edge_grads(
        lambda h, s: slope_two(evf[h, s], h) * cev[s, :, 128 * h : 128 * h + 128].astype(f32),
        lambda h, s: slope_two(ehf[h, s], h) * ceh[s, :, 128 * h : 128 * h + 128].astype(f32),
    )
    ring_grads(third, lambda t: w2[t], 2)
    third.start()

    def out_copy(f):
        return pltpu.make_async_copy(hc.at[f, pl.ds(1, rows), :, pl.ds(0, 256)], out_ref.at[f], lsem.at[3])

    def gx_copy(f):
        return pltpu.make_async_copy(hc.at[f, pl.ds(1, rows), :, pl.ds(512, 256)], gx_ref.at[f], lsem.at[4])

    def second_bias():
        return bias_two[...].astype(f32).reshape(1, 256)

    def third_part():
        @pl.loop(0, faces // 2)
        def _(i):
            pl.when(i == 4)(third.middle)
            grads = []
            for u in range(2):
                f = 2 * i + u
                sl = gelu_slope(join(pre, (face_rows(f),)) + second_bias())[1]
                grad = (cv[f].astype(f32) * sl).astype(bf)
                accb[896:897] += jnp.sum(grad.astype(f32), axis=0, keepdims=True)
                grads.append(grad)
            for u in range(2):
                cv[2 * i + u] = grads[u]
            pair = cat(grads, 0)
            for a in range(3):
                field = cat([hc[2 * i + u, a : a + rows].reshape(area, 768) for u in range(2)], 0)
                acca[768 * a : 768 * a + 768] += dot_tn(field, pair)

    def output_part():
        @pl.loop(0, faces // 2)
        def _(i):
            sums("out", i)
            for u in range(2):
                f = 2 * i + u
                act = gelu_slope(join(pre, (face_rows(f),)) + second_bias())[0]
                field = cat([xv[f].reshape(area, 256), t27[f, 1 : rows + 1].reshape(area, LANES)])
                whole = (act + dot(field, cat([wskip[0:256], wse[...]], 0))).astype(bf)
                hc[f, 1 : rows + 1, :, 0:256] = whole.reshape(rows, cols, 256)
            for u in range(2):
                out_copy(2 * i + u).start()

    def third_back():
        @pl.loop(0, faces // 2)
        def _(i):
            sums("back", i)
            for u in range(2):
                fill(xc[u], cv[2 * i + u].reshape(rows, cols, 256))
            rhs = cat([w2[8 - t] for t in range(TAPS)], 1)
            for u in range(2):
                split(pre, (face_rows(2 * i + u),), dot_nt(cat(windows(xc[u])), rhs))

    def ring_kernel_grads(grad_ref, extra, rcv, rch):
        for s in range(2):
            fresh = dot_tn(rcv[s], gev[s])
            for b in range(3):
                at = BLOCKS[b] + 512 * s if extra else 1536 * s + 256 * b
                grad_ref[at : at + 256] += fresh[256 * b : 256 * b + 256]
            if extra:
                grad_ref[768 + 64 * s : 800 + 64 * s] += fresh[768:800]
            fresh = dot_tn(rch[s], geh[s])
            for a in range(3):
                at = BLOCKS[2 * s] + 256 * a if extra else 768 * a + 512 * s
                grad_ref[at : at + 256] += fresh[256 * a : 256 * a + 256]
                if extra:
                    grad_ref[768 + 32 * a : 800 + 32 * a] += fresh[768 + 128 * a : 800 + 128 * a]

    keep = load(pre, kept, 12)
    third_part()
    keep.wait()
    ring_kernel_grads(acca, False, rc2v, rc2h)
    totals = {}
    for index, (name, first_row, count, way) in enumerate(SUMS):
        if name[0] == "a":
            totals[name] = Total(index, acca, first_row, outa, first_row, landa, first_row, count, way)
        else:
            totals[name] = Total(index, accb, first_row, slope, first_row, slope, 2560 + first_row, count, way)
    sums("middle")
    third_back()
    cload = load(cot_in, cv, 2)
    third.finish()
    third.stage(2)

    @pl.loop(0, faces)
    def _(f):
        for h in range(2):
            for s in range(2):
                pre[h, top(f, s)] += evf[h, s, ring_v(f)]
        for h in range(2):
            for s in range(2):
                pre[h, side(f, s)] += ehf[h, s, ring_h(f)]
        for h in range(2):
            for s in range(2):
                evf[h, s, ring_v(f)] = pre[h, top(f, s)]
                ehf[h, s, ring_h(f)] = pre[h, side(f, s)]

    edge_grads(lambda h, s: evf[h, s] * slev[h, s], lambda h, s: ehf[h, s] * sleh[h, s])
    ring_grads(fourth, w_first, 3)
    fourth.start()
    sums("sent")

    def first_grads(f):
        grad = (join(pre, (face_rows(f),)) * slope[face_rows(f)].astype(f32)).astype(bf)
        hc[f, 1 : rows + 1, :, 256:512] = grad.reshape(rows, cols, 256)

    def shifted_grads(g, start, choose):
        for u in range(3):
            xc[0][1 : rows + 1, :, 256 * u : 256 * u + 256] = choose(xv[3 * g + u])
        grads = cat([hc[3 * g + u, 1 : rows + 1, :, 256:512].reshape(area, 256) for u in range(3)], 0)
        field = cat([
            cat([xc[0][a : a + rows, :, 256 * u : 256 * u + 256].reshape(area, 256) for a in range(3)])
            for u in range(3)], 0)
        accb[pl.ds(start, 768)] += dot_tn(field, grads)
        return grads

    def fourth_start():
        @pl.loop(0, faces // 3)
        def _(g):
            for u in range(3):
                first_grads(3 * g + u)
            grads = shifted_grads(g, 0, lambda v: shifts(v)[0])
            extra = cat([
                cat([t27[3 * g + u, a : a + rows].reshape(area, LANES) for a in range(3)]) for u in range(3)], 0)
            fresh = dot_tn(extra, grads)
            for a in range(3):
                accb[768 + 32 * a : 800 + 32 * a] += fresh[128 * a : 128 * a + 32]

    def free_slopes():
        for target in ({"dp": core_mate}, {"dp": x_mate}):
            pl.semaphore_signal(credit, inc=1, device_id=target, device_id_type=pl.DeviceIdType.MESH)
        for q in range(8):
            @pl.when(place != q)
            def _(q=q):
                pl.semaphore_signal(credit, inc=1, device_id=dev(q // 4, q % 4), device_id_type=pl.DeviceIdType.MESH)

    def fourth_rest():
        @pl.loop(0, 2 * faces // 3)
        def _(i):
            b = 1 + i // 4
            pl.when(i == 2)(fourth.middle)
            sums("more", i)
            shifted_grads(i % 4, pl.multiple_of(256 + 768 * b, 256), lambda v: jnp.where(b == 1, v, shifts(v)[1]))

    ring_kernel_grads(accb, True, rc1v, rc1h)
    fourth_start()
    free_slopes()
    pl.semaphore_wait(credit, 9)
    sums("first")
    keep = load(kept, pre, 12)
    fourth_rest()
    hot = landa.at[0:1152]
    hotload = load(hot_back_in, hot, 11)
    sums("third")
    keep.wait()
    output_part()
    fourth.finish()
    fourth.stage(3)

    def part(u, j, start=0, size=area, stride=1):
        return pl.ds((3 * u + j) * area + start, size, stride=stride)

    def last_part():
        @pl.loop(0, faces // 2)
        def _(i):
            sums("last", i)
            col = lax.broadcasted_iota(jnp.int32, (area, 1), 0) % cols
            for u in range(2):
                f = 2 * i + u
                cot = cv[f]
                rhs = cat([w_first(8 - t) for t in range(TAPS)] + [wskip[0:256]], 1)
                fill(xc[u], hc[f, 1 : rows + 1, :, 256:512])
                main = dot_nt(cat(windows(xc[u]) + [cot]), rhs)
                for h in range(2):
                    pre[0, part(u, h)] = main[:, 128 * h : 128 * h + 128]
                taps = dot_nt(cat([hc[f, 1 : rows + 1, :, 256:512].reshape(area, 256), cot]), cat([we81[0], we81[1]], 1))
                edge = jnp.zeros((cols, LANES), f32)
                lines = (
                    cat([taps[cols:], edge], 0)
                    + pltpu.roll(taps, LANES - 27, axis=1)
                    + cat([edge, pltpu.roll(taps, LANES - 54, axis=1)[: area - cols]], 0))
                after = jnp.where(col == cols - 1, 0.0, pltpu.roll(lines, area - 1, axis=0))
                before = jnp.where(col == 0, 0.0, pltpu.roll(lines, 1, axis=0))
                pre[0, part(u, 2)] = after + pltpu.roll(lines, LANES - 9, axis=1) + pltpu.roll(before, LANES - 18, axis=1)
            for u in range(2):
                f = 2 * i + u
                for j in range(3):
                    for s in range(2):
                        pre[0, part(u, j, area - cols if s else 0, cols)] += evf[j, s, ring_v(f)]
                for j in range(3):
                    for s in range(2):
                        pre[0, part(u, j, cols - 1 if s else 0, rows, cols)] += ehf[j, s, ring_h(f)]
                for c in range(cols):
                    here = pre[0, part(u, 2, c, rows, cols)].astype(bf)
                    rc1h[c // 8, rows16(f * rows, rows), c % 8 * LANES : c % 8 * LANES + LANES] = here
                whole = cat([pre[0, part(u, 0)], pre[0, part(u, 1)]]).astype(bf)
                hc[f, 1 : rows + 1, :, 512:768] = whole.reshape(rows, cols, 256)
            for u in range(2):
                gx_copy(2 * i + u).start()

    cload.wait()
    last_part()
    sums("end")
    hotload.wait()
    back = sum(
        dot_nt(rc1h[k // 4, :, k % 4 * 256 : k % 4 * 256 + 256], hot[144 * k : 144 * k + 144]) for k in range(8))
    for f in range(faces):
        ev[f] = back[f * rows : f * rows + rows].T.astype(bf).reshape(9, cols, rows)
    eout = pltpu.make_async_copy(ev, gext_ref, lsem.at[1])
    eout.start()
    sums("rest")
    tail = slope[768:1024].astype(f32)
    for h in range(2):
        for t in range(TAPS):
            at = 32 * (t // 3) + 9 * (t % 3)
            tails[t, :, 128 * h : 128 * h + 128] = tail[at : at + 9, 128 * h : 128 * h + 128]
    for t in range(TAPS):
        pltpu.make_async_copy(tails.at[t], first_ref.at[t, pl.ds(256, 9)], lsem.at[10]).start()
    for b in range(3):
        @pl.loop(0, 3)
        def _(a):
            accb[pl.ds(pl.multiple_of(BLOCKS[b] + 256 * a, 256), 256)] = slope[
                pl.ds(pl.multiple_of(BLOCKS[b] + 256 * a, 256), 256)].astype(f32)
            pltpu.make_async_copy(
                accb.at[pl.ds(pl.multiple_of(BLOCKS[b] + 256 * a, 256), 256)], first_ref.at[3 * a + b, pl.ds(0, 256)],
                lsem.at[9]).start()
    @pl.loop(0, TAPS)
    def _(t):
        here = pl.ds(pl.multiple_of(256 * t, 256), 256)
        acca[here] = outa[here].astype(f32)
        pltpu.make_async_copy(acca.at[here], second_ref.at[here], lsem.at[8]).start()

    skip_ref[0:256] = outa[2304:2560].astype(f32)
    skip_ref[256:265] = tail[96 + 9 : 96 + 18]
    one_ref[...] = tail[32 + ONE : 32 + ONE + 1]
    two_ref[...] = tail[128:129]
    three_ref[...] = tail[96 + ONE : 96 + ONE + 1]
    pltpu.make_async_copy(out_ref, out_ref, lsem.at[3]).wait()
    pltpu.make_async_copy(gx_ref, gx_ref, lsem.at[4]).wait()
    eout.wait()
    pltpu.make_async_copy(acca.at[0:2304], second_ref, lsem.at[8]).wait()
    pltpu.make_async_copy(accb.at[0:2304], accb.at[0:2304], lsem.at[9]).wait()
    pltpu.make_async_copy(tails, tails, lsem.at[10]).wait()
    for ex in (first, second, third, fourth):
        ex.drain()


def packing(extra, cols, moves):
    hot = np.zeros((extra, cols, cols, LANES), ml_dtypes.bfloat16)
    for start, step in moves:
        for channel in range(extra):
            for column in range(cols):
                if 0 <= column - step < cols:
                    hot[channel, column, column - step, start + channel] = 1
    hot = hot.reshape(extra * cols, cols * LANES // 256, 256)
    return hot.transpose(1, 0, 2).reshape(-1, 256)


def fast_device(
    features, extra_inputs, first_kernel, first_bias, second_kernel, second_bias,
    skip_kernel, skip_bias, seam_table, cotangent,
):
    f32, bf = jnp.float32, jnp.bfloat16
    _, faces, rows, cols, ch = features.shape
    area = rows * cols
    extra = extra_inputs.shape[-1]
    vm, hbm = pl.BlockSpec(memory_space=pltpu.VMEM), pl.BlockSpec(memory_space=pl.ANY)
    shape = jax.ShapeDtypeStruct

    def exchange_bufs(lanes, windows):
        return [
            pltpu.VMEM((2, 192, lanes), bf), pltpu.VMEM((2, 384, lanes), bf), pltpu.VMEM((384, lanes), bf),
            pltpu.VMEM((384, lanes), bf), pltpu.VMEM((2, 192, lanes), bf), pltpu.VMEM((2, 384, lanes), bf),
            pltpu.VMEM((4, 16, lanes), bf), pltpu.VMEM((8 * windows, 16, lanes), bf),
            pltpu.VMEM((2 * windows, 16, lanes), bf),
        ]

    cat_shape = (rows + 2, cols, 3 * ch)
    sums = (SUM_ROWS, ch)
    scratch = [
        pltpu.VMEM((TAPS, ch + extra, ch), bf), pltpu.VMEM((TAPS, ch, ch), bf), pltpu.VMEM((ch + extra, ch), bf),
        pltpu.VMEM((3, LANES, ch), bf), pltpu.VMEM((LANES, ch), bf), pltpu.VMEM((2, LANES, ch), bf),
        pltpu.VMEM((384, 384), bf),
        pltpu.VMEM((4, 16, LANES), f32), pltpu.VMEM((TAPS, extra, ch), f32),
        pltpu.VMEM((faces, rows, cols, ch), bf), pltpu.VMEM((faces, extra, cols, rows), bf),
        pltpu.VMEM((faces, area, ch), bf), pltpu.VMEM((faces, rows + 2, cols, LANES), bf),
        [pltpu.VMEM(cat_shape, bf)] * 2, pltpu.VMEM((faces,) + cat_shape, bf),
        pltpu.VMEM((2, faces * area, LANES), f32), pltpu.VMEM((faces * area, ch), bf),
        pltpu.VMEM((2, 2, 192, LANES), f32), pltpu.VMEM((2, 2, 384, LANES), f32),
        pltpu.VMEM((2, 192, ch), bf), pltpu.VMEM((2, 384, ch), bf),
        pltpu.VMEM((3, area, LANES), f32),
        pltpu.VMEM((3, 2, 192, LANES), f32), pltpu.VMEM((3, 2, 384, LANES), f32),
        pltpu.VMEM((3, 2, 240, LANES), f32), pltpu.VMEM((3, 2, 408, LANES), f32),
        pltpu.VMEM((3, 2, 192, LANES), f32), pltpu.VMEM((3, 2, 384, LANES), f32),
        pltpu.VMEM((2, 192, 896), bf), pltpu.VMEM((2, 384, 1152), bf),
        pltpu.VMEM((2, 192, 768), bf), pltpu.VMEM((2, 384, 768), bf),
        pltpu.VMEM((2, 192, ch), bf), pltpu.VMEM((2, 384, ch), bf),
        pltpu.VMEM(sums, f32), pltpu.VMEM(sums, f32), pltpu.VMEM(sums, bf), pltpu.VMEM(sums, bf),
        [exchange_bufs(384, 0 + 1), exchange_bufs(256, 1), exchange_bufs(256, 1), exchange_bufs(384, 1)],
        pltpu.SemaphoreType.DMA((4, 48)), pltpu.SemaphoreType.DMA((4, 33)),
        pltpu.SemaphoreType.DMA((len(SUMS), 20)), pltpu.SemaphoreType.DMA((len(SUMS), 20)),
        pltpu.SemaphoreType.REGULAR, pltpu.SemaphoreType.REGULAR((len(SUMS), 4)), pltpu.SemaphoreType.DMA((13,)),
    ]
    out = pl.pallas_call(
        whole_block,
        out_shape=(
            shape((faces, rows, cols, ch), bf), shape((faces, rows, cols, ch), bf), shape((faces, extra, cols, rows), bf),
            shape((TAPS * ch, ch), f32), shape((TAPS, ch + extra, ch), f32),
            shape((2, faces * area, LANES), f32), shape((ch + extra, ch), f32),
            shape((1, ch), f32), shape((1, ch), f32), shape((1, ch), f32),
        ),
        in_specs=[hbm] * 5 + [vm] * 4 + [hbm] * 3,
        out_specs=[hbm] * 6 + [vm] * 4,
        scratch_shapes=scratch,
        compiler_params=pltpu.CompilerParams(
            collective_id=0, has_side_effects=True, vmem_limit_bytes=65400 * 1024),
    )(
        features[0], extra_inputs[0].transpose(0, 3, 2, 1), first_kernel.reshape(TAPS, ch + extra, ch),
        second_kernel.reshape(TAPS, ch, ch), skip_kernel, first_bias, second_bias, skip_bias,
        seam_table.transpose(1, 2, 0), cotangent.reshape(faces, area, ch),
        packing(extra, cols, ((0, -1), (extra, 0), (2 * extra, 1))), packing(extra, cols, ((0, 0),)),
    )
    block_output, grad_features, grad_extra, second_grad, first_grad, _, skip_grad, one, two, three = out
    return (
        block_output.reshape(features.shape),
        grad_features.reshape(features.shape),
        grad_extra.transpose(0, 3, 2, 1)[None],
        first_grad.reshape(first_kernel.shape),
        one[0],
        second_grad.reshape(second_kernel.shape),
        two[0],
        skip_grad,
        three[0],
    )


def solution(mesh):
    fits = mesh.shape["ty"] == 2 and mesh.shape["tx"] == 4

    def block(*args):
        tile = args[0].shape
        if fits and tile[1:] == (12, 32, 16, 256) and args[1].shape[-1] == 9:
            return fast_device(*args)
        return per_device(*args)

    return jax.shard_map(
        block,
        mesh=mesh,
        in_specs=(
            P("dp", None, "ty", "tx", None),
            P("dp", None, "ty", "tx", None),
            P(),
            P(),
            P(),
            P(),
            P(),
            P(),
            P(),
            P("dp", None, "ty", "tx", None),
        ),
        out_specs=(
            P("dp", None, "ty", "tx", None),
            P("dp", None, "ty", "tx", None),
            P("dp", None, "ty", "tx", None),
            P(),
            P(),
            P(),
            P(),
            P(),
            P(),
        ),
        check_vma=False,
    )
```
